32 devices in a mesh: ctx: 4 (over z), tp: 8 (over y, x, core).
Axes of the slice: x: 2, y: 2, z: 4, core: 2. Of those that a mesh axis runs over, the one named last changes fastest.
Arguments:
- tokens: bfloat16 [4096, 2048], P(('ctx', 'tp')), may hold values from -6 to 6
- cotangent: bfloat16 [4096, 2048], P(('ctx', 'tp')), may hold values from -6 to 6
- routes: int32 [4096, 1], P(('ctx', 'tp')), may hold values from 0 to 7; in each aligned block of 128 rows (0 to 127, 128 to 255, ...) at most 24 rows name the same one
- gate_weights: float32 [4096, 1], P(('ctx', 'tp')), may hold values from 0.2 to 1
- w_gate: bfloat16 [8, 2048, 768], P('tp'), may hold values from -0.125 to 0.125
- w_up: bfloat16 [8, 2048, 768], P('tp'), may hold values from -0.125 to 0.125
- w_down: bfloat16 [8, 768, 2048], P('tp'), may hold values from -0.21875 to 0.21875
Outputs:
- layer_output: bfloat16 [4096, 2048], P(('ctx', 'tp'))
- token_grad: bfloat16 [4096, 2048], P(('ctx', 'tp'))
- gate_grad: float32 [4096, 1], P(('ctx', 'tp'))
- down_grad: bfloat16 [8, 768, 2048], P('tp', 'ctx')
The draws below stay inside these ranges and needn't reach their ends.
Inputs may be any that keep to these rules, and one draw needn't show every extreme that they name: `routes`: among the 128 tokens of one device (aligned blocks of rows), at most 24 name the same expert; some device's block reaches 24 for some expert.
All inputs are finite; a program needn't handle non-finite values.
Results may differ from the reference program's by a relative error of at most 0.015.
Values may be sent and summed in bfloat16 or wider, within the bound.
No kernel may reach another device: no remote copies, remote signals or barrier semaphores. Data moves between devices by JAX's collectives and lax.ppermute only.
A program may use at most 64 MiB of HBM per device.

```python
import math
import jax
import jax.numpy as jnp
import numpy as np
from jax import lax

D = 2048
FF = 768
TOK_DEV = 128
ROUTES = 1
EXPERTS = 8
CAP = 24
TOKENS = 4096
N_CTX = 4
N_TP = 8


def block_levels(rng, extent, cuts, smallest, high):
    def one(dim, parts):
        draws = jax.random.uniform(jax.random.fold_in(jax.random.fold_in(rng, 6), dim), (parts,), jnp.float32, smallest / len(cuts), high / len(cuts))
        return jnp.repeat(jnp.exp(draws), extent[dim] // parts).reshape((-1,) + (1,) * (len(extent) - dim - 1))

    level = one(*cuts[0])
    for cut in cuts[1:]:
        level = level * one(*cut)
    return level


def assign_block(key, own, number, rows, amount, top, most, slope):
    ranking = jax.random.permutation(key, amount)
    heavy_load, ordinary = load_shares(amount, rows * top, most, slope, True), load_shares(amount, rows * top, most, slope, False)
    places = jnp.arange(amount)

    def named(tallies, offset_by):
        used = int((tallies > 0).sum())
        fixed = max(1, used // 4)
        moved = fixed + (places - fixed + offset_by * (used - fixed)) % max(1, amount - fixed)
        return jnp.zeros((amount,), jnp.int32).at[ranking[jnp.where(places < fixed, places, moved)]].set(jnp.asarray(tallies, jnp.int32))

    tallies = jnp.where(number % 4 == 0, named(heavy_load, number // 4), named(ordinary, number - number // 4 - 1))
    mixed = jax.random.permutation(jax.random.fold_in(own, 3), amount)
    donor, taker = mixed[0:amount // 2 * 2:2], mixed[1:amount // 2 * 2:2]
    room = jnp.minimum(tallies[donor] - 1, most - tallies[taker]) // 2
    room = jnp.where((donor == ranking[0]) | (taker == ranking[0]) | (tallies[taker] == 0), 0, jnp.maximum(room, 0))
    moved = jax.random.randint(jax.random.fold_in(own, 4), (amount // 2,), 0, 1 << 20) % (room + 1)
    tallies = tallies.at[donor].add(-moved).at[taker].add(moved)
    labels = jnp.searchsorted(jnp.cumsum(tallies), jnp.arange(rows * top), side="right").astype(jnp.int32)
    listing = labels.reshape(top, rows).T
    listing = listing[jax.random.permutation(jax.random.fold_in(own, 1), rows)]
    offset_by = jax.random.randint(jax.random.fold_in(own, 2), (rows, 1), 0, top)
    return jnp.take_along_axis(listing, (jnp.arange(top)[None, :] + offset_by) % top, axis=1)


def load_shares(count, total, limit, skew, full):
    portions = [(1 << 20) // math.isqrt(grade ** skew) + 1 for grade in range(1, count + 1)]
    largest = limit if full else min(limit, max(-(-total // count), total * portions[0] // sum(portions)))
    least = 1 if total - largest >= count - 1 else 0
    holding, surplus = [largest] + [least] * (count - 1), total - largest - least * (count - 1)
    while surplus > 0:
        free = [i for i in range(1, count) if holding[i] < largest] or [i for i in range(1, count) if holding[i] < limit]
        mass, remaining = sum([portions[i] for i in free]), surplus
        for i in free:
            addition = min(limit - holding[i], max(1, remaining * portions[i] // mass), surplus)
            holding[i] = holding[i] + addition
            surplus = surplus - addition
    return np.array(holding)


def scatter_about(stream_key, dims, spread, reach, cuts=(), kind=jnp.bfloat16):
    values = jax.random.normal(stream_key, dims, jnp.float32) * spread
    if len(cuts) > 0:
        values = block_levels(stream_key, dims, cuts, -0.22, 0.18) * values
    return jnp.clip(values, min=-reach, max=reach).astype(kind)


def setup_inputs(seed: int = 0) -> dict:
    streams_of = jax.random.split(jax.random.key(seed), 8)
    tokens = scatter_about(streams_of[0], (TOKENS, D), 1.0, 6.0, ((0, 32),))
    cotangent = scatter_about(streams_of[1], (TOKENS, D), 1.0, 6.0, ((0, 32),))
    routes_keys = jax.random.split(jax.random.fold_in(streams_of[2], 1), TOKENS // TOK_DEV)
    routes_turns = jax.random.permutation(jax.random.fold_in(streams_of[2], 3), TOKENS // TOK_DEV)
    routes = jax.vmap(lambda own, number: assign_block(jax.random.fold_in(streams_of[2], 2), own, number, TOK_DEV, EXPERTS, ROUTES, CAP, 2))(routes_keys, routes_turns).reshape((TOKENS, ROUTES))
    gate_weights = jnp.clip(jnp.exp(math.log(1.0) - 1.609438 * jax.random.uniform(streams_of[3], (TOKENS, ROUTES), jnp.float32) ** block_levels(streams_of[3], (TOKENS, ROUTES), ((0, 32),), -0.2, 0.2)), 0.2, 1.0)
    w_gate = scatter_about(streams_of[4], (EXPERTS, D, FF), D ** -0.5, 0.125, ((0, 8),))
    w_up = scatter_about(streams_of[5], (EXPERTS, D, FF), D ** -0.5, 0.125, ((0, 8),))
    w_down = scatter_about(streams_of[6], (EXPERTS, FF, D), FF ** -0.5, 0.21875, ((0, 8),))
    return dict(tokens=tokens, cotangent=cotangent, routes=routes, gate_weights=gate_weights, w_gate=w_gate, w_up=w_up, w_down=w_down)


def expert_block(rows_in, rows_cot, gate_mat, up_mat, down_mat):
    pre_act = jnp.dot(rows_in, gate_mat, preferred_element_type=jnp.float32)
    up_act = jnp.dot(rows_in, up_mat, preferred_element_type=jnp.float32)
    sigma = jax.nn.sigmoid(pre_act)
    hidden = (pre_act * sigma * up_act).astype(jnp.bfloat16)
    output = jnp.dot(hidden, down_mat, preferred_element_type=jnp.float32).astype(jnp.bfloat16)
    dhidden = lax.dot_general(rows_cot, down_mat, (((1,), (1,)), ((), ())), preferred_element_type=jnp.float32)
    dup_act = (dhidden * pre_act * sigma).astype(jnp.bfloat16)
    dpre_act = (dhidden * up_act * sigma * (1.0 + pre_act * (1.0 - sigma))).astype(jnp.bfloat16)
    first = lax.dot_general(dpre_act, gate_mat, (((1,), (1,)), ((), ())), preferred_element_type=jnp.float32)
    second = lax.dot_general(dup_act, up_mat, (((1,), (1,)), ((), ())), preferred_element_type=jnp.float32)
    input_grad = (first + second).astype(jnp.bfloat16)
    return output, input_grad, hidden


def reference(tokens, cotangent, routes, gate_weights, w_gate, w_up, w_down):
    num_tokens = tokens.shape[0]
    width = tokens.shape[1]
    expert_ids = routes[:, 0].astype(jnp.int32)
    owner_ctx = (jnp.arange(num_tokens, dtype=jnp.int32) // (TOK_DEV * N_TP)).astype(jnp.int32)
    keys = (expert_ids * N_CTX + owner_ctx).astype(jnp.int32)
    order = jnp.argsort(keys, stable=True).astype(jnp.int32)
    sorted_keys = keys[order]
    pair_count = EXPERTS * N_CTX
    pair_ids = jnp.arange(pair_count, dtype=jnp.int32)
    starts = jnp.searchsorted(sorted_keys, pair_ids, side="left").astype(jnp.int32)
    ends = jnp.searchsorted(sorted_keys, pair_ids + 1, side="left").astype(jnp.int32)
    slot_count = N_TP * CAP
    offsets = jnp.arange(slot_count, dtype=jnp.int32)
    position = starts[:, None] + offsets[None, :]
    valid = position < ends[:, None]
    safe_pos = jnp.minimum(position, num_tokens - 1).astype(jnp.int32)
    token_index = jnp.where(valid, order[safe_pos], num_tokens).astype(jnp.int32)
    token_index = token_index.reshape(EXPERTS, N_CTX, slot_count)
    scaled = (gate_weights[:, 0:1] * cotangent.astype(jnp.float32)).astype(jnp.bfloat16)
    tokens_pad = jnp.concatenate([tokens, jnp.zeros((1, width), tokens.dtype)], axis=0)
    scaled_pad = jnp.concatenate([scaled, jnp.zeros((1, width), scaled.dtype)], axis=0)

    def per_expert(expert):
        table = token_index[expert]
        gate_mat = w_gate[expert]
        up_mat = w_up[expert]
        down_mat = w_down[expert]

        def per_group(accum, rows):
            rows_in = tokens_pad[rows]
            rows_cot = scaled_pad[rows]
            output, input_grad, hidden = expert_block(rows_in, rows_cot, gate_mat, up_mat, down_mat)
            term = lax.dot_general(hidden, rows_cot, (((0,), (0,)), ((), ())), preferred_element_type=jnp.float32)
            rounded = lax.optimization_barrier(term.astype(jnp.bfloat16))
            return accum + rounded.astype(jnp.float32), (output, input_grad)

        start_acc = jnp.zeros((FF, width), jnp.float32)
        accum, outs = lax.scan(per_group, start_acc, table)
        return accum.astype(jnp.bfloat16), outs[0], outs[1]

    down_grad, out_all, grad_all = lax.map(per_expert, jnp.arange(EXPERTS, dtype=jnp.int32))
    flat_index = token_index.reshape(-1)
    out_tok = jnp.zeros((num_tokens + 1, width), jnp.float32).at[flat_index].add(out_all.reshape(-1, width).astype(jnp.float32))[:num_tokens]
    grad_tok = jnp.zeros((num_tokens + 1, width), jnp.float32).at[flat_index].add(grad_all.reshape(-1, width).astype(jnp.float32))[:num_tokens]
    layer_output = (gate_weights[:, 0:1] * out_tok).astype(jnp.bfloat16)
    token_grad = grad_tok.astype(jnp.bfloat16)
    gate_grad = jnp.sum(cotangent.astype(jnp.float32) * out_tok, axis=1, keepdims=True)
    return layer_output, token_grad, gate_grad, down_grad
```

```python
import functools

import jax
import jax.numpy as jnp
from jax import lax
from jax.experimental import pallas as pl
from jax.experimental.pallas import tpu as pltpu
from jax.sharding import PartitionSpec as P

BF16 = jnp.bfloat16
F32 = jnp.float32
CONTRACT_FIRST = (((0,), (0,)), ((), ()))
CONTRACT_LAST = (((1,), (1,)), ((), ()))


def expert_block(rows_in, rows_cot, gate_mat, up_mat, down_mat):
    pre_act = jnp.dot(rows_in, gate_mat, preferred_element_type=F32)
    up_act = jnp.dot(rows_in, up_mat, preferred_element_type=F32)
    sigma = jax.nn.sigmoid(pre_act)
    hidden = (pre_act * sigma * up_act).astype(BF16)
    output = jnp.dot(hidden, down_mat, preferred_element_type=F32).astype(BF16)
    dhidden = lax.dot_general(rows_cot, down_mat, CONTRACT_LAST, preferred_element_type=F32)
    dup_act = (dhidden * pre_act * sigma).astype(BF16)
    dpre_act = (dhidden * up_act * sigma * (1.0 + pre_act * (1.0 - sigma))).astype(BF16)
    first = lax.dot_general(dpre_act, gate_mat, CONTRACT_LAST, preferred_element_type=F32)
    second = lax.dot_general(dup_act, up_mat, CONTRACT_LAST, preferred_element_type=F32)
    input_grad = (first + second).astype(BF16)
    return (output, input_grad, hidden)


def body_any(tokens, cotangent, routes, gate_weights, w_gate, w_up, w_down):
    tok_rows, width = tokens.shape
    peers = lax.axis_size("tp")
    capacity = 3 * tok_rows * routes.shape[1] // (2 * peers)
    expert_ids = routes[:, 0]
    onehot = (expert_ids[:, None] == jnp.arange(peers, dtype=jnp.int32)[None, :]).astype(jnp.int32)
    rank = jnp.sum((jnp.cumsum(onehot, axis=0) - 1) * onehot, axis=1)
    slot = expert_ids * capacity + rank
    placing = (
        slot[None, :] == jnp.arange(peers * capacity, dtype=jnp.int32)[:, None]
    ).astype(BF16)
    scaled = (gate_weights * cotangent.astype(F32)).astype(BF16)
    send = jnp.dot(
        placing, jnp.concatenate([tokens, scaled], axis=1), preferred_element_type=F32
    ).astype(BF16)
    got = lax.all_to_all(
        send.reshape(peers, capacity, 2 * width), "tp", split_axis=0, concat_axis=0, tiled=True
    ).reshape(-1, 2 * width)
    got_cot = got[:, width:]
    output, input_grad, hidden = expert_block(
        got[:, :width], got_cot, w_gate[0], w_up[0], w_down[0]
    )
    back = lax.all_to_all(
        jnp.concatenate([output, input_grad], axis=1).reshape(peers, capacity, 2 * width),
        "tp", split_axis=0, concat_axis=0, tiled=True,
    ).reshape(-1, 2 * width)
    partial = lax.dot_general(hidden, got_cot, CONTRACT_FIRST, preferred_element_type=F32)
    summed = lax.psum_scatter(partial.astype(BF16), "ctx", scatter_dimension=0, tiled=True)
    home = lax.dot_general(placing, back, CONTRACT_FIRST, preferred_element_type=F32)
    out_tok = home[:, :width]
    layer_output = (gate_weights * out_tok).astype(BF16)
    gate_grad = jnp.sum(cotangent.astype(F32) * out_tok, axis=1, keepdims=True)
    return layer_output, home[:, width:].astype(BF16), gate_grad, summed[None]


VMEM_LIMIT = 32 * 1024 * 1024
TINY = pl.CostEstimate(flops=1, bytes_accessed=1, transcendentals=0)


def call(kernel, outs, **more):
    return pl.pallas_call(
        kernel,
        out_shape=outs,
        cost_estimate=TINY,
        compiler_params=pltpu.CompilerParams(vmem_limit_bytes=VMEM_LIMIT),
        **more,
    )


def shaped(shape, dtype=BF16):
    return jax.ShapeDtypeStruct(shape, dtype)


def diagonal(size):
    return lax.broadcasted_iota(jnp.int32, (size, size), 0) == lax.broadcasted_iota(
        jnp.int32, (size, size), 1
    )


def column(row):
    return jnp.sum(jnp.where(diagonal(row.shape[1]), row, 0), axis=1, keepdims=True)


def send_cot_kernel(peers, capacity, routes, gates, cot, slot_out, *blocks):
    ids = routes[...]
    count = ids.shape[1]
    onehot = lax.broadcasted_iota(jnp.int32, (peers, count), 0) == ids
    upto = lax.broadcasted_iota(jnp.int32, (count, count), 0) <= lax.broadcasted_iota(
        jnp.int32, (count, count), 1
    )
    running = jnp.dot(onehot.astype(BF16), upto.astype(BF16), preferred_element_type=F32)
    rank = jnp.sum(jnp.where(onehot, running - 1.0, 0.0), axis=0, keepdims=True).astype(jnp.int32)
    slot_out[...] = ids * capacity + rank
    own = lax.axis_index("tp")
    slot = (ids ^ own) * capacity + rank
    placing = (lax.broadcasted_iota(jnp.int32, (peers * capacity, count), 0) == slot).astype(BF16)
    gate = column(gates[...])
    step = 512
    for at in range(0, cot.shape[1], step):
        cols = slice(at, at + step)
        scaled = (gate * cot[:, cols].astype(F32)).astype(BF16)
        rows = jnp.dot(placing, scaled, preferred_element_type=F32)
        for k in range(peers):
            blocks[k][:, cols] = rows[k * capacity : (k + 1) * capacity].astype(BF16)


def send_tok_kernel(slot, tok, out):
    placing = (lax.broadcasted_iota(jnp.int32, (out.shape[0], tok.shape[0]), 0) == slot[...]).astype(BF16)
    step = 512
    for at in range(0, tok.shape[1], step):
        cols = slice(at, at + step)
        out[:, cols] = jnp.dot(placing, tok[:, cols], preferred_element_type=F32).astype(BF16)


def gather_kernel(peers, capacity, *refs):
    blocks, (cot_a, cot_b, rows) = refs[:peers], refs[peers:]
    own = lax.axis_index("tp")
    for k in range(peers):
        start = pl.multiple_of((own ^ k) * capacity, 8)
        rows[pl.ds(start, capacity), :] = blocks[k][...].astype(F32)
    half = cot_a.shape[1]
    cot_a[...] = rows[:, :half].astype(BF16)
    cot_b[...] = rows[:, half:].astype(BF16)


def dhidden_kernel(cot_a, cot_b, down, out):
    half = cot_a.shape[1]
    out[...] = lax.dot_general(
        cot_a[...], down[:, :half], CONTRACT_LAST, preferred_element_type=F32
    ) + lax.dot_general(cot_b[...], down[:, half:], CONTRACT_LAST, preferred_element_type=F32)


def hidden_kernel(rows, dhid, gate, up, cot_b, hidden, dpre, dup, *quarters):
    parts, turned = quarters[:4], quarters[4:]
    here = lax.axis_index("ctx")
    tile = pl.program_id(0)
    pre_act = jnp.dot(rows[...], gate[...], preferred_element_type=F32)
    up_act = jnp.dot(rows[...], up[...], preferred_element_type=F32)
    sigma = 1.0 / (1.0 + jnp.exp(-pre_act))
    hid = pre_act * sigma * up_act
    hidden[...] = hid.astype(BF16)
    dh = dhid[...]
    dup[...] = (dh * pre_act * sigma).astype(BF16)
    dpre[...] = (dh * up_act * sigma * (1.0 + pre_act * (1.0 - sigma))).astype(BF16)
    across = hid.T.astype(BF16)
    size = across.shape[0] // 2
    for j in range(2):
        block = across[j * size : (j + 1) * size]
        part = jnp.dot(block, cot_b[...], preferred_element_type=F32).astype(BF16)
        for k in range(4):

            @pl.when((here ^ k) == 2 * tile + j)
            def _():
                parts[k][...] = part
                turned[k][...] = block


def back_kernel(hidden, dpre, dup, gate, up, down, out):
    half = down.shape[1]
    out[:, :half] = jnp.dot(hidden[...], down[...], preferred_element_type=F32).astype(BF16)
    out[:, half:] = (
        lax.dot_general(dpre[...], gate[...], CONTRACT_LAST, preferred_element_type=F32)
        + lax.dot_general(dup[...], up[...], CONTRACT_LAST, preferred_element_type=F32)
    ).astype(BF16)


def home_kernel(slot, gates, back, cot, layer_output, token_grad, gate_grad, total):
    count = cot.shape[0]
    placing = (
        lax.broadcasted_iota(jnp.int32, (count, back.shape[0]), 1) == column(slot[...])
    ).astype(BF16)
    half = cot.shape[1]
    out_tok = jnp.dot(placing, back[:, :half], preferred_element_type=F32)
    layer_output[...] = (column(gates[...]) * out_tok).astype(BF16)
    token_grad[...] = jnp.dot(placing, back[:, half:], preferred_element_type=F32).astype(BF16)
    here = jnp.sum(cot[...].astype(F32) * out_tok, axis=1, keepdims=True)

    @pl.when(pl.program_id(0) == 0)
    def _():
        total[...] = here

    @pl.when(pl.program_id(0) > 0)
    def _():
        total[...] += here

    @pl.when(pl.program_id(0) == pl.num_programs(0) - 1)
    def _():
        gate_grad[...] = jnp.sum(jnp.where(diagonal(count), total[...], 0.0), axis=0, keepdims=True)


def down_kernel(h0, h1, h2, h3, cot_a, near, across, far, far_out, last_out, end_3, mid_3, part, out):
    here = lax.axis_index("ctx")
    outer = (here == 0) | (here == 3)
    half = cot_a.shape[1]

    def times(left, right):
        return jnp.dot(left[...], right[...], preferred_element_type=F32)

    both = times(h0, cot_a) + times(h1, near)

    @pl.when(outer)
    def _():
        out[0, :, :half] = (both + times(h2, far_out) + times(h3, last_out)).astype(BF16)

    @pl.when(jnp.logical_not(outer))
    def _():
        out[0, :, :half] = (both + times(h3, across) + times(h2, far)).astype(BF16)

    out[0, :, half:] = (
        end_3[...].astype(F32) + mid_3[...].astype(F32) + part[...].astype(F32)
    ).astype(BF16)


ENDS = ((0, 1), (1, 0), (2, 3), (3, 2))
MIDDLE = ((1, 2), (2, 1))
INWARD = ((0, 1), (3, 2))
OUTWARD = ((1, 0), (2, 3))


def along(rows, pairs):
    return lax.ppermute(rows, "ctx", pairs)


def plus(left, right):
    return (left.astype(F32) + right.astype(F32)).astype(BF16)


def body_line(tokens, cotangent, routes, gate_weights, w_gate, w_up, w_down):
    count, width = tokens.shape
    peers = lax.axis_size("tp")
    capacity = 3 * count * routes.shape[1] // (2 * peers)
    slots = peers * capacity
    inner = w_gate.shape[2]
    half, quarter = width // 2, inner // 4
    gate_mat, up_mat, down_mat = w_gate[0], w_up[0], w_down[0]
    gates = gate_weights.reshape(1, count)

    slot, *blocks = call(
        functools.partial(send_cot_kernel, peers, capacity),
        [shaped((1, count), jnp.int32)] + [shaped((capacity, width))] * peers,
    )(routes.reshape(1, count), gates, cotangent)
    got = {0: blocks[0]}
    for k in [6, 7, 2, 4, 3, 5, 1]:
        got[k] = lax.ppermute(blocks[k], "tp", [(i, i ^ k) for i in range(peers)])
    send_tok = call(send_tok_kernel, shaped((slots, width)))(slot, tokens)
    rows = lax.all_to_all(
        send_tok.reshape(peers, capacity, width), "tp", split_axis=0, concat_axis=0, tiled=True
    ).reshape(slots, width)

    cot_a, cot_b = call(
        functools.partial(gather_kernel, peers, capacity),
        [shaped((slots, half))] * 2,
        scratch_shapes=[pltpu.VMEM((slots, width), F32)],
    )(*[got[k] for k in range(peers)])
    near = along(cot_a, ENDS)
    across = along(cot_a, MIDDLE)

    whole = lambda *shape: pl.BlockSpec(shape, lambda i: (0,) * len(shape))
    tile = inner // 2
    dhid = call(
        dhidden_kernel,
        shaped((slots, inner), F32),
        grid=(2,),
        in_specs=[whole(slots, half), whole(slots, half), pl.BlockSpec((tile, width), lambda i: (i, 0))],
        out_specs=pl.BlockSpec((slots, tile), lambda i: (0, i)),
    )(cot_a, cot_b, down_mat)
    by_tile = pl.BlockSpec((slots, tile), lambda i: (0, i))
    weights = pl.BlockSpec((width, tile), lambda i: (0, i))
    hidden, dpre, dup, *quarters = call(
        hidden_kernel,
        [shaped((slots, inner))] * 3 + [shaped((quarter, half))] * 4 + [shaped((quarter, slots))] * 4,
        grid=(2,),
        in_specs=[whole(slots, width), by_tile, weights, weights, whole(slots, half)],
        out_specs=[by_tile] * 3 + [whole(quarter, half)] * 4 + [whole(quarter, slots)] * 4,
    )(rows, dhid, gate_mat, up_mat, cot_b)
    part, turned = quarters[:4], quarters[4:]

    in_1 = along(part[3], INWARD)
    far_out = along(across, OUTWARD)
    far = along(near, MIDDLE)
    in_2 = along(part[2], INWARD)

    wide = width // 4
    back = call(
        back_kernel,
        shaped((slots, 2 * width)),
        grid=(4,),
        in_specs=[whole(slots, inner)] * 3
        + [pl.BlockSpec((wide, inner), lambda i: (i, 0))] * 2
        + [pl.BlockSpec((inner, wide), lambda i: (0, i))],
        out_specs=pl.BlockSpec((slots, 2 * wide), lambda i: (0, i)),
    )(hidden, dpre, dup, gate_mat, up_mat, down_mat)
    back = lax.all_to_all(
        back.reshape(peers, capacity, 2 * width), "tp", split_axis=0, concat_axis=0, tiled=True
    ).reshape(slots, 2 * width)

    mid_2 = along(plus(in_1, part[2]), MIDDLE)
    last_out = along(far, OUTWARD)
    turned = [turned[0]] + [
        along(turned[k], tuple((i, i ^ k) for i in range(4))) for k in range(1, 4)
    ]
    end_3 = along(plus(mid_2, part[1]), ENDS)
    mid_3 = along(plus(in_2, part[3]), MIDDLE)

    layer_output, token_grad, gate_grad = call(
        home_kernel,
        [shaped((count, width)), shaped((count, width)), shaped((1, count), F32)],
        grid=(4,),
        in_specs=[
            whole(1, count),
            whole(1, count),
            pl.BlockSpec((slots, 2 * wide), lambda i: (0, i)),
            pl.BlockSpec((count, wide), lambda i: (0, i)),
        ],
        out_specs=[pl.BlockSpec((count, wide), lambda i: (0, i))] * 2 + [whole(1, count)],
        scratch_shapes=[pltpu.VMEM((count, 1), F32)],
    )(slot, gates, back, cotangent)
    down_grad = call(down_kernel, shaped((1, quarter, width)))(
        *turned, cot_a, near, across, far, far_out, last_out, end_3, mid_3, part[0]
    )
    return layer_output, token_grad, gate_grad.reshape(count, 1), down_grad


def solution(mesh):
    rows = P(("ctx", "tp"), None)
    expert = P("tp", None, None)
    line = mesh.shape["ctx"] == 4 and mesh.shape["tp"] == 8
    return jax.shard_map(
        body_line if line else body_any,
        mesh=mesh,
        in_specs=(rows, rows, rows, rows, expert, expert, expert),
        out_specs=(rows, rows, rows, P("tp", "ctx", None)),
        check_vma=False,
    )
```

```python
import functools

import jax
import jax.numpy as jnp
from jax import lax
from jax.experimental import pallas as pl
from jax.experimental.pallas import tpu as pltpu
from jax.sharding import PartitionSpec as P

BF16 = jnp.bfloat16
F32 = jnp.float32
CONTRACT_FIRST = (((0,), (0,)), ((), ()))
CONTRACT_LAST = (((1,), (1,)), ((), ()))


def expert_block(rows_in, rows_cot, gate_mat, up_mat, down_mat):
    pre_act = jnp.dot(rows_in, gate_mat, preferred_element_type=F32)
    up_act = jnp.dot(rows_in, up_mat, preferred_element_type=F32)
    sigma = jax.nn.sigmoid(pre_act)
    hidden = (pre_act * sigma * up_act).astype(BF16)
    output = jnp.dot(hidden, down_mat, preferred_element_type=F32).astype(BF16)
    dhidden = lax.dot_general(rows_cot, down_mat, CONTRACT_LAST, preferred_element_type=F32)
    dup_act = (dhidden * pre_act * sigma).astype(BF16)
    dpre_act = (dhidden * up_act * sigma * (1.0 + pre_act * (1.0 - sigma))).astype(BF16)
    first = lax.dot_general(dpre_act, gate_mat, CONTRACT_LAST, preferred_element_type=F32)
    second = lax.dot_general(dup_act, up_mat, CONTRACT_LAST, preferred_element_type=F32)
    input_grad = (first + second).astype(BF16)
    return (output, input_grad, hidden)


def body_any(tokens, cotangent, routes, gate_weights, w_gate, w_up, w_down):
    tok_rows, width = tokens.shape
    peers = lax.axis_size("tp")
    capacity = 3 * tok_rows * routes.shape[1] // (2 * peers)
    expert_ids = routes[:, 0]
    onehot = (expert_ids[:, None] == jnp.arange(peers, dtype=jnp.int32)[None, :]).astype(jnp.int32)
    rank = jnp.sum((jnp.cumsum(onehot, axis=0) - 1) * onehot, axis=1)
    slot = expert_ids * capacity + rank
    placing = (
        slot[None, :] == jnp.arange(peers * capacity, dtype=jnp.int32)[:, None]
    ).astype(BF16)
    scaled = (gate_weights * cotangent.astype(F32)).astype(BF16)
    send = jnp.dot(
        placing, jnp.concatenate([tokens, scaled], axis=1), preferred_element_type=F32
    ).astype(BF16)
    got = lax.all_to_all(
        send.reshape(peers, capacity, 2 * width), "tp", split_axis=0, concat_axis=0, tiled=True
    ).reshape(-1, 2 * width)
    got_cot = got[:, width:]
    output, input_grad, hidden = expert_block(
        got[:, :width], got_cot, w_gate[0], w_up[0], w_down[0]
    )
    back = lax.all_to_all(
        jnp.concatenate([output, input_grad], axis=1).reshape(peers, capacity, 2 * width),
        "tp", split_axis=0, concat_axis=0, tiled=True,
    ).reshape(-1, 2 * width)
    partial = lax.dot_general(hidden, got_cot, CONTRACT_FIRST, preferred_element_type=F32)
    summed = lax.psum_scatter(partial.astype(BF16), "ctx", scatter_dimension=0, tiled=True)
    home = lax.dot_general(placing, back, CONTRACT_FIRST, preferred_element_type=F32)
    out_tok = home[:, :width]
    layer_output = (gate_weights * out_tok).astype(BF16)
    gate_grad = jnp.sum(cotangent.astype(F32) * out_tok, axis=1, keepdims=True)
    return layer_output, home[:, width:].astype(BF16), gate_grad, summed[None]


VMEM_LIMIT = 24 * 1024 * 1024
TINY = pl.CostEstimate(flops=1, bytes_accessed=1, transcendentals=0)
LONG = pl.CostEstimate(flops=1, bytes_accessed=100_000_000, transcendentals=0)


def call(kernel, outs, cost=TINY, **more):
    return pl.pallas_call(
        kernel,
        out_shape=outs,
        cost_estimate=cost,
        compiler_params=pltpu.CompilerParams(vmem_limit_bytes=VMEM_LIMIT),
        **more,
    )


def shaped(shape, dtype=BF16):
    return jax.ShapeDtypeStruct(shape, dtype)


def in_hbm(array):
    return pltpu.with_memory_space_constraint(array, pltpu.HBM)


def diagonal(size):
    return lax.broadcasted_iota(jnp.int32, (size, size), 0) == lax.broadcasted_iota(
        jnp.int32, (size, size), 1
    )


def column(row):
    return jnp.sum(jnp.where(diagonal(row.shape[1]), row, 0), axis=1, keepdims=True)


def is_outer():
    here = lax.axis_index("ctx")
    return (here == 0) | (here == 3)


def scale_kernel(peers, capacity, routes, gates, cot, slot_out, scaled, to_2, to_3):
    ids = routes[...]
    count, width = cot.shape
    onehot = lax.broadcasted_iota(jnp.int32, (peers, count), 0) == ids
    upto = lax.broadcasted_iota(jnp.int32, (count, count), 0) <= lax.broadcasted_iota(
        jnp.int32, (count, count), 1
    )
    running = jnp.dot(onehot.astype(BF16), upto.astype(BF16), preferred_element_type=F32)
    rank = jnp.sum(jnp.where(onehot, running - 1.0, 0.0), axis=0, keepdims=True).astype(jnp.int32)
    slot = ids * capacity + rank
    slot_out[...] = slot
    scaled[...] = (column(gates[...]) * cot[...].astype(F32)).astype(BF16)
    half = width // 2
    outer = is_outer()

    @pl.when(outer)
    def _():
        to_2[:, :half] = scaled[:, :half]
        to_3[:, :half] = scaled[:, half:]

    @pl.when(jnp.logical_not(outer))
    def _():
        to_2[:, :half] = scaled[:, half:]
        to_3[:, :half] = scaled[:, :half]

    slots = jnp.broadcast_to(column(slot.astype(F32)), (count, to_2.shape[1] - half)).astype(BF16)
    to_2[:, half:] = slots
    to_3[:, half:] = slots


def place(placing, rows, out, at, width):
    step = 512
    for col in range(0, width, step):
        out[:, at + col : at + col + step] = jnp.dot(
            placing, rows[:, col : col + step], preferred_element_type=F32
        ).astype(BF16)


def send_kernel(slot, tok, scaled, out):
    width = tok.shape[1]
    placing = (
        lax.broadcasted_iota(jnp.int32, (out.shape[0], tok.shape[0]), 0) == slot[...]
    ).astype(BF16)
    place(placing, tok, out, 0, width)
    place(placing, scaled, out, width, width)


def remote_kernel(from_2, from_3, out):
    width = out.shape[1] // 2
    count = from_2.shape[0]
    for at, rows in ((0, from_2), (width, from_3)):
        slot = rows[:, width : width + 1].astype(F32).astype(jnp.int32)
        home = (lax.broadcasted_iota(jnp.int32, (count, out.shape[0]), 1) == slot).astype(F32)
        place(home.T.astype(BF16), rows, out, at, width)


def halves_kernel(got, keep, give):
    half = keep.shape[1]
    width = 2 * half
    outer = is_outer()

    @pl.when(outer)
    def _():
        give[...] = got[:, width : width + half]
        keep[...] = got[:, width + half :]

    @pl.when(jnp.logical_not(outer))
    def _():
        keep[...] = got[:, width : width + half]
        give[...] = got[:, width + half :]


def hidden_kernel(got, gate, up, down, hidden, dpre, dup, near, far):
    width = gate.shape[0]
    rows, cot = got.at[:, :width], got.at[:, width:]
    step = 256
    for at in range(0, gate.shape[1], step):
        cols = slice(at, at + step)
        pre_act = jnp.dot(rows[...], gate[:, cols], preferred_element_type=F32)
        up_act = jnp.dot(rows[...], up[:, cols], preferred_element_type=F32)
        dhid = lax.dot_general(cot[...], down[cols, :], CONTRACT_LAST, preferred_element_type=F32)
        sigma = 1.0 / (1.0 + jnp.exp(-pre_act))
        hidden[:, cols] = (pre_act * sigma * up_act).astype(BF16)
        dup[:, cols] = (dhid * pre_act * sigma).astype(BF16)
        dpre[:, cols] = (dhid * up_act * sigma * (1.0 + pre_act * (1.0 - sigma))).astype(BF16)
    half = near.shape[1]
    left, right = hidden[:, :half], hidden[:, half:]
    on_left = lax.axis_index("ctx") < 2

    @pl.when(on_left)
    def _():
        near[...] = left
        far[...] = right

    @pl.when(jnp.logical_not(on_left))
    def _():
        near[...] = right
        far[...] = left


def back_kernel(hidden, dpre, dup, gate, up, down, *refs):
    out = refs[-1]
    width = down.shape[1]
    step = 512
    for at in range(0, width, step):
        cols = slice(at, at + step)
        out[:, cols] = jnp.dot(hidden[...], down[:, cols], preferred_element_type=F32).astype(BF16)
        out[:, width + at : width + at + step] = (
            lax.dot_general(dpre[...], gate[cols, :], CONTRACT_LAST, preferred_element_type=F32)
            + lax.dot_general(dup[...], up[cols, :], CONTRACT_LAST, preferred_element_type=F32)
        ).astype(BF16)


def quarters_kernel(h_own, h_1, h_2, h_3, own, from_1, remote, mine, other):
    half = own.shape[1]
    even = lax.rem(lax.axis_index("ctx"), 2) == 0

    def times(left, right):
        return lax.dot_general(left[...], right, CONTRACT_FIRST, preferred_element_type=F32)

    step = 512
    for at in range(0, half, step):
        cols, later = slice(at, at + step), slice(half + at, half + at + step)
        total = (
            times(h_own, own[:, cols])
            + times(h_1, from_1[:, cols])
            + times(h_2, remote[:, cols])
            + times(h_3, remote[:, later])
        )
        rows = total.shape[0] // 2
        low, high = total[:rows].astype(BF16), total[rows:].astype(BF16)
        mine[:, cols] = jnp.where(even, low, high)
        other[:, cols] = jnp.where(even, high, low)


def home_kernel(slot, gates, back, cot, layer_output, token_grad, gate_grad):
    count, width = cot.shape
    placing = (
        lax.broadcasted_iota(jnp.int32, (count, back.shape[0]), 1) == column(slot[...])
    ).astype(BF16)
    gate = column(gates[...])
    total = jnp.zeros((count, 1), F32)
    step = 512
    for at in range(0, width, step):
        cols = slice(at, at + step)
        out_tok = jnp.dot(placing, back[:, cols], preferred_element_type=F32)
        layer_output[:, cols] = (gate * out_tok).astype(BF16)
        total += jnp.sum(cot[:, cols].astype(F32) * out_tok, axis=1, keepdims=True)
        grad_cols = slice(width + at, width + at + step)
        token_grad[:, cols] = jnp.dot(
            placing, back[:, grad_cols], preferred_element_type=F32
        ).astype(BF16)
    gate_grad[...] = jnp.sum(jnp.where(diagonal(count), total, 0.0), axis=0, keepdims=True)


def join_kernel(mine, got, out):
    half = mine.shape[1]
    outer = is_outer()

    @pl.when(outer)
    def _():
        out[0, :, :half] = got[...]
        out[0, :, half:] = mine[...]

    @pl.when(jnp.logical_not(outer))
    def _():
        out[0, :, :half] = mine[...]
        out[0, :, half:] = got[...]


def along(rows, step):
    return lax.ppermute(rows, "ctx", [(i, i ^ step) for i in range(4)])


def body_line(tokens, cotangent, routes, gate_weights, w_gate, w_up, w_down):
    count, width = tokens.shape
    peers = lax.axis_size("tp")
    capacity = 3 * count * routes.shape[1] // (2 * peers)
    slots = peers * capacity
    inner = w_gate.shape[2]
    quarter = inner // 4
    gates = gate_weights.reshape(1, count)
    whole = pl.BlockSpec()
    after = pl.BlockSpec(memory_space=pl.ANY)

    def over_tp(rows):
        wide = rows.shape[1]
        return lax.all_to_all(
            rows.reshape(peers, capacity, wide), "tp", split_axis=0, concat_axis=0, tiled=True
        ).reshape(slots, wide)

    half = width // 2
    slot, scaled, to_2, to_3 = call(
        functools.partial(scale_kernel, peers, capacity),
        [shaped((1, count), jnp.int32), pltpu.HBM((count, width), BF16)]
        + [pltpu.HBM((count, half + 128), BF16)] * 2,
    )(routes.reshape(1, count), gates, in_hbm(cotangent))
    from_2, from_3 = along(to_2, 2), along(to_3, 3)
    got = over_tp(
        call(send_kernel, pltpu.HBM((slots, 2 * width), BF16), LONG)(
            slot, in_hbm(tokens), in_hbm(scaled)
        )
    )
    remote = over_tp(
        call(remote_kernel, shaped((slots, width)))(from_2, from_3)
    )
    keep, give = call(halves_kernel, [pltpu.HBM((slots, half), BF16)] * 2)(got)
    from_1 = along(give, 1)

    gate_mat, up_mat, down_mat = w_gate[0], w_up[0], w_down[0]
    hidden, dpre, dup, near, far = call(
        hidden_kernel,
        [shaped((slots, inner))] * 3 + [pltpu.HBM((slots, inner // 2), BF16)] * 2,
    )(got, gate_mat, up_mat, down_mat)
    h_1, h_2, h_3 = along(near, 1), along(far, 2), along(far, 3)
    back = over_tp(
        call(
            back_kernel,
            pltpu.HBM((slots, 2 * width), BF16),
        )(hidden, dpre, dup, gate_mat, up_mat, down_mat)
    )

    mine, other = call(
        quarters_kernel, [shaped((quarter, half)), pltpu.HBM((quarter, half), BF16)]
    )(near, h_1, h_2, h_3, keep, from_1, remote)
    swapped = along(other, 1)

    layer_output, token_grad, gate_grad = call(
        home_kernel,
        [shaped((count, width)), shaped((count, width)), shaped((1, count), F32)],
    )(slot, gates, back, in_hbm(cotangent))
    down_grad = call(join_kernel, shaped((1, quarter, width)))(mine, swapped)
    return layer_output, token_grad, gate_grad.reshape(count, 1), down_grad


def solution(mesh):
    rows = P(("ctx", "tp"), None)
    expert = P("tp", None, None)
    line = mesh.shape["ctx"] == 4 and mesh.shape["tp"] == 8
    return jax.shard_map(
        body_line if line else body_any,
        mesh=mesh,
        in_specs=(rows, rows, rows, rows, expert, expert, expert),
        out_specs=(rows, rows, rows, P("tp", "ctx", None)),
        check_vma=False,
    )
```

```python
import functools

import jax
import jax.numpy as jnp
from jax import lax
from jax.experimental import pallas as pl
from jax.experimental.pallas import tpu as pltpu
from jax.sharding import PartitionSpec as P

BF16 = jnp.bfloat16
F32 = jnp.float32
CONTRACT_FIRST = (((0,), (0,)), ((), ()))
CONTRACT_LAST = (((1,), (1,)), ((), ()))


def expert_block(rows_in, rows_cot, gate_mat, up_mat, down_mat):
    pre_act = jnp.dot(rows_in, gate_mat, preferred_element_type=F32)
    up_act = jnp.dot(rows_in, up_mat, preferred_element_type=F32)
    sigma = jax.nn.sigmoid(pre_act)
    hidden = (pre_act * sigma * up_act).astype(BF16)
    output = jnp.dot(hidden, down_mat, preferred_element_type=F32).astype(BF16)
    dhidden = lax.dot_general(rows_cot, down_mat, CONTRACT_LAST, preferred_element_type=F32)
    dup_act = (dhidden * pre_act * sigma).astype(BF16)
    dpre_act = (dhidden * up_act * sigma * (1.0 + pre_act * (1.0 - sigma))).astype(BF16)
    first = lax.dot_general(dpre_act, gate_mat, CONTRACT_LAST, preferred_element_type=F32)
    second = lax.dot_general(dup_act, up_mat, CONTRACT_LAST, preferred_element_type=F32)
    input_grad = (first + second).astype(BF16)
    return (output, input_grad, hidden)


def body_any(tokens, cotangent, routes, gate_weights, w_gate, w_up, w_down):
    tok_rows, width = tokens.shape
    peers = lax.axis_size("tp")
    capacity = 3 * tok_rows * routes.shape[1] // (2 * peers)
    expert_ids = routes[:, 0]
    onehot = (expert_ids[:, None] == jnp.arange(peers, dtype=jnp.int32)[None, :]).astype(jnp.int32)
    rank = jnp.sum((jnp.cumsum(onehot, axis=0) - 1) * onehot, axis=1)
    slot = expert_ids * capacity + rank
    placing = (
        slot[None, :] == jnp.arange(peers * capacity, dtype=jnp.int32)[:, None]
    ).astype(BF16)
    scaled = (gate_weights * cotangent.astype(F32)).astype(BF16)
    send = jnp.dot(
        placing, jnp.concatenate([tokens, scaled], axis=1), preferred_element_type=F32
    ).astype(BF16)
    got = lax.all_to_all(
        send.reshape(peers, capacity, 2 * width), "tp", split_axis=0, concat_axis=0, tiled=True
    ).reshape(-1, 2 * width)
    got_cot = got[:, width:]
    output, input_grad, hidden = expert_block(
        got[:, :width], got_cot, w_gate[0], w_up[0], w_down[0]
    )
    back = lax.all_to_all(
        jnp.concatenate([output, input_grad], axis=1).reshape(peers, capacity, 2 * width),
        "tp", split_axis=0, concat_axis=0, tiled=True,
    ).reshape(-1, 2 * width)
    partial = lax.dot_general(hidden, got_cot, CONTRACT_FIRST, preferred_element_type=F32)
    summed = lax.psum_scatter(partial.astype(BF16), "ctx", scatter_dimension=0, tiled=True)
    home = lax.dot_general(placing, back, CONTRACT_FIRST, preferred_element_type=F32)
    out_tok = home[:, :width]
    layer_output = (gate_weights * out_tok).astype(BF16)
    gate_grad = jnp.sum(cotangent.astype(F32) * out_tok, axis=1, keepdims=True)
    return layer_output, home[:, width:].astype(BF16), gate_grad, summed[None]


WIDE = 512
VMEM_LIMIT = 24 * 1024 * 1024
TINY = pl.CostEstimate(flops=1, bytes_accessed=1, transcendentals=0)


def call(kernel, outs, cost=TINY, **more):
    return pl.pallas_call(
        kernel,
        out_shape=outs,
        cost_estimate=cost,
        compiler_params=pltpu.CompilerParams(vmem_limit_bytes=VMEM_LIMIT),
        **more,
    )


def shaped(shape, dtype=BF16):
    return jax.ShapeDtypeStruct(shape, dtype)


def in_hbm(array):
    return pltpu.with_memory_space_constraint(array, pltpu.HBM)


def diagonal(size):
    return lax.broadcasted_iota(jnp.int32, (size, size), 0) == lax.broadcasted_iota(
        jnp.int32, (size, size), 1
    )


def column(row):
    return jnp.sum(jnp.where(diagonal(row.shape[1]), row, 0), axis=1, keepdims=True)


def place(placing, rows, out, at, width):
    step = 512
    for col in range(0, width, step):
        out[:, at + col : at + col + step] = jnp.dot(
            placing, rows[:, col : col + step], preferred_element_type=F32
        ).astype(BF16)


def send_kernel(peers, capacity, routes, gates, tok, cot, slot_out, out, across, scaled):
    ids = routes[...]
    count, width = cot.shape
    onehot = lax.broadcasted_iota(jnp.int32, (peers, count), 0) == ids
    upto = lax.broadcasted_iota(jnp.int32, (count, count), 0) <= lax.broadcasted_iota(
        jnp.int32, (count, count), 1
    )
    running = jnp.dot(onehot.astype(BF16), upto.astype(BF16), preferred_element_type=F32)
    rank = jnp.sum(jnp.where(onehot, running - 1.0, 0.0), axis=0, keepdims=True).astype(jnp.int32)
    slot = ids * capacity + rank
    slot_out[...] = slot
    scaled[...] = (column(gates[...]) * cot[...].astype(F32)).astype(BF16)
    across[:, :width] = scaled[...]
    across[:, width:] = jnp.broadcast_to(
        column(slot.astype(F32)), (count, across.shape[1] - width)
    ).astype(BF16)
    placing = (
        lax.broadcasted_iota(jnp.int32, (peers * capacity, count), 0) == slot
    ).astype(BF16)
    place(placing, tok, out, 0, width)
    place(placing, scaled, out, width, width)


def remote_kernel(after, rows, out):
    count, width = rows.shape[0], out.shape[1]
    slot = rows[:, width : width + 1].astype(F32).astype(jnp.int32)
    home = (lax.broadcasted_iota(jnp.int32, (count, out.shape[0]), 1) == slot).astype(F32)
    place(home.T.astype(BF16), rows, out, 0, width)


def hidden_kernel(got, gate, up, down, hidden, dpre, dup, near, far):
    width = gate.shape[0]
    rows, cot = got.at[:, :width], got.at[:, width:]
    tile = pl.program_id(0)
    pre_act = jnp.dot(rows[...], gate[...], preferred_element_type=F32)
    up_act = jnp.dot(rows[...], up[...], preferred_element_type=F32)
    dhid = lax.dot_general(cot[...], down[...], CONTRACT_LAST, preferred_element_type=F32)
    sigma = 1.0 / (1.0 + jnp.exp(-pre_act))
    hid = (pre_act * sigma * up_act).astype(BF16)
    hidden[...] = hid
    dup[...] = (dhid * pre_act * sigma).astype(BF16)
    dpre[...] = (dhid * up_act * sigma * (1.0 + pre_act * (1.0 - sigma))).astype(BF16)
    size, half = hid.shape[1], near.shape[1]
    on_left = lax.axis_index("ctx") < 2
    for left, right, mine in ((near, far, on_left), (far, near, jnp.logical_not(on_left))):
        for t in range(2 * half // size):
            low, high = t * size, (t + 1) * size
            cut = min(max(half - low, 0), size)

            @pl.when(mine & (tile == t))
            def _():
                if cut > 0:
                    left[:, low : low + cut] = hid[:, :cut]
                if cut < size:
                    right[:, low + cut - half : high - half] = hid[:, cut:]


def back_kernel(hidden, dpre, dup, gate, up, down, out):
    wide = down.shape[1]
    out[:, :wide] = jnp.dot(hidden[...], down[...], preferred_element_type=F32).astype(BF16)
    out[:, wide:] = (
        lax.dot_general(dpre[...], gate[...], CONTRACT_LAST, preferred_element_type=F32)
        + lax.dot_general(dup[...], up[...], CONTRACT_LAST, preferred_element_type=F32)
    ).astype(BF16)


def pass_kernel(*refs):
    pass


def quarters_kernel(h_own, h_remote, got, remote, mine, other):
    width = remote.shape[1]
    even = lax.rem(lax.axis_index("ctx"), 2) == 0

    def times(left, right):
        return lax.dot_general(left[...], right, CONTRACT_FIRST, preferred_element_type=F32)

    step = 512
    for at in range(0, width, step):
        cols = slice(at, at + step)
        total = times(h_own, got[:, width + at : width + at + step]) + times(
            h_remote, remote[:, cols]
        )
        rows = total.shape[0] // 2
        low, high = total[:rows].astype(BF16), total[rows:].astype(BF16)
        mine[:, cols] = jnp.where(even, low, high)
        other[:, cols] = jnp.where(even, high, low)


def home_kernel(slot, gates, back, cot, layer_output, token_grad, gate_grad):
    count, width = cot.shape
    placing = (
        lax.broadcasted_iota(jnp.int32, (count, back.shape[0]), 1) == column(slot[...])
    ).astype(BF16)
    gate = column(gates[...])
    total = jnp.zeros((count, 1), F32)
    step = WIDE
    for at in range(0, width, step):
        cols = slice(at, at + step)
        out_tok = jnp.dot(placing, back[:, 2 * at : 2 * at + step], preferred_element_type=F32)
        layer_output[:, cols] = (gate * out_tok).astype(BF16)
        total += jnp.sum(cot[:, cols].astype(F32) * out_tok, axis=1, keepdims=True)
        grad_cols = slice(2 * at + step, 2 * at + 2 * step)
        token_grad[:, cols] = jnp.dot(
            placing, back[:, grad_cols], preferred_element_type=F32
        ).astype(BF16)
    gate_grad[...] = jnp.sum(jnp.where(diagonal(count), total, 0.0), axis=0, keepdims=True)


def add_kernel(left, right, out):
    out[0] = (left[...].astype(F32) + right[...].astype(F32)).astype(BF16)


def along(rows, step):
    return lax.ppermute(rows, "ctx", [(i, i ^ step) for i in range(4)])


def body_line(tokens, cotangent, routes, gate_weights, w_gate, w_up, w_down):
    count, width = tokens.shape
    peers = lax.axis_size("tp")
    capacity = 3 * count * routes.shape[1] // (2 * peers)
    slots = peers * capacity
    inner = w_gate.shape[2]
    quarter = inner // 4
    gates = gate_weights.reshape(1, count)
    whole = pl.BlockSpec()
    after = pl.BlockSpec(memory_space=pl.ANY)

    def over_tp(rows):
        wide = rows.shape[1]
        return lax.all_to_all(
            rows.reshape(peers, capacity, wide), "tp", split_axis=0, concat_axis=0, tiled=True
        ).reshape(slots, wide)

    slot, send, across = call(
        functools.partial(send_kernel, peers, capacity),
        [shaped((1, count), jnp.int32), pltpu.HBM((slots, 2 * width), BF16)]
        + [pltpu.HBM((count, width + 128), BF16)],
        scratch_shapes=[pltpu.VMEM((count, width), BF16)],
    )(in_hbm(routes.reshape(1, count)), in_hbm(gates), in_hbm(tokens), in_hbm(cotangent))
    rows_across = along(across, 3)
    got = over_tp(send)
    constant = lambda *shape: pl.BlockSpec(shape, lambda i: (0, 0))
    gate_mat, up_mat, down_mat = in_hbm(w_gate[0]), in_hbm(w_up[0]), in_hbm(w_down[0])
    tile = 256
    by_tile = pl.BlockSpec((slots, tile), lambda i: (0, i))
    hidden, dpre, dup, near, far = call(
        hidden_kernel,
        [pltpu.HBM((slots, inner), BF16)] * 3 + [pltpu.HBM((slots, inner // 2), BF16)] * 2,
        grid=(inner // tile,),
        in_specs=[constant(slots, 2 * width)]
        + [pl.BlockSpec((width, tile), lambda i: (0, i))] * 2
        + [pl.BlockSpec((tile, width), lambda i: (i, 0))],
        out_specs=[by_tile] * 3 + [constant(slots, inner // 2)] * 2,
    )(got, gate_mat, up_mat, down_mat)
    far_across = along(far, 3)
    remote = over_tp(
        call(remote_kernel, shaped((slots, width)), in_specs=[after, whole])(near, rows_across)
    )
    back = call(
        back_kernel,
        pltpu.HBM((slots, 2 * width), BF16),
        grid=(width // WIDE,),
        in_specs=[constant(slots, inner)] * 3
        + [pl.BlockSpec((WIDE, inner), lambda i: (i, 0))] * 2
        + [pl.BlockSpec((inner, WIDE), lambda i: (0, i))],
        out_specs=pl.BlockSpec((slots, 2 * WIDE), lambda i: (0, i)),
    )(hidden, dpre, dup, gate_mat, up_mat, down_mat)
    back = over_tp(
        call(
            pass_kernel,
            pltpu.HBM((slots, 2 * width), BF16),
            in_specs=[after] * 2,
            out_specs=after,
            input_output_aliases={0: 0},
        )(back, far_across)
    )

    mine, other = call(
        quarters_kernel, [shaped((quarter, width)), pltpu.HBM((quarter, width), BF16)]
    )(near, far_across, got, remote)
    swapped = along(other, 1)

    layer_output, token_grad, gate_grad = call(
        home_kernel,
        [shaped((count, width)), shaped((count, width)), shaped((1, count), F32)],
    )(slot, gates, back, in_hbm(cotangent))
    down_grad = call(add_kernel, shaped((1, quarter, width)))(mine, swapped)
    return layer_output, token_grad, gate_grad.reshape(count, 1), down_grad


def solution(mesh):
    rows = P(("ctx", "tp"), None)
    expert = P("tp", None, None)
    line = mesh.shape["ctx"] == 4 and mesh.shape["tp"] == 8
    return jax.shard_map(
        body_line if line else body_any,
        mesh=mesh,
        in_specs=(rows, rows, rows, rows, expert, expert, expert),
        out_specs=(rows, rows, rows, P("tp", "ctx", None)),
        check_vma=False,
    )
```

```python
import functools

import jax
import jax.numpy as jnp
from jax import lax
from jax.experimental import pallas as pl
from jax.experimental.pallas import tpu as pltpu
from jax.sharding import PartitionSpec as P

BF16 = jnp.bfloat16
F32 = jnp.float32
CONTRACT_FIRST = (((0,), (0,)), ((), ()))
CONTRACT_LAST = (((1,), (1,)), ((), ()))


def expert_block(rows_in, rows_cot, gate_mat, up_mat, down_mat):
    pre_act = jnp.dot(rows_in, gate_mat, preferred_element_type=F32)
    up_act = jnp.dot(rows_in, up_mat, preferred_element_type=F32)
    sigma = jax.nn.sigmoid(pre_act)
    hidden = (pre_act * sigma * up_act).astype(BF16)
    output = jnp.dot(hidden, down_mat, preferred_element_type=F32).astype(BF16)
    dhidden = lax.dot_general(rows_cot, down_mat, CONTRACT_LAST, preferred_element_type=F32)
    dup_act = (dhidden * pre_act * sigma).astype(BF16)
    dpre_act = (dhidden * up_act * sigma * (1.0 + pre_act * (1.0 - sigma))).astype(BF16)
    first = lax.dot_general(dpre_act, gate_mat, CONTRACT_LAST, preferred_element_type=F32)
    second = lax.dot_general(dup_act, up_mat, CONTRACT_LAST, preferred_element_type=F32)
    input_grad = (first + second).astype(BF16)
    return (output, input_grad, hidden)


def body_any(tokens, cotangent, routes, gate_weights, w_gate, w_up, w_down):
    tok_rows, width = tokens.shape
    peers = lax.axis_size("tp")
    capacity = 3 * tok_rows * routes.shape[1] // (2 * peers)
    expert_ids = routes[:, 0]
    onehot = (expert_ids[:, None] == jnp.arange(peers, dtype=jnp.int32)[None, :]).astype(jnp.int32)
    rank = jnp.sum((jnp.cumsum(onehot, axis=0) - 1) * onehot, axis=1)
    slot = expert_ids * capacity + rank
    placing = (
        slot[None, :] == jnp.arange(peers * capacity, dtype=jnp.int32)[:, None]
    ).astype(BF16)
    scaled = (gate_weights * cotangent.astype(F32)).astype(BF16)
    send = jnp.dot(
        placing, jnp.concatenate([tokens, scaled], axis=1), preferred_element_type=F32
    ).astype(BF16)
    got = lax.all_to_all(
        send.reshape(peers, capacity, 2 * width), "tp", split_axis=0, concat_axis=0, tiled=True
    ).reshape(-1, 2 * width)
    got_cot = got[:, width:]
    output, input_grad, hidden = expert_block(
        got[:, :width], got_cot, w_gate[0], w_up[0], w_down[0]
    )
    back = lax.all_to_all(
        jnp.concatenate([output, input_grad], axis=1).reshape(peers, capacity, 2 * width),
        "tp", split_axis=0, concat_axis=0, tiled=True,
    ).reshape(-1, 2 * width)
    partial = lax.dot_general(hidden, got_cot, CONTRACT_FIRST, preferred_element_type=F32)
    summed = lax.psum_scatter(partial.astype(BF16), "ctx", scatter_dimension=0, tiled=True)
    home = lax.dot_general(placing, back, CONTRACT_FIRST, preferred_element_type=F32)
    out_tok = home[:, :width]
    layer_output = (gate_weights * out_tok).astype(BF16)
    gate_grad = jnp.sum(cotangent.astype(F32) * out_tok, axis=1, keepdims=True)
    return layer_output, home[:, width:].astype(BF16), gate_grad, summed[None]


WIDE = 512
VMEM_LIMIT = 24 * 1024 * 1024
TINY = pl.CostEstimate(flops=1, bytes_accessed=1, transcendentals=0)


def call(kernel, outs, cost=TINY, **more):
    return pl.pallas_call(
        kernel,
        out_shape=outs,
        cost_estimate=cost,
        compiler_params=pltpu.CompilerParams(vmem_limit_bytes=VMEM_LIMIT),
        **more,
    )


def shaped(shape, dtype=BF16):
    return jax.ShapeDtypeStruct(shape, dtype)


def in_hbm(array):
    return pltpu.with_memory_space_constraint(array, pltpu.HBM)


def diagonal(size):
    return lax.broadcasted_iota(jnp.int32, (size, size), 0) == lax.broadcasted_iota(
        jnp.int32, (size, size), 1
    )


def column(row):
    return jnp.sum(jnp.where(diagonal(row.shape[1]), row, 0), axis=1, keepdims=True)


def place(placing, rows, out, at, width):
    step = 512
    for col in range(0, width, step):
        out[:, at + col : at + col + step] = jnp.dot(
            placing, rows[:, col : col + step], preferred_element_type=F32
        ).astype(BF16)


def send_kernel(peers, capacity, routes, gates, tok, cot, slot_out, across, *refs):
    blocks, scaled = refs[:-1], refs[-1]
    ids = routes[...]
    count, width = cot.shape
    onehot = lax.broadcasted_iota(jnp.int32, (peers, count), 0) == ids
    upto = lax.broadcasted_iota(jnp.int32, (count, count), 0) <= lax.broadcasted_iota(
        jnp.int32, (count, count), 1
    )
    running = jnp.dot(onehot.astype(BF16), upto.astype(BF16), preferred_element_type=F32)
    rank = jnp.sum(jnp.where(onehot, running - 1.0, 0.0), axis=0, keepdims=True).astype(jnp.int32)
    slot = ids * capacity + rank
    slot_out[...] = slot
    scaled[...] = (column(gates[...]) * cot[...].astype(F32)).astype(BF16)
    across[:, :width] = scaled[...]
    across[:, width:] = jnp.broadcast_to(
        column(slot.astype(F32)), (count, across.shape[1] - width)
    ).astype(BF16)
    slot = (ids ^ lax.axis_index("tp")) * capacity + rank
    placing = (
        lax.broadcasted_iota(jnp.int32, (peers * capacity, count), 0) == slot
    ).astype(BF16)
    step = 512
    for at, rows in ((0, tok), (width, scaled)):
        for col in range(0, width, step):
            placed = jnp.dot(placing, rows[:, col : col + step], preferred_element_type=F32)
            for k, block in enumerate(blocks):
                block[:, at + col : at + col + step] = placed[
                    k * capacity : (k + 1) * capacity
                ].astype(BF16)


def remote_kernel(rows, *refs):
    out = refs[-1]
    count, width = rows.shape[0], out.shape[1]
    slot = rows[:, width : width + 1].astype(F32).astype(jnp.int32)
    home = (lax.broadcasted_iota(jnp.int32, (count, out.shape[0]), 1) == slot).astype(F32)
    place(home.T.astype(BF16), rows, out, 0, width)


def tile_copies(tiles, sems):
    copies = [
        [pltpu.make_async_copy(source, target, sems.at[t, i]) for i, (source, target) in enumerate(pairs)]
        for t, pairs in enumerate(tiles)
    ]
    for tile in copies:
        for copy in tile:
            copy.start()
    return copies


def hidden_kernel(peers, *refs):
    blocks, (gate, up, down, hidden, dpre, dup, near, far, cot) = refs[:peers], refs[peers : peers + 9]
    gate_in, up_in, down_in, wide, rows, sems = refs[peers + 9 :]
    width, inner = gate.shape
    capacity = blocks[0].shape[0]
    step = inner // sems.shape[0]
    tiles = [slice(at, at + step) for at in range(0, inner, step)]
    copies = tile_copies(
        [
            (
                (gate.at[:, t], gate_in.at[:, t]),
                (up.at[:, t], up_in.at[:, t]),
                (down.at[t, :], down_in.at[t, :]),
            )
            for t in tiles
        ],
        sems,
    )
    own = lax.axis_index("tp")
    for k, block in enumerate(blocks):
        start = pl.multiple_of((own ^ k) * capacity, 8)
        wide[pl.ds(start, capacity), :] = block[...].astype(F32)
    rows[...] = wide[...].astype(BF16)
    cot[...] = rows[:, width:]
    for t, tile in zip(tiles, copies):
        for copy in tile:
            copy.wait()
        pre_act = jnp.dot(rows[:, :width], gate_in[:, t], preferred_element_type=F32)
        up_act = jnp.dot(rows[:, :width], up_in[:, t], preferred_element_type=F32)
        dhid = lax.dot_general(
            rows[:, width:], down_in[t, :], CONTRACT_LAST, preferred_element_type=F32
        )
        sigma = 1.0 / (1.0 + jnp.exp(-pre_act))
        hidden[:, t] = (pre_act * sigma * up_act).astype(BF16)
        dup[:, t] = (dhid * pre_act * sigma).astype(BF16)
        dpre[:, t] = (dhid * up_act * sigma * (1.0 + pre_act * (1.0 - sigma))).astype(BF16)
    half = near.shape[1]
    on_left = lax.axis_index("ctx") < 2
    left, right = hidden[:, :half], hidden[:, half:]
    near[...] = jnp.where(on_left, left, right)
    far[...] = jnp.where(on_left, right, left)


def back_kernel(hidden, dpre, dup, gate, up, down, out, gate_in, up_in, down_in, sems):
    width = down.shape[1]
    tiles = [slice(at, at + WIDE) for at in range(0, width, WIDE)]
    copies = tile_copies(
        [
            (
                (down.at[:, t], down_in.at[:, t]),
                (gate.at[t, :], gate_in.at[t, :]),
                (up.at[t, :], up_in.at[t, :]),
            )
            for t in tiles
        ],
        sems,
    )
    for t, tile in zip(tiles, copies):
        for copy in tile:
            copy.wait()
        at = 2 * t.start
        out[:, at : at + WIDE] = jnp.dot(
            hidden[...], down_in[:, t], preferred_element_type=F32
        ).astype(BF16)
        out[:, at + WIDE : at + 2 * WIDE] = (
            lax.dot_general(dpre[...], gate_in[t, :], CONTRACT_LAST, preferred_element_type=F32)
            + lax.dot_general(dup[...], up_in[t, :], CONTRACT_LAST, preferred_element_type=F32)
        ).astype(BF16)


def pass_kernel(*refs):
    pass


def quarters_kernel(h_own, h_remote, own, remote, mine, other):
    width = remote.shape[1]
    even = lax.rem(lax.axis_index("ctx"), 2) == 0

    def times(left, right):
        return lax.dot_general(left[...], right, CONTRACT_FIRST, preferred_element_type=F32)

    step = 512
    for at in range(0, width, step):
        cols = slice(at, at + step)
        total = times(h_own, own[:, cols]) + times(
            h_remote, remote[:, cols]
        )
        rows = total.shape[0] // 2
        low, high = total[:rows].astype(BF16), total[rows:].astype(BF16)
        mine[:, cols] = jnp.where(even, low, high)
        other[:, cols] = jnp.where(even, high, low)


def home_kernel(slot, gates, back, cot, layer_output, token_grad, gate_grad):
    count, width = cot.shape
    placing = (
        lax.broadcasted_iota(jnp.int32, (count, back.shape[0]), 1) == column(slot[...])
    ).astype(BF16)
    gate = column(gates[...])
    total = jnp.zeros((count, 1), F32)
    step = WIDE
    for at in range(0, width, step):
        cols = slice(at, at + step)
        out_tok = jnp.dot(placing, back[:, 2 * at : 2 * at + step], preferred_element_type=F32)
        layer_output[:, cols] = (gate * out_tok).astype(BF16)
        total += jnp.sum(cot[:, cols].astype(F32) * out_tok, axis=1, keepdims=True)
        grad_cols = slice(2 * at + step, 2 * at + 2 * step)
        token_grad[:, cols] = jnp.dot(
            placing, back[:, grad_cols], preferred_element_type=F32
        ).astype(BF16)
    gate_grad[...] = jnp.sum(jnp.where(diagonal(count), total, 0.0), axis=0, keepdims=True)


def add_kernel(left, right, out):
    out[0] = (left[...].astype(F32) + right[...].astype(F32)).astype(BF16)


def along(rows, step):
    return lax.ppermute(rows, "ctx", [(i, i ^ step) for i in range(4)])


def body_line(tokens, cotangent, routes, gate_weights, w_gate, w_up, w_down):
    count, width = tokens.shape
    peers = lax.axis_size("tp")
    capacity = 3 * count * routes.shape[1] // (2 * peers)
    slots = peers * capacity
    inner = w_gate.shape[2]
    quarter = inner // 4
    gates = gate_weights.reshape(1, count)
    whole = pl.BlockSpec()
    after = pl.BlockSpec(memory_space=pl.ANY)

    def over_tp(rows):
        wide = rows.shape[1]
        return lax.all_to_all(
            rows.reshape(peers, capacity, wide), "tp", split_axis=0, concat_axis=0, tiled=True
        ).reshape(slots, wide)

    slot, across, *blocks = call(
        functools.partial(send_kernel, peers, capacity),
        [shaped((1, count), jnp.int32), pltpu.HBM((count, width + 128), BF16)]
        + [pltpu.HBM((capacity, 2 * width), BF16)] * peers,
        scratch_shapes=[pltpu.VMEM((count, width), BF16)],
    )(in_hbm(routes.reshape(1, count)), in_hbm(gates), in_hbm(tokens), in_hbm(cotangent))
    rows_across = along(across, 3)
    got = [in_hbm(blocks[0])] + [
        lax.ppermute(blocks[k], "tp", [(i, i ^ k) for i in range(peers)]) for k in range(1, peers)
    ]

    weights = [in_hbm(w[0]) for w in (w_gate, w_up, w_down)]
    held = [pltpu.VMEM(w.shape, BF16) for w in weights]
    in_place = pl.BlockSpec(memory_space=pltpu.HBM)
    hidden, dpre, dup, near, far, cot = call(
        functools.partial(hidden_kernel, peers),
        [pltpu.HBM((slots, inner), BF16)] * 3
        + [pltpu.HBM((slots, inner // 2), BF16)] * 2
        + [pltpu.HBM((slots, width), BF16)],
        in_specs=[whole] * peers + [in_place] * 3,
        scratch_shapes=held
        + [
            pltpu.VMEM((slots, 2 * width), F32),
            pltpu.VMEM((slots, 2 * width), BF16),
            pltpu.SemaphoreType.DMA((3, 3)),
        ],
    )(*got, *weights)
    far_across = along(far, 3)
    remote = over_tp(
        call(
            remote_kernel, shaped((slots, width)), in_specs=[whole] + [after] * (peers - 1)
        )(rows_across, *got[1:])
    )
    back = call(
        back_kernel,
        pltpu.HBM((slots, 2 * width), BF16),
        in_specs=[whole] * 3 + [in_place] * 3,
        scratch_shapes=held + [pltpu.SemaphoreType.DMA((width // WIDE, 3))],
    )(in_hbm(hidden), in_hbm(dpre), in_hbm(dup), *weights)
    back = over_tp(
        call(
            pass_kernel,
            pltpu.HBM((slots, 2 * width), BF16),
            in_specs=[after] * 2,
            out_specs=after,
            input_output_aliases={0: 0},
        )(in_hbm(back), far_across)
    )

    mine, other = call(
        quarters_kernel, [shaped((quarter, width)), pltpu.HBM((quarter, width), BF16)]
    )(in_hbm(near), far_across, in_hbm(cot), remote)
    swapped = along(other, 1)

    layer_output, token_grad, gate_grad = call(
        home_kernel,
        [shaped((count, width)), shaped((count, width)), shaped((1, count), F32)],
    )(slot, gates, back, in_hbm(cotangent))
    down_grad = call(add_kernel, shaped((1, quarter, width)))(mine, swapped)
    return layer_output, token_grad, gate_grad.reshape(count, 1), down_grad


def solution(mesh):
    rows = P(("ctx", "tp"), None)
    expert = P("tp", None, None)
    line = mesh.shape["ctx"] == 4 and mesh.shape["tp"] == 8
    return jax.shard_map(
        body_line if line else body_any,
        mesh=mesh,
        in_specs=(rows, rows, rows, rows, expert, expert, expert),
        out_specs=(rows, rows, rows, P("tp", "ctx", None)),
        check_vma=False,
    )
```

```python
import functools

import jax
import jax.numpy as jnp
from jax import lax
from jax.experimental import pallas as pl
from jax.experimental.pallas import tpu as pltpu
from jax.sharding import PartitionSpec as P

BF16 = jnp.bfloat16
F32 = jnp.float32
CONTRACT_FIRST = (((0,), (0,)), ((), ()))
CONTRACT_LAST = (((1,), (1,)), ((), ()))


def expert_block(rows_in, rows_cot, gate_mat, up_mat, down_mat):
    pre_act = jnp.dot(rows_in, gate_mat, preferred_element_type=F32)
    up_act = jnp.dot(rows_in, up_mat, preferred_element_type=F32)
    sigma = jax.nn.sigmoid(pre_act)
    hidden = (pre_act * sigma * up_act).astype(BF16)
    output = jnp.dot(hidden, down_mat, preferred_element_type=F32).astype(BF16)
    dhidden = lax.dot_general(rows_cot, down_mat, CONTRACT_LAST, preferred_element_type=F32)
    dup_act = (dhidden * pre_act * sigma).astype(BF16)
    dpre_act = (dhidden * up_act * sigma * (1.0 + pre_act * (1.0 - sigma))).astype(BF16)
    first = lax.dot_general(dpre_act, gate_mat, CONTRACT_LAST, preferred_element_type=F32)
    second = lax.dot_general(dup_act, up_mat, CONTRACT_LAST, preferred_element_type=F32)
    input_grad = (first + second).astype(BF16)
    return (output, input_grad, hidden)


def body_any(tokens, cotangent, routes, gate_weights, w_gate, w_up, w_down):
    tok_rows, width = tokens.shape
    peers = lax.axis_size("tp")
    capacity = 3 * tok_rows * routes.shape[1] // (2 * peers)
    expert_ids = routes[:, 0]
    onehot = (expert_ids[:, None] == jnp.arange(peers, dtype=jnp.int32)[None, :]).astype(jnp.int32)
    rank = jnp.sum((jnp.cumsum(onehot, axis=0) - 1) * onehot, axis=1)
    slot = expert_ids * capacity + rank
    placing = (
        slot[None, :] == jnp.arange(peers * capacity, dtype=jnp.int32)[:, None]
    ).astype(BF16)
    scaled = (gate_weights * cotangent.astype(F32)).astype(BF16)
    send = jnp.dot(
        placing, jnp.concatenate([tokens, scaled], axis=1), preferred_element_type=F32
    ).astype(BF16)
    got = lax.all_to_all(
        send.reshape(peers, capacity, 2 * width), "tp", split_axis=0, concat_axis=0, tiled=True
    ).reshape(-1, 2 * width)
    got_cot = got[:, width:]
    output, input_grad, hidden = expert_block(
        got[:, :width], got_cot, w_gate[0], w_up[0], w_down[0]
    )
    back = lax.all_to_all(
        jnp.concatenate([output, input_grad], axis=1).reshape(peers, capacity, 2 * width),
        "tp", split_axis=0, concat_axis=0, tiled=True,
    ).reshape(-1, 2 * width)
    partial = lax.dot_general(hidden, got_cot, CONTRACT_FIRST, preferred_element_type=F32)
    summed = lax.psum_scatter(partial.astype(BF16), "ctx", scatter_dimension=0, tiled=True)
    home = lax.dot_general(placing, back, CONTRACT_FIRST, preferred_element_type=F32)
    out_tok = home[:, :width]
    layer_output = (gate_weights * out_tok).astype(BF16)
    gate_grad = jnp.sum(cotangent.astype(F32) * out_tok, axis=1, keepdims=True)
    return layer_output, home[:, width:].astype(BF16), gate_grad, summed[None]


LANES = 128
TILES = 3
TAIL = 16
WIDE = 512
VMEM_LIMIT = 24 * 1024 * 1024
TINY = pl.CostEstimate(flops=1, bytes_accessed=1, transcendentals=0)


def call(kernel, outs, cost=TINY, **more):
    return pl.pallas_call(
        kernel,
        out_shape=outs,
        cost_estimate=cost,
        compiler_params=pltpu.CompilerParams(vmem_limit_bytes=VMEM_LIMIT),
        **more,
    )


def shaped(shape, dtype=BF16):
    return jax.ShapeDtypeStruct(shape, dtype)


def in_hbm(array):
    return pltpu.with_memory_space_constraint(array, pltpu.HBM)


def diagonal(size):
    return lax.broadcasted_iota(jnp.int32, (size, size), 0) == lax.broadcasted_iota(
        jnp.int32, (size, size), 1
    )


def column(row):
    return jnp.sum(jnp.where(diagonal(row.shape[1]), row, 0), axis=1, keepdims=True)


def place(placing, rows, out, at, width):
    step = 512
    for col in range(0, width, step):
        out[:, at + col : at + col + step] = jnp.dot(
            placing, rows[:, col : col + step], preferred_element_type=F32
        ).astype(BF16)


def send_kernel(peers, capacity, routes, gates, tok, cot, slot_out, across, *refs):
    blocks, scaled = refs[:-1], refs[-1]
    ids = routes[...]
    count, width = cot.shape
    onehot = lax.broadcasted_iota(jnp.int32, (peers, count), 0) == ids
    upto = lax.broadcasted_iota(jnp.int32, (count, count), 0) <= lax.broadcasted_iota(
        jnp.int32, (count, count), 1
    )
    running = jnp.dot(onehot.astype(BF16), upto.astype(BF16), preferred_element_type=F32)
    rank = jnp.sum(jnp.where(onehot, running - 1.0, 0.0), axis=0, keepdims=True).astype(jnp.int32)
    slot = ids * capacity + rank
    slot_out[...] = slot
    scaled[...] = (column(gates[...]) * cot[...].astype(F32)).astype(BF16)
    chunks = width // LANES
    for c in range(chunks):
        across[c * count : (c + 1) * count] = scaled[:, c * LANES : (c + 1) * LANES]
    across[chunks * count :] = jnp.broadcast_to(slot.astype(F32), (TAIL, count)).astype(BF16)
    slot = (ids ^ lax.axis_index("tp")) * capacity + rank
    placing = (
        lax.broadcasted_iota(jnp.int32, (peers * capacity, count), 0) == slot
    ).astype(BF16)
    step = 512
    for at, rows in ((0, tok), (width, scaled)):
        for col in range(0, width, step):
            placed = jnp.dot(placing, rows[:, col : col + step], preferred_element_type=F32)
            for k, block in enumerate(blocks):
                block[:, at + col : at + col + step] = placed[
                    k * capacity : (k + 1) * capacity
                ].astype(BF16)


def remote_kernel(rows, *refs):
    out = refs[-1]
    count, chunks = LANES, out.shape[1] // LANES
    slot = rows[chunks * count : chunks * count + 8].astype(F32)[:1].astype(jnp.int32)
    placing = (
        lax.broadcasted_iota(jnp.int32, (out.shape[0], count), 0) == slot
    ).astype(BF16)
    group = WIDE // LANES
    for c in range(0, chunks, group):
        some = [rows[i * count : (i + 1) * count] for i in range(c, c + group)]
        out[:, c * LANES : (c + group) * LANES] = jnp.dot(
            placing, jnp.concatenate(some, axis=1), preferred_element_type=F32
        ).astype(BF16)


def staged(stages, sems, ahead=3):
    copies, used = [], 0
    for pairs in stages:
        copies.append(
            [pltpu.make_async_copy(source, target, sems.at[used + i]) for i, (source, target) in enumerate(pairs)]
        )
        used += len(pairs)
    for stage in copies[:ahead]:
        for copy in stage:
            copy.start()
    left = list(range(len(copies)))

    def arrive():
        now = left.pop(0)
        for copy in copies[now]:
            copy.wait()
        if now + ahead < len(copies):
            for copy in copies[now + ahead]:
                copy.start()

    return arrive


def hidden_kernel(order, *refs):
    peers = len(order)
    blocks, (gate, up, hidden, by_up, by_pre, near, far, cot, same) = refs[:peers], refs[peers : peers + 9]
    gate_in, up_in, wide, rows, sems = refs[peers + 9 :]
    width, inner = gate.shape
    capacity = blocks[0].shape[0]
    step = inner // TILES
    tiles = [slice(at, at + step) for at in range(0, inner, step)]
    arrive = staged(
        [((gate.at[:, t], gate_in.at[:, t]), (up.at[:, t], up_in.at[:, t])) for t in tiles], sems
    )
    own = lax.axis_index("tp")
    for k, block in zip(order, blocks):
        start = pl.multiple_of((own ^ k) * capacity, 8)
        wide[pl.ds(start, capacity), :] = block[...].astype(F32)
    rows[...] = wide[:, :width].astype(BF16)
    cot[...] = wide[:, width:].astype(BF16)
    same[...] = cot[...]
    for t in tiles:
        arrive()
        pre = jnp.dot(rows[...], gate_in[:, t], preferred_element_type=F32)
        up_act = jnp.dot(rows[...], up_in[:, t], preferred_element_type=F32)
        sigma = 1.0 / (1.0 + jnp.exp(-pre))
        silu = pre * sigma
        hidden[:, t] = (silu * up_act).astype(BF16)
        by_up[:, t] = silu.astype(BF16)
        by_pre[:, t] = (up_act * sigma * (1.0 + pre * (1.0 - sigma))).astype(BF16)
    half = near.shape[1]
    on_left = lax.axis_index("ctx") < 2
    left, right = hidden[:, :half], hidden[:, half:]
    near[...] = jnp.where(on_left, left, right)
    far[...] = jnp.where(on_left, right, left)


def back_kernel(
    hidden, by_up, by_pre, cot, gate, up, down, out,
    gate_in, up_in, down_in, dpre, dup, stage, sems, out_sems,
):
    inner, width = down.shape
    step = inner // TILES
    inner_tiles = [slice(at, at + step) for at in range(0, inner, step)]
    tiles = [slice(at, at + WIDE) for at in range(0, width, WIDE)]
    stages = [[(down.at[t, :], down_in.at[t, :])] for t in inner_tiles]
    stages += [[(gate.at[t, :], gate_in.at[t, :]), (up.at[t, :], up_in.at[t, :])] for t in tiles]
    arrive = staged(stages, sems)
    for t in inner_tiles:
        arrive()
        dhid = lax.dot_general(cot[...], down_in[t, :], CONTRACT_LAST, preferred_element_type=F32)
        dup[:, t] = (dhid * by_up[:, t].astype(F32)).astype(BF16)
        dpre[:, t] = (dhid * by_pre[:, t].astype(F32)).astype(BF16)
    leaving = []
    for i, t in enumerate(tiles):
        at = 2 * t.start
        both = slice(at, at + 2 * WIDE)
        stage[:, at : at + WIDE] = jnp.dot(
            hidden[...], down_in[:, t], preferred_element_type=F32
        ).astype(BF16)
        arrive()
        stage[:, at + WIDE : at + 2 * WIDE] = (
            lax.dot_general(dpre[...], gate_in[t, :], CONTRACT_LAST, preferred_element_type=F32)
            + lax.dot_general(dup[...], up_in[t, :], CONTRACT_LAST, preferred_element_type=F32)
        ).astype(BF16)
        leave = pltpu.make_async_copy(stage.at[:, both], out.at[:, both], out_sems.at[i])
        leave.start()
        leaving.append(leave)
    for leave in leaving:
        leave.wait()


def pass_kernel(*refs):
    pass


def quarters_kernel(h_own, h_remote, own, remote, mine, other, stage, sems):
    width = remote.shape[1]
    even = lax.rem(lax.axis_index("ctx"), 2) == 0
    left, right = h_own[...].astype(F32).T, h_remote[...].astype(F32).T
    size = left.shape[0] // 2

    def halves(turned):
        low, high = turned[:size].astype(BF16), turned[size:].astype(BF16)
        return jnp.where(even, low, high), jnp.where(even, high, low)

    (own_mine, own_other), (remote_mine, remote_other) = halves(left), halves(right)
    leaving = []
    for i, at in enumerate(range(0, width, WIDE)):
        cols = slice(at, at + WIDE)
        stage[:, cols] = (
            jnp.dot(own_other, own[:, cols], preferred_element_type=F32)
            + jnp.dot(remote_other, remote[:, cols], preferred_element_type=F32)
        ).astype(BF16)
        leave = pltpu.make_async_copy(stage.at[:, cols], other.at[:, cols], sems.at[i])
        leave.start()
        leaving.append(leave)
    for at in range(0, width, WIDE):
        cols = slice(at, at + WIDE)
        mine[:, cols] = (
            jnp.dot(own_mine, own[:, cols], preferred_element_type=F32)
            + jnp.dot(remote_mine, remote[:, cols], preferred_element_type=F32)
        ).astype(BF16)
    for leave in leaving:
        leave.wait()


def home_kernel(slot, gates, back, cot, layer_output, token_grad, gate_grad):
    count, width = cot.shape
    placing = (
        lax.broadcasted_iota(jnp.int32, (count, back.shape[0]), 1) == column(slot[...])
    ).astype(BF16)
    gate = column(gates[...])
    total = jnp.zeros((count, 1), F32)
    step = WIDE
    for at in range(0, width, step):
        cols = slice(at, at + step)
        out_tok = jnp.dot(placing, back[:, 2 * at : 2 * at + step], preferred_element_type=F32)
        layer_output[:, cols] = (gate * out_tok).astype(BF16)
        total += jnp.sum(cot[:, cols].astype(F32) * out_tok, axis=1, keepdims=True)
        grad_cols = slice(2 * at + step, 2 * at + 2 * step)
        token_grad[:, cols] = jnp.dot(
            placing, back[:, grad_cols], preferred_element_type=F32
        ).astype(BF16)
    gate_grad[...] = jnp.sum(jnp.where(diagonal(count), total, 0.0), axis=0, keepdims=True)


def add_kernel(left, right, out):
    out[0] = (left[...].astype(F32) + right[...].astype(F32)).astype(BF16)


def along(rows, step):
    return lax.ppermute(rows, "ctx", [(i, i ^ step) for i in range(4)])


def body_line(tokens, cotangent, routes, gate_weights, w_gate, w_up, w_down):
    count, width = tokens.shape
    peers = lax.axis_size("tp")
    capacity = 3 * count * routes.shape[1] // (2 * peers)
    slots = peers * capacity
    inner = w_gate.shape[2]
    quarter = inner // 4
    gates = gate_weights.reshape(1, count)
    whole, in_place = pl.BlockSpec(), pl.BlockSpec(memory_space=pltpu.HBM)
    after = pl.BlockSpec(memory_space=pl.ANY)

    def over_tp(rows):
        wide = rows.shape[1]
        return lax.all_to_all(
            rows.reshape(peers, capacity, wide), "tp", split_axis=0, concat_axis=0, tiled=True
        ).reshape(slots, wide)

    slot, across, *blocks = call(
        functools.partial(send_kernel, peers, capacity),
        [
            shaped((1, count), jnp.int32),
            pltpu.HBM((width // LANES * count + TAIL, LANES), BF16),
        ]
        + [pltpu.HBM((capacity, 2 * width), BF16)] * peers,
        scratch_shapes=[pltpu.VMEM((count, width), BF16)],
    )(in_hbm(routes.reshape(1, count)), in_hbm(gates), in_hbm(tokens), in_hbm(cotangent))
    rows_across = along(across, 3)
    got = {0: in_hbm(blocks[0])}
    for k in range(1, peers):
        got[k] = lax.ppermute(blocks[k], "tp", [(i, i ^ k) for i in range(peers)])
    order = (6, 7, 4, 5, 2, 3, 1, 0)
    got = [got[k] for k in order]

    gate_mat, up_mat, down_mat = [in_hbm(w[0]) for w in (w_gate, w_up, w_down)]
    held = [pltpu.VMEM((width, inner), BF16)] * 2
    dma = pltpu.SemaphoreType.DMA
    hidden, by_up, by_pre, near, far, cot, same = call(
        functools.partial(hidden_kernel, order),
        [shaped((slots, inner))] * 3
        + [pltpu.HBM((slots, inner // 2), BF16)] * 2
        + [shaped((slots, width)), pltpu.HBM((slots, width), BF16)],
        in_specs=[whole] * peers + [in_place] * 2,
        scratch_shapes=held
        + [
            pltpu.VMEM((slots, 2 * width), F32),
            pltpu.VMEM((slots, width), BF16),
            dma((2 * TILES,)),
        ],
    )(*got, gate_mat, up_mat)
    near, same = in_hbm(near), in_hbm(same)
    far_across = along(far, 3)
    remote = over_tp(
        call(
            remote_kernel, shaped((slots, width)), in_specs=[whole] + [after] * (peers - 1)
        )(rows_across, *[g for k, g in zip(order, got) if k])
    )
    tiles = width // WIDE
    back = call(
        back_kernel,
        pltpu.HBM((slots, 2 * width), BF16),
        in_specs=[whole] * 4 + [in_place] * 3,
        out_specs=in_place,
        scratch_shapes=held
        + [pltpu.VMEM((inner, width), BF16)]
        + [pltpu.VMEM((slots, inner), BF16)] * 2
        + [pltpu.VMEM((slots, 2 * width), BF16), dma((TILES + 2 * tiles,)), dma((tiles,))],
    )(hidden, by_up, by_pre, cot, gate_mat, up_mat, down_mat)
    back = over_tp(
        call(
            pass_kernel,
            pltpu.HBM((slots, 2 * width), BF16),
            in_specs=[after] * 2,
            out_specs=after,
            input_output_aliases={0: 0},
        )(in_hbm(back), far_across)
    )

    mine, other = call(
        quarters_kernel,
        [shaped((quarter, width)), pltpu.HBM((quarter, width), BF16)],
        out_specs=[whole, in_place],
        scratch_shapes=[
            pltpu.VMEM((quarter, width), BF16),
            pltpu.SemaphoreType.DMA((width // WIDE,)),
        ],
    )(near, far_across, same, remote)
    swapped = along(other, 1)

    layer_output, token_grad, gate_grad = call(
        home_kernel,
        [shaped((count, width)), shaped((count, width)), shaped((1, count), F32)],
    )(slot, gates, back, in_hbm(cotangent))
    down_grad = call(add_kernel, shaped((1, quarter, width)))(mine, swapped)
    return layer_output, token_grad, gate_grad.reshape(count, 1), down_grad


def solution(mesh):
    rows = P(("ctx", "tp"), None)
    expert = P("tp", None, None)
    line = mesh.shape["ctx"] == 4 and mesh.shape["tp"] == 8
    return jax.shard_map(
        body_line if line else body_any,
        mesh=mesh,
        in_specs=(rows, rows, rows, rows, expert, expert, expert),
        out_specs=(rows, rows, rows, P("tp", "ctx", None)),
        check_vma=False,
    )
```

```python
import functools

import jax
import jax.numpy as jnp
from jax import lax
from jax.experimental import pallas as pl
from jax.experimental.pallas import tpu as pltpu
from jax.sharding import PartitionSpec as P

BF16 = jnp.bfloat16
F32 = jnp.float32
CONTRACT_FIRST = (((0,), (0,)), ((), ()))
CONTRACT_LAST = (((1,), (1,)), ((), ()))


def expert_block(rows_in, rows_cot, gate_mat, up_mat, down_mat):
    pre_act = jnp.dot(rows_in, gate_mat, preferred_element_type=F32)
    up_act = jnp.dot(rows_in, up_mat, preferred_element_type=F32)
    sigma = jax.nn.sigmoid(pre_act)
    hidden = (pre_act * sigma * up_act).astype(BF16)
    output = jnp.dot(hidden, down_mat, preferred_element_type=F32).astype(BF16)
    dhidden = lax.dot_general(rows_cot, down_mat, CONTRACT_LAST, preferred_element_type=F32)
    dup_act = (dhidden * pre_act * sigma).astype(BF16)
    dpre_act = (dhidden * up_act * sigma * (1.0 + pre_act * (1.0 - sigma))).astype(BF16)
    first = lax.dot_general(dpre_act, gate_mat, CONTRACT_LAST, preferred_element_type=F32)
    second = lax.dot_general(dup_act, up_mat, CONTRACT_LAST, preferred_element_type=F32)
    input_grad = (first + second).astype(BF16)
    return (output, input_grad, hidden)


def body_any(tokens, cotangent, routes, gate_weights, w_gate, w_up, w_down):
    tok_rows, width = tokens.shape
    peers = lax.axis_size("tp")
    capacity = 3 * tok_rows * routes.shape[1] // (2 * peers)
    expert_ids = routes[:, 0]
    onehot = (expert_ids[:, None] == jnp.arange(peers, dtype=jnp.int32)[None, :]).astype(jnp.int32)
    rank = jnp.sum((jnp.cumsum(onehot, axis=0) - 1) * onehot, axis=1)
    slot = expert_ids * capacity + rank
    placing = (
        slot[None, :] == jnp.arange(peers * capacity, dtype=jnp.int32)[:, None]
    ).astype(BF16)
    scaled = (gate_weights * cotangent.astype(F32)).astype(BF16)
    send = jnp.dot(
        placing, jnp.concatenate([tokens, scaled], axis=1), preferred_element_type=F32
    ).astype(BF16)
    got = lax.all_to_all(
        send.reshape(peers, capacity, 2 * width), "tp", split_axis=0, concat_axis=0, tiled=True
    ).reshape(-1, 2 * width)
    got_cot = got[:, width:]
    output, input_grad, hidden = expert_block(
        got[:, :width], got_cot, w_gate[0], w_up[0], w_down[0]
    )
    back = lax.all_to_all(
        jnp.concatenate([output, input_grad], axis=1).reshape(peers, capacity, 2 * width),
        "tp", split_axis=0, concat_axis=0, tiled=True,
    ).reshape(-1, 2 * width)
    partial = lax.dot_general(hidden, got_cot, CONTRACT_FIRST, preferred_element_type=F32)
    summed = lax.psum_scatter(partial.astype(BF16), "ctx", scatter_dimension=0, tiled=True)
    home = lax.dot_general(placing, back, CONTRACT_FIRST, preferred_element_type=F32)
    out_tok = home[:, :width]
    layer_output = (gate_weights * out_tok).astype(BF16)
    gate_grad = jnp.sum(cotangent.astype(F32) * out_tok, axis=1, keepdims=True)
    return layer_output, home[:, width:].astype(BF16), gate_grad, summed[None]


LANES = 128
TILES, BACK_TILES = 3, 2
TAIL = 16
WIDE = 1024
VMEM_LIMIT = 24 * 1024 * 1024
TINY = pl.CostEstimate(flops=1, bytes_accessed=1, transcendentals=0)


def call(kernel, outs, cost=TINY, **more):
    return pl.pallas_call(
        kernel,
        out_shape=outs,
        cost_estimate=cost,
        compiler_params=pltpu.CompilerParams(vmem_limit_bytes=VMEM_LIMIT),
        **more,
    )


def shaped(shape, dtype=BF16):
    return jax.ShapeDtypeStruct(shape, dtype)


def in_hbm(array):
    return pltpu.with_memory_space_constraint(array, pltpu.HBM)


def diagonal(size):
    return lax.broadcasted_iota(jnp.int32, (size, size), 0) == lax.broadcasted_iota(
        jnp.int32, (size, size), 1
    )


def column(row):
    return jnp.sum(jnp.where(diagonal(row.shape[1]), row, 0), axis=1, keepdims=True)


def place(placing, rows, out, at, width):
    step = 512
    for col in range(0, width, step):
        out[:, at + col : at + col + step] = jnp.dot(
            placing, rows[:, col : col + step], preferred_element_type=F32
        ).astype(BF16)


def send_kernel(peers, capacity, routes, gates, tok, cot, slot_out, across, *refs):
    blocks, scaled = refs[:-1], refs[-1]
    ids = routes[...]
    count, width = cot.shape
    onehot = lax.broadcasted_iota(jnp.int32, (peers, count), 0) == ids
    upto = lax.broadcasted_iota(jnp.int32, (count, count), 0) <= lax.broadcasted_iota(
        jnp.int32, (count, count), 1
    )
    running = jnp.dot(onehot.astype(BF16), upto.astype(BF16), preferred_element_type=F32)
    rank = jnp.sum(jnp.where(onehot, running - 1.0, 0.0), axis=0, keepdims=True).astype(jnp.int32)
    slot = ids * capacity + rank
    slot_out[...] = slot
    scaled[...] = (column(gates[...]) * cot[...].astype(F32)).astype(BF16)
    chunks = width // LANES
    for c in range(chunks):
        across[c * count : (c + 1) * count] = scaled[:, c * LANES : (c + 1) * LANES]
    across[chunks * count :] = jnp.broadcast_to(slot.astype(F32), (TAIL, count)).astype(BF16)
    slot = (ids ^ lax.axis_index("tp")) * capacity + rank
    placing = (
        lax.broadcasted_iota(jnp.int32, (peers * capacity, count), 0) == slot
    ).astype(BF16)
    step = 512
    for at, rows in ((0, tok), (width, scaled)):
        for col in range(0, width, step):
            placed = jnp.dot(placing, rows[:, col : col + step], preferred_element_type=F32)
            for k, block in enumerate(blocks):
                block[:, at + col : at + col + step] = placed[
                    k * capacity : (k + 1) * capacity
                ].astype(BF16)


def remote_kernel(rows, *refs):
    out = refs[-1]
    count, chunks = LANES, out.shape[1] // LANES
    slot = rows[chunks * count : chunks * count + 8].astype(F32)[:1].astype(jnp.int32)
    placing = (
        lax.broadcasted_iota(jnp.int32, (out.shape[0], count), 0) == slot
    ).astype(BF16)
    group = WIDE // LANES
    for c in range(0, chunks, group):
        some = [rows[i * count : (i + 1) * count] for i in range(c, c + group)]
        out[:, c * LANES : (c + group) * LANES] = jnp.dot(
            placing, jnp.concatenate(some, axis=1), preferred_element_type=F32
        ).astype(BF16)


def staged(stages, sems, ahead=3):
    copies, used = [], 0
    for pairs in stages:
        copies.append(
            [pltpu.make_async_copy(source, target, sems.at[used + i]) for i, (source, target) in enumerate(pairs)]
        )
        used += len(pairs)
    for stage in copies[:ahead]:
        for copy in stage:
            copy.start()
    left = list(range(len(copies)))

    def arrive():
        now = left.pop(0)
        for copy in copies[now]:
            copy.wait()
        if now + ahead < len(copies):
            for copy in copies[now + ahead]:
                copy.start()

    return arrive


def hidden_kernel(order, *refs):
    peers = len(order)
    blocks, (gate, up, hidden, by_up, by_pre, near, far, cot, same) = refs[:peers], refs[peers : peers + 9]
    gate_in, up_in, wide, rows, sems = refs[peers + 9 :]
    width, inner = gate.shape
    capacity = blocks[0].shape[0]
    step = inner // TILES
    tiles = [slice(at, at + step) for at in range(0, inner, step)]
    arrive = staged(
        [((gate.at[:, t], gate_in.at[:, t]), (up.at[:, t], up_in.at[:, t])) for t in tiles], sems
    )
    own = lax.axis_index("tp")
    for k, block in zip(order, blocks):
        start = pl.multiple_of((own ^ k) * capacity, 8)
        wide[pl.ds(start, capacity), :] = block[...].astype(F32)
    rows[...] = wide[:, :width].astype(BF16)
    cot[...] = wide[:, width:].astype(BF16)
    same[...] = cot[...]
    for t in tiles:
        arrive()
        pre = jnp.dot(rows[...], gate_in[:, t], preferred_element_type=F32)
        up_act = jnp.dot(rows[...], up_in[:, t], preferred_element_type=F32)
        sigma = 1.0 / (1.0 + jnp.exp(-pre))
        silu = pre * sigma
        hidden[:, t] = (silu * up_act).astype(BF16)
        by_up[:, t] = silu.astype(BF16)
        by_pre[:, t] = (up_act * sigma * (1.0 + pre * (1.0 - sigma))).astype(BF16)
    half = near.shape[1]
    on_left = lax.axis_index("ctx") < 2
    left, right = hidden[:, :half], hidden[:, half:]
    near[...] = jnp.where(on_left, left, right)
    far[...] = jnp.where(on_left, right, left)


def back_kernel(
    hidden, by_up, by_pre, cot, gate, up, down, out,
    gate_in, up_in, down_in, dpre, dup, stage, sems, out_sems,
):
    inner, width = down.shape
    step = inner // BACK_TILES
    inner_tiles = [slice(at, at + step) for at in range(0, inner, step)]
    tiles = [slice(at, at + WIDE) for at in range(0, width, WIDE)]
    stages = [[(down.at[t, :], down_in.at[t, :])] for t in inner_tiles]
    stages += [[(gate.at[t, :], gate_in.at[t, :]), (up.at[t, :], up_in.at[t, :])] for t in tiles]
    arrive = staged(stages, sems)
    for t in inner_tiles:
        arrive()
        dhid = lax.dot_general(cot[...], down_in[t, :], CONTRACT_LAST, preferred_element_type=F32)
        dup[:, t] = (dhid * by_up[:, t].astype(F32)).astype(BF16)
        dpre[:, t] = (dhid * by_pre[:, t].astype(F32)).astype(BF16)
    leaving = []
    for i, t in enumerate(tiles):
        at = 2 * t.start
        both = slice(at, at + 2 * WIDE)
        stage[:, at : at + WIDE] = jnp.dot(
            hidden[...], down_in[:, t], preferred_element_type=F32
        ).astype(BF16)
        arrive()
        stage[:, at + WIDE : at + 2 * WIDE] = (
            lax.dot_general(dpre[...], gate_in[t, :], CONTRACT_LAST, preferred_element_type=F32)
            + lax.dot_general(dup[...], up_in[t, :], CONTRACT_LAST, preferred_element_type=F32)
        ).astype(BF16)
        leave = pltpu.make_async_copy(stage.at[:, both], out.at[:, both], out_sems.at[i])
        leave.start()
        leaving.append(leave)
    for leave in leaving:
        leave.wait()


def pass_kernel(*refs):
    pass


def quarters_kernel(h_own, h_remote, own, remote, mine, other, stage, sems):
    width = remote.shape[1]
    even = lax.rem(lax.axis_index("ctx"), 2) == 0
    left, right = h_own[...].astype(F32).T, h_remote[...].astype(F32).T
    size = left.shape[0] // 2

    def halves(turned):
        low, high = turned[:size].astype(BF16), turned[size:].astype(BF16)
        return jnp.where(even, low, high), jnp.where(even, high, low)

    (own_mine, own_other), (remote_mine, remote_other) = halves(left), halves(right)
    leaving = []
    for i, at in enumerate(range(0, width, WIDE)):
        cols = slice(at, at + WIDE)
        stage[:, cols] = (
            jnp.dot(own_other, own[:, cols], preferred_element_type=F32)
            + jnp.dot(remote_other, remote[:, cols], preferred_element_type=F32)
        ).astype(BF16)
        leave = pltpu.make_async_copy(stage.at[:, cols], other.at[:, cols], sems.at[i])
        leave.start()
        leaving.append(leave)
    for at in range(0, width, WIDE):
        cols = slice(at, at + WIDE)
        mine[:, cols] = (
            jnp.dot(own_mine, own[:, cols], preferred_element_type=F32)
            + jnp.dot(remote_mine, remote[:, cols], preferred_element_type=F32)
        ).astype(BF16)
    for leave in leaving:
        leave.wait()


def home_kernel(slot, gates, back, cot, layer_output, token_grad, gate_grad):
    count, width = cot.shape
    placing = (
        lax.broadcasted_iota(jnp.int32, (count, back.shape[0]), 1) == column(slot[...])
    ).astype(BF16)
    gate = column(gates[...])
    total = jnp.zeros((count, 1), F32)
    step = WIDE
    for at in range(0, width, step):
        cols = slice(at, at + step)
        out_tok = jnp.dot(placing, back[:, 2 * at : 2 * at + step], preferred_element_type=F32)
        layer_output[:, cols] = (gate * out_tok).astype(BF16)
        total += jnp.sum(cot[:, cols].astype(F32) * out_tok, axis=1, keepdims=True)
        grad_cols = slice(2 * at + step, 2 * at + 2 * step)
        token_grad[:, cols] = jnp.dot(
            placing, back[:, grad_cols], preferred_element_type=F32
        ).astype(BF16)
    gate_grad[...] = jnp.sum(jnp.where(diagonal(count), total, 0.0), axis=0, keepdims=True)


def add_kernel(left, right, out):
    out[0] = (left[...].astype(F32) + right[...].astype(F32)).astype(BF16)


def along(rows, step):
    return lax.ppermute(rows, "ctx", [(i, i ^ step) for i in range(4)])


def body_line(tokens, cotangent, routes, gate_weights, w_gate, w_up, w_down):
    count, width = tokens.shape
    peers = lax.axis_size("tp")
    capacity = 3 * count * routes.shape[1] // (2 * peers)
    slots = peers * capacity
    inner = w_gate.shape[2]
    quarter = inner // 4
    gates = gate_weights.reshape(1, count)
    whole, in_place = pl.BlockSpec(), pl.BlockSpec(memory_space=pltpu.HBM)
    after = pl.BlockSpec(memory_space=pl.ANY)

    def over_tp(rows):
        wide = rows.shape[1]
        return lax.all_to_all(
            rows.reshape(peers, capacity, wide), "tp", split_axis=0, concat_axis=0, tiled=True
        ).reshape(slots, wide)

    slot, across, *blocks = call(
        functools.partial(send_kernel, peers, capacity),
        [
            shaped((1, count), jnp.int32),
            pltpu.HBM((width // LANES * count + TAIL, LANES), BF16),
        ]
        + [pltpu.HBM((capacity, 2 * width), BF16)] * peers,
        scratch_shapes=[pltpu.VMEM((count, width), BF16)],
    )(in_hbm(routes.reshape(1, count)), in_hbm(gates), in_hbm(tokens), in_hbm(cotangent))
    rows_across = along(across, 3)
    got = {0: in_hbm(blocks[0])}
    for k in range(1, peers):
        got[k] = lax.ppermute(blocks[k], "tp", [(i, i ^ k) for i in range(peers)])
    order = (6, 7, 4, 5, 2, 3, 1, 0)
    got = [got[k] for k in order]

    gate_mat, up_mat, down_mat = [in_hbm(w[0]) for w in (w_gate, w_up, w_down)]
    held = [pltpu.VMEM((width, inner), BF16)] * 2
    dma = pltpu.SemaphoreType.DMA
    hidden, by_up, by_pre, near, far, cot, same = call(
        functools.partial(hidden_kernel, order),
        [shaped((slots, inner))] * 3
        + [pltpu.HBM((slots, inner // 2), BF16)] * 2
        + [shaped((slots, width)), pltpu.HBM((slots, width), BF16)],
        in_specs=[whole] * peers + [in_place] * 2,
        scratch_shapes=held
        + [
            pltpu.VMEM((slots, 2 * width), F32),
            pltpu.VMEM((slots, width), BF16),
            dma((2 * TILES,)),
        ],
    )(*got, gate_mat, up_mat)
    near, same = in_hbm(near), in_hbm(same)
    far_across = along(far, 3)
    remote = over_tp(
        call(
            remote_kernel, shaped((slots, width)), in_specs=[whole] + [after] * (peers - 1)
        )(rows_across, *[g for k, g in zip(order, got) if k])
    )
    tiles = width // WIDE
    back = call(
        back_kernel,
        pltpu.HBM((slots, 2 * width), BF16),
        in_specs=[whole] * 4 + [in_place] * 3,
        out_specs=in_place,
        scratch_shapes=held
        + [pltpu.VMEM((inner, width), BF16)]
        + [pltpu.VMEM((slots, inner), BF16)] * 2
        + [pltpu.VMEM((slots, 2 * width), BF16), dma((BACK_TILES + 2 * tiles,)), dma((tiles,))],
    )(hidden, by_up, by_pre, cot, gate_mat, up_mat, down_mat)
    back = over_tp(
        call(
            pass_kernel,
            pltpu.HBM((slots, 2 * width), BF16),
            in_specs=[after] * 2,
            out_specs=after,
            input_output_aliases={0: 0},
        )(in_hbm(back), far_across)
    )

    mine, other = call(
        quarters_kernel,
        [shaped((quarter, width)), pltpu.HBM((quarter, width), BF16)],
        out_specs=[whole, in_place],
        scratch_shapes=[
            pltpu.VMEM((quarter, width), BF16),
            pltpu.SemaphoreType.DMA((width // WIDE,)),
        ],
    )(near, far_across, same, remote)
    swapped = along(other, 1)

    layer_output, token_grad, gate_grad = call(
        home_kernel,
        [shaped((count, width)), shaped((count, width)), shaped((1, count), F32)],
    )(slot, gates, back, in_hbm(cotangent))
    down_grad = call(add_kernel, shaped((1, quarter, width)))(mine, swapped)
    return layer_output, token_grad, gate_grad.reshape(count, 1), down_grad


def solution(mesh):
    rows = P(("ctx", "tp"), None)
    expert = P("tp", None, None)
    line = mesh.shape["ctx"] == 4 and mesh.shape["tp"] == 8
    return jax.shard_map(
        body_line if line else body_any,
        mesh=mesh,
        in_specs=(rows, rows, rows, rows, expert, expert, expert),
        out_specs=(rows, rows, rows, P("tp", "ctx", None)),
        check_vma=False,
    )
```

```python
import functools

import jax
import jax.numpy as jnp
from jax import lax
from jax.experimental import pallas as pl
from jax.experimental.pallas import tpu as pltpu
from jax.sharding import PartitionSpec as P

BF16 = jnp.bfloat16
F32 = jnp.float32
CONTRACT_FIRST = (((0,), (0,)), ((), ()))
CONTRACT_LAST = (((1,), (1,)), ((), ()))


def expert_block(rows_in, rows_cot, gate_mat, up_mat, down_mat):
    pre_act = jnp.dot(rows_in, gate_mat, preferred_element_type=F32)
    up_act = jnp.dot(rows_in, up_mat, preferred_element_type=F32)
    sigma = jax.nn.sigmoid(pre_act)
    hidden = (pre_act * sigma * up_act).astype(BF16)
    output = jnp.dot(hidden, down_mat, preferred_element_type=F32).astype(BF16)
    dhidden = lax.dot_general(rows_cot, down_mat, CONTRACT_LAST, preferred_element_type=F32)
    dup_act = (dhidden * pre_act * sigma).astype(BF16)
    dpre_act = (dhidden * up_act * sigma * (1.0 + pre_act * (1.0 - sigma))).astype(BF16)
    first = lax.dot_general(dpre_act, gate_mat, CONTRACT_LAST, preferred_element_type=F32)
    second = lax.dot_general(dup_act, up_mat, CONTRACT_LAST, preferred_element_type=F32)
    input_grad = (first + second).astype(BF16)
    return (output, input_grad, hidden)


def body_any(tokens, cotangent, routes, gate_weights, w_gate, w_up, w_down):
    tok_rows, width = tokens.shape
    peers = lax.axis_size("tp")
    capacity = 3 * tok_rows * routes.shape[1] // (2 * peers)
    expert_ids = routes[:, 0]
    onehot = (expert_ids[:, None] == jnp.arange(peers, dtype=jnp.int32)[None, :]).astype(jnp.int32)
    rank = jnp.sum((jnp.cumsum(onehot, axis=0) - 1) * onehot, axis=1)
    slot = expert_ids * capacity + rank
    placing = (
        slot[None, :] == jnp.arange(peers * capacity, dtype=jnp.int32)[:, None]
    ).astype(BF16)
    scaled = (gate_weights * cotangent.astype(F32)).astype(BF16)
    send = jnp.dot(
        placing, jnp.concatenate([tokens, scaled], axis=1), preferred_element_type=F32
    ).astype(BF16)
    got = lax.all_to_all(
        send.reshape(peers, capacity, 2 * width), "tp", split_axis=0, concat_axis=0, tiled=True
    ).reshape(-1, 2 * width)
    got_cot = got[:, width:]
    output, input_grad, hidden = expert_block(
        got[:, :width], got_cot, w_gate[0], w_up[0], w_down[0]
    )
    back = lax.all_to_all(
        jnp.concatenate([output, input_grad], axis=1).reshape(peers, capacity, 2 * width),
        "tp", split_axis=0, concat_axis=0, tiled=True,
    ).reshape(-1, 2 * width)
    partial = lax.dot_general(hidden, got_cot, CONTRACT_FIRST, preferred_element_type=F32)
    summed = lax.psum_scatter(partial.astype(BF16), "ctx", scatter_dimension=0, tiled=True)
    home = lax.dot_general(placing, back, CONTRACT_FIRST, preferred_element_type=F32)
    out_tok = home[:, :width]
    layer_output = (gate_weights * out_tok).astype(BF16)
    gate_grad = jnp.sum(cotangent.astype(F32) * out_tok, axis=1, keepdims=True)
    return layer_output, home[:, width:].astype(BF16), gate_grad, summed[None]


LANES = 128
TILES, BACK_TILES = 3, 2
TAIL = 16
WIDE = 1024
VMEM_LIMIT = 24 * 1024 * 1024
TINY = pl.CostEstimate(flops=1, bytes_accessed=1, transcendentals=0)


def call(kernel, outs, cost=TINY, **more):
    return pl.pallas_call(
        kernel,
        out_shape=outs,
        cost_estimate=cost,
        compiler_params=pltpu.CompilerParams(vmem_limit_bytes=VMEM_LIMIT),
        **more,
    )


def shaped(shape, dtype=BF16):
    return jax.ShapeDtypeStruct(shape, dtype)


def in_hbm(array):
    return pltpu.with_memory_space_constraint(array, pltpu.HBM)


def diagonal(size):
    return lax.broadcasted_iota(jnp.int32, (size, size), 0) == lax.broadcasted_iota(
        jnp.int32, (size, size), 1
    )


def column(row):
    return jnp.sum(jnp.where(diagonal(row.shape[1]), row, 0), axis=1, keepdims=True)


def place(placing, rows, out, at, width):
    step = 512
    for col in range(0, width, step):
        out[:, at + col : at + col + step] = jnp.dot(
            placing, rows[:, col : col + step], preferred_element_type=F32
        ).astype(BF16)


def send_kernel(peers, capacity, routes, gates, tok, cot, slot_out, across, *refs):
    blocks, scaled = refs[:-1], refs[-1]
    ids = routes[...]
    count, width = cot.shape
    onehot = lax.broadcasted_iota(jnp.int32, (peers, count), 0) == ids
    upto = lax.broadcasted_iota(jnp.int32, (count, count), 0) <= lax.broadcasted_iota(
        jnp.int32, (count, count), 1
    )
    running = jnp.dot(onehot.astype(BF16), upto.astype(BF16), preferred_element_type=F32)
    rank = jnp.sum(jnp.where(onehot, running - 1.0, 0.0), axis=0, keepdims=True).astype(jnp.int32)
    slot = ids * capacity + rank
    slot_out[0:1] = slot
    scaled[...] = (column(gates[...]) * cot[...].astype(F32)).astype(BF16)
    chunks = width // LANES
    for c in range(chunks):
        across[c * count : (c + 1) * count] = scaled[:, c * LANES : (c + 1) * LANES]
    across[chunks * count :] = jnp.broadcast_to(slot.astype(F32), (TAIL, count)).astype(BF16)
    slot = (ids ^ lax.axis_index("tp")) * capacity + rank
    slot_out[1:2] = slot
    placing = (
        lax.broadcasted_iota(jnp.int32, (peers * capacity, count), 0) == slot
    ).astype(BF16)
    step = 512
    for at, rows in ((0, tok), (width, scaled)):
        for col in range(0, width, step):
            placed = jnp.dot(placing, rows[:, col : col + step], preferred_element_type=F32)
            for k, block in enumerate(blocks):
                block[:, at + col : at + col + step] = placed[
                    k * capacity : (k + 1) * capacity
                ].astype(BF16)


def remote_kernel(rows, *refs):
    out = refs[-1]
    count, chunks = LANES, out.shape[1] // LANES
    slot = rows[chunks * count : chunks * count + 8].astype(F32)[:1].astype(jnp.int32)
    placing = (
        lax.broadcasted_iota(jnp.int32, (out.shape[0], count), 0) == slot
    ).astype(BF16)
    group = WIDE // LANES
    for c in range(0, chunks, group):
        some = [rows[i * count : (i + 1) * count] for i in range(c, c + group)]
        out[:, c * LANES : (c + group) * LANES] = jnp.dot(
            placing, jnp.concatenate(some, axis=1), preferred_element_type=F32
        ).astype(BF16)


def staged(stages, sems, ahead=3):
    copies, used = [], 0
    for pairs in stages:
        copies.append(
            [pltpu.make_async_copy(source, target, sems.at[used + i]) for i, (source, target) in enumerate(pairs)]
        )
        used += len(pairs)
    for stage in copies[:ahead]:
        for copy in stage:
            copy.start()
    left = list(range(len(copies)))

    def arrive():
        now = left.pop(0)
        for copy in copies[now]:
            copy.wait()
        if now + ahead < len(copies):
            for copy in copies[now + ahead]:
                copy.start()

    return arrive


def hidden_kernel(order, *refs):
    peers = len(order)
    blocks, (gate, up, hidden, by_up, by_pre, near, far, cot, same) = refs[:peers], refs[peers : peers + 9]
    gate_in, up_in, wide, rows, sems = refs[peers + 9 :]
    width, inner = gate.shape
    capacity = blocks[0].shape[0]
    step = inner // TILES
    tiles = [slice(at, at + step) for at in range(0, inner, step)]
    arrive = staged(
        [((gate.at[:, t], gate_in.at[:, t]), (up.at[:, t], up_in.at[:, t])) for t in tiles], sems
    )
    for k, block in zip(order, blocks):
        wide[k * capacity : (k + 1) * capacity, :] = block[...].astype(F32)
    rows[...] = wide[:, :width].astype(BF16)
    cot[...] = wide[:, width:].astype(BF16)
    same[...] = cot[...]
    for t in tiles:
        arrive()
        pre = jnp.dot(rows[...], gate_in[:, t], preferred_element_type=F32)
        up_act = jnp.dot(rows[...], up_in[:, t], preferred_element_type=F32)
        sigma = 1.0 / (1.0 + jnp.exp(-pre))
        silu = pre * sigma
        hidden[:, t] = (silu * up_act).astype(BF16)
        by_up[:, t] = silu.astype(BF16)
        by_pre[:, t] = (up_act * sigma * (1.0 + pre * (1.0 - sigma))).astype(BF16)
    half = near.shape[1]
    on_left = lax.axis_index("ctx") < 2
    left, right = hidden[:, :half], hidden[:, half:]
    near[...] = jnp.where(on_left, left, right)
    gone = jnp.where(on_left, right, left).astype(F32)
    own = lax.axis_index("tp")
    for k in range(peers):
        start = pl.multiple_of((own ^ k) * capacity, 8)
        wide[pl.ds(start, capacity), :half] = gone[k * capacity : (k + 1) * capacity]
    far[...] = wide[:, :half].astype(BF16)


def back_kernel(
    hidden, by_up, by_pre, cot, gate, up, down, *refs,
):
    blocks, (gate_in, up_in, down_in, dpre, dup, sems) = refs[:-6], refs[-6:]
    capacity = blocks[0].shape[0]
    inner, width = down.shape
    step = inner // BACK_TILES
    inner_tiles = [slice(at, at + step) for at in range(0, inner, step)]
    tiles = [slice(at, at + WIDE) for at in range(0, width, WIDE)]
    stages = [[(down.at[t, :], down_in.at[t, :])] for t in inner_tiles]
    stages += [[(gate.at[t, :], gate_in.at[t, :]), (up.at[t, :], up_in.at[t, :])] for t in tiles]
    arrive = staged(stages, sems)
    for t in inner_tiles:
        arrive()
        dhid = lax.dot_general(cot[...], down_in[t, :], CONTRACT_LAST, preferred_element_type=F32)
        dup[:, t] = (dhid * by_up[:, t].astype(F32)).astype(BF16)
        dpre[:, t] = (dhid * by_pre[:, t].astype(F32)).astype(BF16)

    def leave(at, rows):
        for i, block in enumerate(blocks):
            block[:, at : at + WIDE] = rows[i * capacity : (i + 1) * capacity].astype(BF16)

    for t in tiles:
        leave(t.start, jnp.dot(hidden[...], down_in[:, t], preferred_element_type=F32))
        arrive()
        leave(
            width + t.start,
            lax.dot_general(dpre[...], gate_in[t, :], CONTRACT_LAST, preferred_element_type=F32)
            + lax.dot_general(dup[...], up_in[t, :], CONTRACT_LAST, preferred_element_type=F32),
        )


def quarters_kernel(after, h_own, h_remote, own, remote, mine, other, stage, sems):
    width = remote.shape[1]
    even = lax.rem(lax.axis_index("ctx"), 2) == 0
    left, right = h_own[...].astype(F32).T, h_remote[...].astype(F32).T
    size = left.shape[0] // 2

    def halves(turned):
        low, high = turned[:size].astype(BF16), turned[size:].astype(BF16)
        return jnp.where(even, low, high), jnp.where(even, high, low)

    (own_mine, own_other), (remote_mine, remote_other) = halves(left), halves(right)
    leaving = []
    for i, at in enumerate(range(0, width, WIDE)):
        cols = slice(at, at + WIDE)
        stage[:, cols] = (
            jnp.dot(own_other, own[:, cols], preferred_element_type=F32)
            + jnp.dot(remote_other, remote[:, cols], preferred_element_type=F32)
        ).astype(BF16)
        leave = pltpu.make_async_copy(stage.at[:, cols], other.at[:, cols], sems.at[i])
        leave.start()
        leaving.append(leave)
    for at in range(0, width, WIDE):
        cols = slice(at, at + WIDE)
        mine[:, cols] = (
            jnp.dot(own_mine, own[:, cols], preferred_element_type=F32)
            + jnp.dot(remote_mine, remote[:, cols], preferred_element_type=F32)
        ).astype(BF16)
    for leave in leaving:
        leave.wait()


def home_kernel(order, after, slot, gates, cot, *refs):
    peers = len(order)
    blocks, (layer_output, token_grad, gate_grad, wide) = refs[:peers], refs[peers:]
    count, width = cot.shape
    capacity = blocks[0].shape[0]
    for k, block in zip(order, blocks):
        wide[k * capacity : (k + 1) * capacity, :] = block[...].astype(F32)
    placing = (
        lax.broadcasted_iota(jnp.int32, (count, wide.shape[0]), 1) == column(slot[1:2])
    ).astype(BF16)
    gate = column(gates[...])
    total = jnp.zeros((count, 1), F32)
    step = 512
    for at in range(0, width, step):
        cols, later = slice(at, at + step), slice(width + at, width + at + step)
        out_tok = jnp.dot(placing, wide[:, cols].astype(BF16), preferred_element_type=F32)
        layer_output[:, cols] = (gate * out_tok).astype(BF16)
        total += jnp.sum(cot[:, cols].astype(F32) * out_tok, axis=1, keepdims=True)
        token_grad[:, cols] = jnp.dot(
            placing, wide[:, later].astype(BF16), preferred_element_type=F32
        ).astype(BF16)
    gate_grad[...] = jnp.sum(jnp.where(diagonal(count), total, 0.0), axis=0, keepdims=True)


def add_kernel(left, right, out):
    out[0] = (left[...].astype(F32) + right[...].astype(F32)).astype(BF16)


def along(rows, step):
    return lax.ppermute(rows, "ctx", [(i, i ^ step) for i in range(4)])


def body_line(tokens, cotangent, routes, gate_weights, w_gate, w_up, w_down):
    count, width = tokens.shape
    peers = lax.axis_size("tp")
    capacity = 3 * count * routes.shape[1] // (2 * peers)
    slots = peers * capacity
    inner = w_gate.shape[2]
    quarter = inner // 4
    gates = gate_weights.reshape(1, count)
    whole, in_place = pl.BlockSpec(), pl.BlockSpec(memory_space=pltpu.HBM)
    after = pl.BlockSpec(memory_space=pl.ANY)

    def over_tp(rows):
        wide = rows.shape[1]
        return lax.all_to_all(
            rows.reshape(peers, capacity, wide), "tp", split_axis=0, concat_axis=0, tiled=True
        ).reshape(slots, wide)

    slot, across, *blocks = call(
        functools.partial(send_kernel, peers, capacity),
        [
            shaped((2, count), jnp.int32),
            pltpu.HBM((width // LANES * count + TAIL, LANES), BF16),
        ]
        + [pltpu.HBM((capacity, 2 * width), BF16)] * peers,
        scratch_shapes=[pltpu.VMEM((count, width), BF16)],
    )(in_hbm(routes.reshape(1, count)), in_hbm(gates), in_hbm(tokens), in_hbm(cotangent))
    rows_across = along(across, 3)
    got = {0: in_hbm(blocks[0])}
    for k in range(1, peers):
        got[k] = lax.ppermute(blocks[k], "tp", [(i, i ^ k) for i in range(peers)])
    order = (6, 7, 2, 4, 3, 5, 1, 0)
    got = [got[k] for k in order]

    gate_mat, up_mat, down_mat = [in_hbm(w[0]) for w in (w_gate, w_up, w_down)]
    held = [pltpu.VMEM((width, inner), BF16)] * 2
    dma = pltpu.SemaphoreType.DMA
    hidden, by_up, by_pre, near, far, cot, same = call(
        functools.partial(hidden_kernel, order),
        [shaped((slots, inner))] * 3
        + [pltpu.HBM((slots, inner // 2), BF16)] * 2
        + [shaped((slots, width)), pltpu.HBM((slots, width), BF16)],
        in_specs=[whole] * peers + [in_place] * 2,
        scratch_shapes=held
        + [
            pltpu.VMEM((slots, 2 * width), F32),
            pltpu.VMEM((slots, width), BF16),
            dma((2 * TILES,)),
        ],
    )(*got, gate_mat, up_mat)
    near, same = in_hbm(near), in_hbm(same)
    far_across = along(far, 3)
    remote = over_tp(
        call(
            remote_kernel, shaped((slots, width)), in_specs=[whole] + [after] * (peers - 1)
        )(rows_across, *[g for k, g in zip(order, got) if k])
    )
    back = call(
        back_kernel,
        [pltpu.HBM((capacity, 2 * width), BF16)] * peers,
        in_specs=[whole] * 4 + [in_place] * 3,
        scratch_shapes=held
        + [pltpu.VMEM((inner, width), BF16)]
        + [pltpu.VMEM((slots, inner), BF16)] * 2
        + [dma((BACK_TILES + 2 * (width // WIDE),))],
    )(hidden, by_up, by_pre, cot, gate_mat, up_mat, down_mat)
    home = [
        lax.ppermute(back[k], "tp", [(i, i ^ k) for i in range(peers)]) if k else in_hbm(back[0])
        for k in order
    ]

    mine, other = call(
        quarters_kernel,
        [shaped((quarter, width)), pltpu.HBM((quarter, width), BF16)],
        in_specs=[after] + [whole] * 4,
        out_specs=[whole, in_place],
        scratch_shapes=[
            pltpu.VMEM((quarter, width), BF16),
            dma((width // WIDE,)),
        ],
    )(in_hbm(back[0]), near, far_across, same, remote)
    swapped = along(other, 1)

    down_grad = call(add_kernel, shaped((1, quarter, width)))(mine, swapped)
    layer_output, token_grad, gate_grad = call(
        functools.partial(home_kernel, order),
        [shaped((count, width)), shaped((count, width)), shaped((1, count), F32)],
        in_specs=[after] + [whole] * (3 + peers),
        scratch_shapes=[pltpu.VMEM((slots, 2 * width), F32)],
    )(in_hbm(down_grad), slot, gates, cotangent, *home)
    return layer_output, token_grad, gate_grad.reshape(count, 1), down_grad


def solution(mesh):
    rows = P(("ctx", "tp"), None)
    expert = P("tp", None, None)
    line = mesh.shape["ctx"] == 4 and mesh.shape["tp"] == 8
    return jax.shard_map(
        body_line if line else body_any,
        mesh=mesh,
        in_specs=(rows, rows, rows, rows, expert, expert, expert),
        out_specs=(rows, rows, rows, P("tp", "ctx", None)),
        check_vma=False,
    )
```

```python
import functools

import jax
import jax.numpy as jnp
from jax import lax
from jax.experimental import pallas as pl
from jax.experimental.pallas import tpu as pltpu
from jax.sharding import PartitionSpec as P

BF16 = jnp.bfloat16
F32 = jnp.float32
CONTRACT_FIRST = (((0,), (0,)), ((), ()))
CONTRACT_LAST = (((1,), (1,)), ((), ()))


def expert_block(rows_in, rows_cot, gate_mat, up_mat, down_mat):
    pre_act = jnp.dot(rows_in, gate_mat, preferred_element_type=F32)
    up_act = jnp.dot(rows_in, up_mat, preferred_element_type=F32)
    sigma = jax.nn.sigmoid(pre_act)
    hidden = (pre_act * sigma * up_act).astype(BF16)
    output = jnp.dot(hidden, down_mat, preferred_element_type=F32).astype(BF16)
    dhidden = lax.dot_general(rows_cot, down_mat, CONTRACT_LAST, preferred_element_type=F32)
    dup_act = (dhidden * pre_act * sigma).astype(BF16)
    dpre_act = (dhidden * up_act * sigma * (1.0 + pre_act * (1.0 - sigma))).astype(BF16)
    first = lax.dot_general(dpre_act, gate_mat, CONTRACT_LAST, preferred_element_type=F32)
    second = lax.dot_general(dup_act, up_mat, CONTRACT_LAST, preferred_element_type=F32)
    input_grad = (first + second).astype(BF16)
    return (output, input_grad, hidden)


def body_any(tokens, cotangent, routes, gate_weights, w_gate, w_up, w_down):
    tok_rows, width = tokens.shape
    peers = lax.axis_size("tp")
    capacity = 3 * tok_rows * routes.shape[1] // (2 * peers)
    expert_ids = routes[:, 0]
    onehot = (expert_ids[:, None] == jnp.arange(peers, dtype=jnp.int32)[None, :]).astype(jnp.int32)
    rank = jnp.sum((jnp.cumsum(onehot, axis=0) - 1) * onehot, axis=1)
    slot = expert_ids * capacity + rank
    placing = (
        slot[None, :] == jnp.arange(peers * capacity, dtype=jnp.int32)[:, None]
    ).astype(BF16)
    scaled = (gate_weights * cotangent.astype(F32)).astype(BF16)
    send = jnp.dot(
        placing, jnp.concatenate([tokens, scaled], axis=1), preferred_element_type=F32
    ).astype(BF16)
    got = lax.all_to_all(
        send.reshape(peers, capacity, 2 * width), "tp", split_axis=0, concat_axis=0, tiled=True
    ).reshape(-1, 2 * width)
    got_cot = got[:, width:]
    output, input_grad, hidden = expert_block(
        got[:, :width], got_cot, w_gate[0], w_up[0], w_down[0]
    )
    back = lax.all_to_all(
        jnp.concatenate([output, input_grad], axis=1).reshape(peers, capacity, 2 * width),
        "tp", split_axis=0, concat_axis=0, tiled=True,
    ).reshape(-1, 2 * width)
    partial = lax.dot_general(hidden, got_cot, CONTRACT_FIRST, preferred_element_type=F32)
    summed = lax.psum_scatter(partial.astype(BF16), "ctx", scatter_dimension=0, tiled=True)
    home = lax.dot_general(placing, back, CONTRACT_FIRST, preferred_element_type=F32)
    out_tok = home[:, :width]
    layer_output = (gate_weights * out_tok).astype(BF16)
    gate_grad = jnp.sum(cotangent.astype(F32) * out_tok, axis=1, keepdims=True)
    return layer_output, home[:, width:].astype(BF16), gate_grad, summed[None]


LANES = 128
TILES, BACK_TILES = 3, 2
TAIL = 16
WIDE = 1024
VMEM_LIMIT = 24 * 1024 * 1024
TINY = pl.CostEstimate(flops=1, bytes_accessed=1, transcendentals=0)


def call(kernel, outs, cost=TINY, **more):
    return pl.pallas_call(
        kernel,
        out_shape=outs,
        cost_estimate=cost,
        compiler_params=pltpu.CompilerParams(vmem_limit_bytes=VMEM_LIMIT),
        **more,
    )


def shaped(shape, dtype=BF16):
    return jax.ShapeDtypeStruct(shape, dtype)


def in_hbm(array):
    return pltpu.with_memory_space_constraint(array, pltpu.HBM)


def diagonal(size):
    return lax.broadcasted_iota(jnp.int32, (size, size), 0) == lax.broadcasted_iota(
        jnp.int32, (size, size), 1
    )


def column(row):
    return jnp.sum(jnp.where(diagonal(row.shape[1]), row, 0), axis=1, keepdims=True)


def place(placing, rows, out, at, width):
    step = 512
    for col in range(0, width, step):
        out[:, at + col : at + col + step] = jnp.dot(
            placing, rows[:, col : col + step], preferred_element_type=F32
        ).astype(BF16)


def send_kernel(peers, capacity, routes, gates, tok, cot, slot_out, across, *refs):
    blocks, scaled = refs[:-1], refs[-1]
    ids = routes[...]
    count, width = cot.shape
    onehot = lax.broadcasted_iota(jnp.int32, (peers, count), 0) == ids
    upto = lax.broadcasted_iota(jnp.int32, (count, count), 0) <= lax.broadcasted_iota(
        jnp.int32, (count, count), 1
    )
    running = jnp.dot(onehot.astype(BF16), upto.astype(BF16), preferred_element_type=F32)
    rank = jnp.sum(jnp.where(onehot, running - 1.0, 0.0), axis=0, keepdims=True).astype(jnp.int32)
    slot = ids * capacity + rank
    slot_out[0:1] = slot
    scaled[...] = (column(gates[...]) * cot[...].astype(F32)).astype(BF16)
    chunks = width // LANES
    for c in range(chunks):
        across[c * count : (c + 1) * count] = scaled[:, c * LANES : (c + 1) * LANES]
    across[chunks * count :] = jnp.broadcast_to(slot.astype(F32), (TAIL, count)).astype(BF16)
    slot = (ids ^ lax.axis_index("tp")) * capacity + rank
    slot_out[1:2] = slot
    placing = (
        lax.broadcasted_iota(jnp.int32, (peers * capacity, count), 0) == slot
    ).astype(BF16)
    step = 512
    for at, rows in ((0, tok), (width, scaled)):
        for col in range(0, width, step):
            placed = jnp.dot(placing, rows[:, col : col + step], preferred_element_type=F32)
            for k, block in enumerate(blocks):
                block[:, at + col : at + col + step] = placed[
                    k * capacity : (k + 1) * capacity
                ].astype(BF16)


def remote_kernel(rows, *refs):
    out = refs[-1]
    count, chunks = LANES, out.shape[1] // LANES
    slot = rows[chunks * count : chunks * count + 8].astype(F32)[:1].astype(jnp.int32)
    placing = (
        lax.broadcasted_iota(jnp.int32, (out.shape[0], count), 0) == slot
    ).astype(BF16)
    group = WIDE // LANES
    for c in range(0, chunks, group):
        some = [rows[i * count : (i + 1) * count] for i in range(c, c + group)]
        out[:, c * LANES : (c + group) * LANES] = jnp.dot(
            placing, jnp.concatenate(some, axis=1), preferred_element_type=F32
        ).astype(BF16)


def staged(stages, sems, ahead=3):
    copies, used = [], 0
    for pairs in stages:
        copies.append(
            [pltpu.make_async_copy(source, target, sems.at[used + i]) for i, (source, target) in enumerate(pairs)]
        )
        used += len(pairs)
    for stage in copies[:ahead]:
        for copy in stage:
            copy.start()
    left = list(range(len(copies)))

    def arrive():
        now = left.pop(0)
        for copy in copies[now]:
            copy.wait()
        if now + ahead < len(copies):
            for copy in copies[now + ahead]:
                copy.start()

    return arrive


def hidden_kernel(order, *refs):
    peers = len(order)
    blocks, (gate, up, hidden, by_up, by_pre, near, far, cot) = refs[:peers], refs[peers : peers + 8]
    gate_in, up_in, wide, rows, sems = refs[peers + 8 :]
    width, inner = gate.shape
    capacity = blocks[0].shape[0]
    step = inner // TILES
    tiles = [slice(at, at + step) for at in range(0, inner, step)]
    arrive = staged(
        [((gate.at[:, t], gate_in.at[:, t]), (up.at[:, t], up_in.at[:, t])) for t in tiles], sems
    )
    for k, block in zip(order, blocks):
        at = slice(k * capacity, (k + 1) * capacity)
        rows[at] = block[:, :width]
        cot[at] = block[:, width:]
    for t in tiles:
        arrive()
        pre = jnp.dot(rows[...], gate_in[:, t], preferred_element_type=F32)
        up_act = jnp.dot(rows[...], up_in[:, t], preferred_element_type=F32)
        sigma = 1.0 / (1.0 + jnp.exp(-pre))
        silu = pre * sigma
        hidden[:, t] = (silu * up_act).astype(BF16)
        by_up[:, t] = silu.astype(BF16)
        by_pre[:, t] = (up_act * sigma * (1.0 + pre * (1.0 - sigma))).astype(BF16)
    half = near.shape[1]
    on_left = lax.axis_index("ctx") < 2
    left, right = hidden[:, :half], hidden[:, half:]
    near[...] = jnp.where(on_left, left, right)
    gone = jnp.where(on_left, right, left).astype(F32)
    own = lax.axis_index("tp")
    for k in range(peers):
        start = pl.multiple_of((own ^ k) * capacity, 8)
        wide[pl.ds(start, capacity), :] = gone[k * capacity : (k + 1) * capacity]
    far[...] = wide[...].astype(BF16)


def back_kernel(
    hidden, by_up, by_pre, cot, gate, up, down, *refs,
):
    blocks, (gate_in, up_in, down_in, dpre, dup, sems) = refs[:-6], refs[-6:]
    capacity = blocks[0].shape[0]
    inner, width = down.shape
    step = inner // BACK_TILES
    inner_tiles = [slice(at, at + step) for at in range(0, inner, step)]
    tiles = [slice(at, at + WIDE) for at in range(0, width, WIDE)]
    stages = [[(down.at[t, :], down_in.at[t, :])] for t in inner_tiles]
    stages += [[(gate.at[t, :], gate_in.at[t, :]), (up.at[t, :], up_in.at[t, :])] for t in tiles]
    arrive = staged(stages, sems)
    for t in inner_tiles:
        arrive()
        dhid = lax.dot_general(cot[...], down_in[t, :], CONTRACT_LAST, preferred_element_type=F32)
        dup[:, t] = (dhid * by_up[:, t].astype(F32)).astype(BF16)
        dpre[:, t] = (dhid * by_pre[:, t].astype(F32)).astype(BF16)

    def leave(at, rows):
        for i, block in enumerate(blocks):
            block[:, at : at + WIDE] = rows[i * capacity : (i + 1) * capacity].astype(BF16)

    for t in tiles:
        leave(t.start, jnp.dot(hidden[...], down_in[:, t], preferred_element_type=F32))
        arrive()
        leave(
            width + t.start,
            lax.dot_general(dpre[...], gate_in[t, :], CONTRACT_LAST, preferred_element_type=F32)
            + lax.dot_general(dup[...], up_in[t, :], CONTRACT_LAST, preferred_element_type=F32),
        )


def quarters_kernel(after, h_own, h_remote, own, remote, mine, other, stage, sems):
    width = remote.shape[1]
    even = lax.rem(lax.axis_index("ctx"), 2) == 0
    left, right = h_own[...].astype(F32).T, h_remote[...].astype(F32).T
    size = left.shape[0] // 2

    def halves(turned):
        low, high = turned[:size].astype(BF16), turned[size:].astype(BF16)
        return jnp.where(even, low, high), jnp.where(even, high, low)

    (own_mine, own_other), (remote_mine, remote_other) = halves(left), halves(right)
    leaving = []
    for i, at in enumerate(range(0, width, WIDE)):
        cols = slice(at, at + WIDE)
        stage[:, cols] = (
            jnp.dot(own_other, own[:, cols], preferred_element_type=F32)
            + jnp.dot(remote_other, remote[:, cols], preferred_element_type=F32)
        ).astype(BF16)
        leave = pltpu.make_async_copy(stage.at[:, cols], other.at[:, cols], sems.at[i])
        leave.start()
        leaving.append(leave)
    for at in range(0, width, WIDE):
        cols = slice(at, at + WIDE)
        mine[:, cols] = (
            jnp.dot(own_mine, own[:, cols], preferred_element_type=F32)
            + jnp.dot(remote_mine, remote[:, cols], preferred_element_type=F32)
        ).astype(BF16)
    for leave in leaving:
        leave.wait()


def home_kernel(order, after, slot, gates, cot, *refs):
    peers = len(order)
    blocks, (layer_output, token_grad, gate_grad, wide) = refs[:peers], refs[peers:]
    count, width = cot.shape
    capacity = blocks[0].shape[0]
    for k, block in zip(order, blocks):
        wide[k * capacity : (k + 1) * capacity, :] = block[...]
    placing = (
        lax.broadcasted_iota(jnp.int32, (count, wide.shape[0]), 1) == column(slot[1:2])
    ).astype(BF16)
    gate = column(gates[...])
    total = jnp.zeros((count, 1), F32)
    step = 512
    for at in range(0, width, step):
        cols, later = slice(at, at + step), slice(width + at, width + at + step)
        out_tok = jnp.dot(placing, wide[:, cols], preferred_element_type=F32)
        layer_output[:, cols] = (gate * out_tok).astype(BF16)
        total += jnp.sum(cot[:, cols].astype(F32) * out_tok, axis=1, keepdims=True)
        token_grad[:, cols] = jnp.dot(
            placing, wide[:, later], preferred_element_type=F32
        ).astype(BF16)
    gate_grad[...] = jnp.sum(jnp.where(diagonal(count), total, 0.0), axis=0, keepdims=True)


def add_kernel(left, right, out):
    out[0] = (left[...].astype(F32) + right[...].astype(F32)).astype(BF16)


def along(rows, step):
    return lax.ppermute(rows, "ctx", [(i, i ^ step) for i in range(4)])


def body_line(tokens, cotangent, routes, gate_weights, w_gate, w_up, w_down):
    count, width = tokens.shape
    peers = lax.axis_size("tp")
    capacity = 3 * count * routes.shape[1] // (2 * peers)
    slots = peers * capacity
    inner = w_gate.shape[2]
    quarter = inner // 4
    gates = gate_weights.reshape(1, count)
    whole, in_place = pl.BlockSpec(), pl.BlockSpec(memory_space=pltpu.HBM)
    after = pl.BlockSpec(memory_space=pl.ANY)

    def over_tp(rows):
        wide = rows.shape[1]
        return lax.all_to_all(
            rows.reshape(peers, capacity, wide), "tp", split_axis=0, concat_axis=0, tiled=True
        ).reshape(slots, wide)

    slot, across, *blocks = call(
        functools.partial(send_kernel, peers, capacity),
        [
            shaped((2, count), jnp.int32),
            pltpu.HBM((width // LANES * count + TAIL, LANES), BF16),
        ]
        + [pltpu.HBM((capacity, 2 * width), BF16)] * peers,
        scratch_shapes=[pltpu.VMEM((count, width), BF16)],
    )(in_hbm(routes.reshape(1, count)), in_hbm(gates), in_hbm(tokens), in_hbm(cotangent))
    rows_across = along(across, 3)
    got = {0: in_hbm(blocks[0])}
    for k in range(1, peers):
        got[k] = lax.ppermute(blocks[k], "tp", [(i, i ^ k) for i in range(peers)])
    order = (6, 7, 2, 4, 3, 5, 1, 0)
    got = [got[k] for k in order]

    gate_mat, up_mat, down_mat = [in_hbm(w[0]) for w in (w_gate, w_up, w_down)]
    held = [pltpu.VMEM((width, inner), BF16)] * 2
    dma = pltpu.SemaphoreType.DMA
    hidden, by_up, by_pre, near, far, cot = call(
        functools.partial(hidden_kernel, order),
        [shaped((slots, inner))] * 3
        + [shaped((slots, inner // 2)), pltpu.HBM((slots, inner // 2), BF16)]
        + [shaped((slots, width))],
        in_specs=[whole] * peers + [in_place] * 2,
        scratch_shapes=held
        + [
            pltpu.VMEM((slots, inner // 2), F32),
            pltpu.VMEM((slots, width), BF16),
            dma((2 * TILES,)),
        ],
    )(*got, gate_mat, up_mat)
    far_across = along(far, 3)
    remote = over_tp(
        call(
            remote_kernel, shaped((slots, width)), in_specs=[whole] + [after] * (peers - 1)
        )(rows_across, *[g for k, g in zip(order, got) if k])
    )
    back = call(
        back_kernel,
        [pltpu.HBM((capacity, 2 * width), BF16)] * peers,
        in_specs=[whole] * 4 + [in_place] * 3,
        scratch_shapes=held
        + [pltpu.VMEM((inner, width), BF16)]
        + [pltpu.VMEM((slots, inner), BF16)] * 2
        + [dma((BACK_TILES + 2 * (width // WIDE),))],
    )(hidden, by_up, by_pre, cot, gate_mat, up_mat, down_mat)
    home = [
        lax.ppermute(back[k], "tp", [(i, i ^ k) for i in range(peers)]) if k else in_hbm(back[0])
        for k in order
    ]

    mine, other = call(
        quarters_kernel,
        [shaped((quarter, width)), pltpu.HBM((quarter, width), BF16)],
        in_specs=[after] + [whole] * 4,
        out_specs=[whole, in_place],
        scratch_shapes=[
            pltpu.VMEM((quarter, width), BF16),
            dma((width // WIDE,)),
        ],
    )(in_hbm(back[0]), near, far_across, cot, remote)
    swapped = along(other, 1)

    down_grad = call(add_kernel, shaped((1, quarter, width)))(mine, swapped)
    layer_output, token_grad, gate_grad = call(
        functools.partial(home_kernel, order),
        [shaped((count, width)), shaped((count, width)), shaped((1, count), F32)],
        in_specs=[after] + [whole] * (3 + peers),
        scratch_shapes=[pltpu.VMEM((slots, 2 * width), BF16)],
    )(in_hbm(down_grad), slot, gates, cotangent, *home)
    return layer_output, token_grad, gate_grad.reshape(count, 1), down_grad


def body(tokens, cotangent, routes, gate_weights, w_gate, w_up, w_down):
    count, width = tokens.shape
    peers, inner = lax.axis_size("tp"), w_gate.shape[2]
    capacity = 3 * count * routes.shape[1] // (2 * peers)
    on_line = lax.axis_size("ctx") == 4 and peers == 8
    even = count == LANES and capacity % 8 == 0 and peers * capacity <= 256
    tiled = width % (2 * WIDE) == 0 and inner % (2 * TILES * LANES) == 0 and w_gate.shape[0] == 1
    chosen = body_line if on_line and even and tiled else body_any
    return chosen(tokens, cotangent, routes, gate_weights, w_gate, w_up, w_down)


def solution(mesh):
    rows = P(("ctx", "tp"), None)
    expert = P("tp", None, None)
    return jax.shard_map(
        body,
        mesh=mesh,
        in_specs=(rows, rows, rows, rows, expert, expert, expert),
        out_specs=(rows, rows, rows, P("tp", "ctx", None)),
        check_vma=False,
    )
```

```python
import functools

import jax
import jax.numpy as jnp
from jax import lax
from jax.experimental import pallas as pl
from jax.experimental.pallas import tpu as pltpu
from jax.sharding import PartitionSpec as P

BF16 = jnp.bfloat16
F32 = jnp.float32
CONTRACT_FIRST = (((0,), (0,)), ((), ()))
CONTRACT_LAST = (((1,), (1,)), ((), ()))


def expert_block(rows_in, rows_cot, gate_mat, up_mat, down_mat):
    pre_act = jnp.dot(rows_in, gate_mat, preferred_element_type=F32)
    up_act = jnp.dot(rows_in, up_mat, preferred_element_type=F32)
    sigma = jax.nn.sigmoid(pre_act)
    hidden = (pre_act * sigma * up_act).astype(BF16)
    output = jnp.dot(hidden, down_mat, preferred_element_type=F32).astype(BF16)
    dhidden = lax.dot_general(rows_cot, down_mat, CONTRACT_LAST, preferred_element_type=F32)
    dup_act = (dhidden * pre_act * sigma).astype(BF16)
    dpre_act = (dhidden * up_act * sigma * (1.0 + pre_act * (1.0 - sigma))).astype(BF16)
    first = lax.dot_general(dpre_act, gate_mat, CONTRACT_LAST, preferred_element_type=F32)
    second = lax.dot_general(dup_act, up_mat, CONTRACT_LAST, preferred_element_type=F32)
    input_grad = (first + second).astype(BF16)
    return (output, input_grad, hidden)


def body_any(tokens, cotangent, routes, gate_weights, w_gate, w_up, w_down):
    tok_rows, width = tokens.shape
    peers = lax.axis_size("tp")
    capacity = 3 * tok_rows * routes.shape[1] // (2 * peers)
    expert_ids = routes[:, 0]
    onehot = (expert_ids[:, None] == jnp.arange(peers, dtype=jnp.int32)[None, :]).astype(jnp.int32)
    rank = jnp.sum((jnp.cumsum(onehot, axis=0) - 1) * onehot, axis=1)
    slot = expert_ids * capacity + rank
    placing = (
        slot[None, :] == jnp.arange(peers * capacity, dtype=jnp.int32)[:, None]
    ).astype(BF16)
    scaled = (gate_weights * cotangent.astype(F32)).astype(BF16)
    send = jnp.dot(
        placing, jnp.concatenate([tokens, scaled], axis=1), preferred_element_type=F32
    ).astype(BF16)
    got = lax.all_to_all(
        send.reshape(peers, capacity, 2 * width), "tp", split_axis=0, concat_axis=0, tiled=True
    ).reshape(-1, 2 * width)
    got_cot = got[:, width:]
    output, input_grad, hidden = expert_block(
        got[:, :width], got_cot, w_gate[0], w_up[0], w_down[0]
    )
    back = lax.all_to_all(
        jnp.concatenate([output, input_grad], axis=1).reshape(peers, capacity, 2 * width),
        "tp", split_axis=0, concat_axis=0, tiled=True,
    ).reshape(-1, 2 * width)
    partial = lax.dot_general(hidden, got_cot, CONTRACT_FIRST, preferred_element_type=F32)
    summed = lax.psum_scatter(partial.astype(BF16), "ctx", scatter_dimension=0, tiled=True)
    home = lax.dot_general(placing, back, CONTRACT_FIRST, preferred_element_type=F32)
    out_tok = home[:, :width]
    layer_output = (gate_weights * out_tok).astype(BF16)
    gate_grad = jnp.sum(cotangent.astype(F32) * out_tok, axis=1, keepdims=True)
    return layer_output, home[:, width:].astype(BF16), gate_grad, summed[None]


LANES = 128
TILES, BACK_TILES = 3, 2
TAIL = 16
WIDE = 1024
VMEM_LIMIT = 24 * 1024 * 1024
TINY = pl.CostEstimate(flops=1, bytes_accessed=1, transcendentals=0)


def call(kernel, outs, cost=TINY, **more):
    return pl.pallas_call(
        kernel,
        out_shape=outs,
        cost_estimate=cost,
        compiler_params=pltpu.CompilerParams(vmem_limit_bytes=VMEM_LIMIT),
        **more,
    )


def shaped(shape, dtype=BF16):
    return jax.ShapeDtypeStruct(shape, dtype)


def in_hbm(array):
    return pltpu.with_memory_space_constraint(array, pltpu.HBM)


def diagonal(size):
    return lax.broadcasted_iota(jnp.int32, (size, size), 0) == lax.broadcasted_iota(
        jnp.int32, (size, size), 1
    )


def column(row):
    return jnp.sum(jnp.where(diagonal(row.shape[1]), row, 0), axis=1, keepdims=True)


def place(placing, rows, out, at, width):
    step = 512
    for col in range(0, width, step):
        out[:, at + col : at + col + step] = jnp.dot(
            placing, rows[:, col : col + step], preferred_element_type=F32
        ).astype(BF16)


def send_kernel(peers, capacity, routes, gates, tok, cot, slot_out, across, *refs):
    blocks, scaled = refs[:-1], refs[-1]
    ids = routes[...]
    count, width = cot.shape
    onehot = lax.broadcasted_iota(jnp.int32, (peers, count), 0) == ids
    upto = lax.broadcasted_iota(jnp.int32, (count, count), 0) <= lax.broadcasted_iota(
        jnp.int32, (count, count), 1
    )
    running = jnp.dot(onehot.astype(BF16), upto.astype(BF16), preferred_element_type=F32)
    rank = jnp.sum(jnp.where(onehot, running - 1.0, 0.0), axis=0, keepdims=True).astype(jnp.int32)
    slot = ids * capacity + rank
    slot_out[0:1] = slot
    scaled[...] = (column(gates[...]) * cot[...].astype(F32)).astype(BF16)
    chunks = width // LANES
    for c in range(chunks):
        across[c * count : (c + 1) * count] = scaled[:, c * LANES : (c + 1) * LANES]
    across[chunks * count :] = jnp.broadcast_to(slot.astype(F32), (TAIL, count)).astype(BF16)
    slot = (ids ^ lax.axis_index("tp")) * capacity + rank
    slot_out[1:2] = slot
    placing = (
        lax.broadcasted_iota(jnp.int32, (peers * capacity, count), 0) == slot
    ).astype(BF16)
    step = 512
    for at, rows in ((0, tok), (width, scaled)):
        for col in range(0, width, step):
            placed = jnp.dot(placing, rows[:, col : col + step], preferred_element_type=F32)
            for k, block in enumerate(blocks):
                block[:, at + col : at + col + step] = placed[
                    k * capacity : (k + 1) * capacity
                ].astype(BF16)


def remote_kernel(rows, *refs):
    out = refs[-1]
    count, chunks = LANES, out.shape[1] // LANES
    slot = rows[chunks * count : chunks * count + 8].astype(F32)[:1].astype(jnp.int32)
    placing = (
        lax.broadcasted_iota(jnp.int32, (out.shape[0], count), 0) == slot
    ).astype(BF16)
    group = WIDE // LANES
    for c in range(0, chunks, group):
        some = [rows[i * count : (i + 1) * count] for i in range(c, c + group)]
        out[:, c * LANES : (c + group) * LANES] = jnp.dot(
            placing, jnp.concatenate(some, axis=1), preferred_element_type=F32
        ).astype(BF16)


def staged(stages, sems, ahead=3):
    copies, used = [], 0
    for pairs in stages:
        copies.append(
            [pltpu.make_async_copy(source, target, sems.at[used + i]) for i, (source, target) in enumerate(pairs)]
        )
        used += len(pairs)
    for stage in copies[:ahead]:
        for copy in stage:
            copy.start()
    left = list(range(len(copies)))

    def arrive():
        now = left.pop(0)
        for copy in copies[now]:
            copy.wait()
        if now + ahead < len(copies):
            for copy in copies[now + ahead]:
                copy.start()

    return arrive


def hidden_kernel(order, *refs):
    peers = len(order)
    blocks, (gate, up, hidden, by_up, by_pre, near, far, cot) = refs[:peers], refs[peers : peers + 8]
    gate_in, up_in, wide, rows, sems = refs[peers + 8 :]
    width, inner = gate.shape
    capacity = blocks[0].shape[0]
    step = inner // TILES
    tiles = [slice(at, at + step) for at in range(0, inner, step)]
    arrive = staged(
        [((gate.at[:, t], gate_in.at[:, t]), (up.at[:, t], up_in.at[:, t])) for t in tiles], sems
    )
    for k, block in zip(order, blocks):
        at = slice(k * capacity, (k + 1) * capacity)
        rows[at] = block[:, :width]
        cot[at] = block[:, width:]
    for t in tiles:
        arrive()
        pre = jnp.dot(rows[...], gate_in[:, t], preferred_element_type=F32)
        up_act = jnp.dot(rows[...], up_in[:, t], preferred_element_type=F32)
        sigma = 1.0 / (1.0 + jnp.exp(-pre))
        silu = pre * sigma
        hidden[:, t] = (silu * up_act).astype(BF16)
        by_up[:, t] = silu.astype(BF16)
        by_pre[:, t] = (up_act * sigma * (1.0 + pre * (1.0 - sigma))).astype(BF16)
    half = near.shape[1]
    on_left = lax.axis_index("ctx") < 2
    left, right = hidden[:, :half], hidden[:, half:]
    near[...] = jnp.where(on_left, left, right)
    gone = jnp.where(on_left, right, left).astype(F32)
    own = lax.axis_index("tp")
    for k in range(peers):
        start = pl.multiple_of((own ^ k) * capacity, 8)
        wide[pl.ds(start, capacity), :] = gone[k * capacity : (k + 1) * capacity]
    far[...] = wide[...].astype(BF16)


def back_kernel(
    hidden, by_up, by_pre, cot, gate, up, down, *refs,
):
    blocks, (gate_in, up_in, down_in, dpre, dup, sems) = refs[:-6], refs[-6:]
    capacity = blocks[0].shape[0]
    inner, width = down.shape
    step = inner // BACK_TILES
    inner_tiles = [slice(at, at + step) for at in range(0, inner, step)]
    tiles = [slice(at, at + WIDE) for at in range(0, width, WIDE)]
    stages = [[(down.at[t, :], down_in.at[t, :])] for t in inner_tiles]
    stages += [[(gate.at[t, :], gate_in.at[t, :]), (up.at[t, :], up_in.at[t, :])] for t in tiles]
    arrive = staged(stages, sems)
    for t in inner_tiles:
        arrive()
        dhid = lax.dot_general(cot[...], down_in[t, :], CONTRACT_LAST, preferred_element_type=F32)
        dup[:, t] = (dhid * by_up[:, t].astype(F32)).astype(BF16)
        dpre[:, t] = (dhid * by_pre[:, t].astype(F32)).astype(BF16)

    def leave(at, rows):
        for i, block in enumerate(blocks):
            block[:, at : at + WIDE] = rows[i * capacity : (i + 1) * capacity].astype(BF16)

    for t in tiles:
        leave(t.start, jnp.dot(hidden[...], down_in[:, t], preferred_element_type=F32))
        arrive()
        leave(
            width + t.start,
            lax.dot_general(dpre[...], gate_in[t, :], CONTRACT_LAST, preferred_element_type=F32)
            + lax.dot_general(dup[...], up_in[t, :], CONTRACT_LAST, preferred_element_type=F32),
        )


def quarters_kernel(after, h_own, h_remote, own, remote, mine, other, stage, sems):
    width = remote.shape[1]
    even = lax.rem(lax.axis_index("ctx"), 2) == 0
    left, right = h_own[...].astype(F32).T, h_remote[...].astype(F32).T
    size = left.shape[0] // 2

    def halves(turned):
        low, high = turned[:size].astype(BF16), turned[size:].astype(BF16)
        return jnp.where(even, low, high), jnp.where(even, high, low)

    (own_mine, own_other), (remote_mine, remote_other) = halves(left), halves(right)
    leaving = []
    for i, at in enumerate(range(0, width, WIDE)):
        cols = slice(at, at + WIDE)
        stage[:, cols] = (
            jnp.dot(own_other, own[:, cols], preferred_element_type=F32)
            + jnp.dot(remote_other, remote[:, cols], preferred_element_type=F32)
        ).astype(BF16)
        leave = pltpu.make_async_copy(stage.at[:, cols], other.at[:, cols], sems.at[i])
        leave.start()
        leaving.append(leave)
    for at in range(0, width, WIDE):
        cols = slice(at, at + WIDE)
        mine[:, cols] = (
            jnp.dot(own_mine, own[:, cols], preferred_element_type=F32)
            + jnp.dot(remote_mine, remote[:, cols], preferred_element_type=F32)
        ).astype(BF16)
    for leave in leaving:
        leave.wait()


def home_kernel(order, after, slot, gates, cot, *refs):
    peers = len(order)
    blocks, (layer_output, token_grad, gate_grad, wide) = refs[:peers], refs[peers:]
    count, width = cot.shape
    capacity = blocks[0].shape[0]
    for k, block in zip(order, blocks):
        wide[k * capacity : (k + 1) * capacity, :] = block[...]
    placing = (
        lax.broadcasted_iota(jnp.int32, (count, wide.shape[0]), 1) == column(slot[1:2])
    ).astype(BF16)
    gate = column(gates[...])
    total = jnp.zeros((count, 1), F32)
    step = 512
    for at in range(0, width, step):
        cols, later = slice(at, at + step), slice(width + at, width + at + step)
        out_tok = jnp.dot(placing, wide[:, cols], preferred_element_type=F32)
        layer_output[:, cols] = (gate * out_tok).astype(BF16)
        total += jnp.sum(cot[:, cols].astype(F32) * out_tok, axis=1, keepdims=True)
        token_grad[:, cols] = jnp.dot(
            placing, wide[:, later], preferred_element_type=F32
        ).astype(BF16)
    gate_grad[...] = jnp.sum(jnp.where(diagonal(count), total, 0.0), axis=0, keepdims=True)


def add_kernel(left, right, out):
    out[0] = (left[...].astype(F32) + right[...].astype(F32)).astype(BF16)


def along(rows, step):
    return lax.ppermute(rows, "ctx", [(i, i ^ step) for i in range(4)])


def body_line(tokens, cotangent, routes, gate_weights, w_gate, w_up, w_down):
    count, width = tokens.shape
    peers = lax.axis_size("tp")
    capacity = 3 * count * routes.shape[1] // (2 * peers)
    slots = peers * capacity
    inner = w_gate.shape[2]
    quarter = inner // 4
    gates = gate_weights.reshape(1, count)
    whole, in_place = pl.BlockSpec(), pl.BlockSpec(memory_space=pltpu.HBM)
    after = pl.BlockSpec(memory_space=pl.ANY)

    def over_tp(rows):
        wide = rows.shape[1]
        return lax.all_to_all(
            rows.reshape(peers, capacity, wide), "tp", split_axis=0, concat_axis=0, tiled=True
        ).reshape(slots, wide)

    slot, across, *blocks = call(
        functools.partial(send_kernel, peers, capacity),
        [
            shaped((2, count), jnp.int32),
            pltpu.HBM((width // LANES * count + TAIL, LANES), BF16),
        ]
        + [shaped((capacity, 2 * width))]
        + [pltpu.HBM((capacity, 2 * width), BF16)] * (peers - 1),
        scratch_shapes=[pltpu.VMEM((count, width), BF16)],
    )(in_hbm(routes.reshape(1, count)), in_hbm(gates), in_hbm(tokens), in_hbm(cotangent))
    rows_across = along(across, 3)
    got = {0: blocks[0]}
    for k in range(1, peers):
        got[k] = lax.ppermute(blocks[k], "tp", [(i, i ^ k) for i in range(peers)])
    order = (6, 7, 2, 4, 3, 5, 1, 0)
    got = [got[k] for k in order]

    gate_mat, up_mat, down_mat = [in_hbm(w[0]) for w in (w_gate, w_up, w_down)]
    held = [pltpu.VMEM((width, inner), BF16)] * 2
    dma = pltpu.SemaphoreType.DMA
    hidden, by_up, by_pre, near, far, cot = call(
        functools.partial(hidden_kernel, order),
        [shaped((slots, inner))] * 3
        + [shaped((slots, inner // 2)), pltpu.HBM((slots, inner // 2), BF16)]
        + [shaped((slots, width))],
        in_specs=[whole] * peers + [in_place] * 2,
        scratch_shapes=held
        + [
            pltpu.VMEM((slots, inner // 2), F32),
            pltpu.VMEM((slots, width), BF16),
            dma((2 * TILES,)),
        ],
    )(*got, gate_mat, up_mat)
    far_across = along(far, 3)
    remote = over_tp(
        call(
            remote_kernel, shaped((slots, width)), in_specs=[whole] + [after] * (peers - 1)
        )(rows_across, *[g for k, g in zip(order, got) if k])
    )
    back = call(
        back_kernel,
        [shaped((capacity, 2 * width))] + [pltpu.HBM((capacity, 2 * width), BF16)] * (peers - 1),
        in_specs=[whole] * 4 + [in_place] * 3,
        scratch_shapes=held
        + [pltpu.VMEM((inner, width), BF16)]
        + [pltpu.VMEM((slots, inner), BF16)] * 2
        + [dma((BACK_TILES + 2 * (width // WIDE),))],
    )(hidden, by_up, by_pre, cot, gate_mat, up_mat, down_mat)
    home = [
        lax.ppermute(back[k], "tp", [(i, i ^ k) for i in range(peers)]) if k else back[0]
        for k in order
    ]

    mine, other = call(
        quarters_kernel,
        [shaped((quarter, width)), pltpu.HBM((quarter, width), BF16)],
        in_specs=[after] + [whole] * 4,
        out_specs=[whole, in_place],
        scratch_shapes=[
            pltpu.VMEM((quarter, width), BF16),
            dma((width // WIDE,)),
        ],
    )(in_hbm(back[1]), near, far_across, cot, remote)
    swapped = along(other, 1)

    down_grad = call(add_kernel, shaped((1, quarter, width)))(mine, swapped)
    layer_output, token_grad, gate_grad = call(
        functools.partial(home_kernel, order),
        [shaped((count, width)), shaped((count, width)), shaped((1, count), F32)],
        in_specs=[after] + [whole] * (3 + peers),
        scratch_shapes=[pltpu.VMEM((slots, 2 * width), BF16)],
    )(in_hbm(down_grad), slot, gates, cotangent, *home)
    return layer_output, token_grad, gate_grad.reshape(count, 1), down_grad


def body(tokens, cotangent, routes, gate_weights, w_gate, w_up, w_down):
    count, width = tokens.shape
    peers, inner = lax.axis_size("tp"), w_gate.shape[2]
    capacity = 3 * count * routes.shape[1] // (2 * peers)
    on_line = lax.axis_size("ctx") == 4 and peers == 8
    even = count == LANES and capacity % 8 == 0 and peers * capacity <= 256
    tiled = width % (2 * WIDE) == 0 and inner % (2 * TILES * LANES) == 0 and w_gate.shape[0] == 1
    chosen = body_line if on_line and even and tiled else body_any
    return chosen(tokens, cotangent, routes, gate_weights, w_gate, w_up, w_down)


def solution(mesh):
    rows = P(("ctx", "tp"), None)
    expert = P("tp", None, None)
    return jax.shard_map(
        body,
        mesh=mesh,
        in_specs=(rows, rows, rows, rows, expert, expert, expert),
        out_specs=(rows, rows, rows, P("tp", "ctx", None)),
        check_vma=False,
    )
```

```python
import functools

import jax
import jax.numpy as jnp
from jax import lax
from jax.experimental import pallas as pl
from jax.experimental.pallas import tpu as pltpu
from jax.sharding import PartitionSpec as P

BF16 = jnp.bfloat16
F32 = jnp.float32
CONTRACT_FIRST = (((0,), (0,)), ((), ()))
CONTRACT_LAST = (((1,), (1,)), ((), ()))


def expert_block(rows_in, rows_cot, gate_mat, up_mat, down_mat):
    pre_act = jnp.dot(rows_in, gate_mat, preferred_element_type=F32)
    up_act = jnp.dot(rows_in, up_mat, preferred_element_type=F32)
    sigma = jax.nn.sigmoid(pre_act)
    hidden = (pre_act * sigma * up_act).astype(BF16)
    output = jnp.dot(hidden, down_mat, preferred_element_type=F32).astype(BF16)
    dhidden = lax.dot_general(rows_cot, down_mat, CONTRACT_LAST, preferred_element_type=F32)
    dup_act = (dhidden * pre_act * sigma).astype(BF16)
    dpre_act = (dhidden * up_act * sigma * (1.0 + pre_act * (1.0 - sigma))).astype(BF16)
    first = lax.dot_general(dpre_act, gate_mat, CONTRACT_LAST, preferred_element_type=F32)
    second = lax.dot_general(dup_act, up_mat, CONTRACT_LAST, preferred_element_type=F32)
    input_grad = (first + second).astype(BF16)
    return (output, input_grad, hidden)


def body_any(tokens, cotangent, routes, gate_weights, w_gate, w_up, w_down):
    tok_rows, width = tokens.shape
    peers = lax.axis_size("tp")
    capacity = 3 * tok_rows * routes.shape[1] // (2 * peers)
    expert_ids = routes[:, 0]
    onehot = (expert_ids[:, None] == jnp.arange(peers, dtype=jnp.int32)[None, :]).astype(jnp.int32)
    rank = jnp.sum((jnp.cumsum(onehot, axis=0) - 1) * onehot, axis=1)
    slot = expert_ids * capacity + rank
    placing = (
        slot[None, :] == jnp.arange(peers * capacity, dtype=jnp.int32)[:, None]
    ).astype(BF16)
    scaled = (gate_weights * cotangent.astype(F32)).astype(BF16)
    send = jnp.dot(
        placing, jnp.concatenate([tokens, scaled], axis=1), preferred_element_type=F32
    ).astype(BF16)
    got = lax.all_to_all(
        send.reshape(peers, capacity, 2 * width), "tp", split_axis=0, concat_axis=0, tiled=True
    ).reshape(-1, 2 * width)
    got_cot = got[:, width:]
    output, input_grad, hidden = expert_block(
        got[:, :width], got_cot, w_gate[0], w_up[0], w_down[0]
    )
    back = lax.all_to_all(
        jnp.concatenate([output, input_grad], axis=1).reshape(peers, capacity, 2 * width),
        "tp", split_axis=0, concat_axis=0, tiled=True,
    ).reshape(-1, 2 * width)
    partial = lax.dot_general(hidden, got_cot, CONTRACT_FIRST, preferred_element_type=F32)
    summed = lax.psum_scatter(partial.astype(BF16), "ctx", scatter_dimension=0, tiled=True)
    home = lax.dot_general(placing, back, CONTRACT_FIRST, preferred_element_type=F32)
    out_tok = home[:, :width]
    layer_output = (gate_weights * out_tok).astype(BF16)
    gate_grad = jnp.sum(cotangent.astype(F32) * out_tok, axis=1, keepdims=True)
    return layer_output, home[:, width:].astype(BF16), gate_grad, summed[None]


LANES = 128
TILES, BACK_TILES = 3, 2
TAIL = 16
WIDE = 1024
VMEM_LIMIT = 24 * 1024 * 1024
TINY = pl.CostEstimate(flops=1, bytes_accessed=1, transcendentals=0)


def call(kernel, outs, cost=TINY, **more):
    return pl.pallas_call(
        kernel,
        out_shape=outs,
        cost_estimate=cost,
        compiler_params=pltpu.CompilerParams(vmem_limit_bytes=VMEM_LIMIT),
        **more,
    )


def shaped(shape, dtype=BF16):
    return jax.ShapeDtypeStruct(shape, dtype)


def in_hbm(array):
    return pltpu.with_memory_space_constraint(array, pltpu.HBM)


def diagonal(size):
    return lax.broadcasted_iota(jnp.int32, (size, size), 0) == lax.broadcasted_iota(
        jnp.int32, (size, size), 1
    )


def column(row):
    return jnp.sum(jnp.where(diagonal(row.shape[1]), row, 0), axis=1, keepdims=True)


def place(placing, rows, out, at, width):
    step = 512
    for col in range(0, width, step):
        out[:, at + col : at + col + step] = jnp.dot(
            placing, rows[:, col : col + step], preferred_element_type=F32
        ).astype(BF16)


def send_kernel(peers, capacity, routes, gates, tok, cot, slot_out, across, *refs):
    blocks, scaled = refs[:-1], refs[-1]
    ids = routes[...]
    count, width = cot.shape
    onehot = lax.broadcasted_iota(jnp.int32, (peers, count), 0) == ids
    upto = lax.broadcasted_iota(jnp.int32, (count, count), 0) <= lax.broadcasted_iota(
        jnp.int32, (count, count), 1
    )
    running = jnp.dot(onehot.astype(BF16), upto.astype(BF16), preferred_element_type=F32)
    rank = jnp.sum(jnp.where(onehot, running - 1.0, 0.0), axis=0, keepdims=True).astype(jnp.int32)
    slot = ids * capacity + rank
    slot_out[0:1] = slot
    scaled[...] = (column(gates[...]) * cot[...].astype(F32)).astype(BF16)
    chunks = width // LANES
    for c in range(chunks):
        across[c * count : (c + 1) * count] = scaled[:, c * LANES : (c + 1) * LANES]
    across[chunks * count :] = jnp.broadcast_to(slot.astype(F32), (TAIL, count)).astype(BF16)
    slot = (ids ^ lax.axis_index("tp")) * capacity + rank
    slot_out[1:2] = slot
    placing = (
        lax.broadcasted_iota(jnp.int32, (peers * capacity, count), 0) == slot
    ).astype(BF16)
    step = 512
    for at, rows in ((0, tok), (width, scaled)):
        for col in range(0, width, step):
            placed = jnp.dot(placing, rows[:, col : col + step], preferred_element_type=F32)
            for k, block in enumerate(blocks):
                block[:, at + col : at + col + step] = placed[
                    k * capacity : (k + 1) * capacity
                ].astype(BF16)


def remote_kernel(rows, *refs):
    out = refs[-1]
    count, chunks = LANES, out.shape[1] // LANES
    slot = rows[chunks * count : chunks * count + 8].astype(F32)[:1].astype(jnp.int32)
    placing = (
        lax.broadcasted_iota(jnp.int32, (out.shape[0], count), 0) == slot
    ).astype(BF16)
    group = WIDE // LANES
    for c in range(0, chunks, group):
        some = [rows[i * count : (i + 1) * count] for i in range(c, c + group)]
        out[:, c * LANES : (c + group) * LANES] = jnp.dot(
            placing, jnp.concatenate(some, axis=1), preferred_element_type=F32
        ).astype(BF16)


def staged(stages, sems, ahead=3):
    copies, used = [], 0
    for pairs in stages:
        copies.append(
            [pltpu.make_async_copy(source, target, sems.at[used + i]) for i, (source, target) in enumerate(pairs)]
        )
        used += len(pairs)
    for stage in copies[:ahead]:
        for copy in stage:
            copy.start()
    left = list(range(len(copies)))

    def arrive():
        now = left.pop(0)
        for copy in copies[now]:
            copy.wait()
        if now + ahead < len(copies):
            for copy in copies[now + ahead]:
                copy.start()

    return arrive


def hidden_kernel(order, *refs):
    peers = len(order)
    blocks, (gate, up, hidden, by_up, by_pre, near, far, cot) = refs[:peers], refs[peers : peers + 8]
    gate_in, up_in, wide, rows, sems = refs[peers + 8 :]
    width, inner = gate.shape
    capacity = blocks[0].shape[0]
    step = inner // TILES
    tiles = [slice(at, at + step) for at in range(0, inner, step)]
    arrive = staged(
        [((gate.at[:, t], gate_in.at[:, t]), (up.at[:, t], up_in.at[:, t])) for t in tiles], sems
    )
    for k, block in zip(order, blocks):
        at = slice(k * capacity, (k + 1) * capacity)
        rows[at] = block[:, :width]
        cot[at] = block[:, width:]
    for t in tiles:
        arrive()
        pre = jnp.dot(rows[...], gate_in[:, t], preferred_element_type=F32)
        up_act = jnp.dot(rows[...], up_in[:, t], preferred_element_type=F32)
        sigma = 1.0 / (1.0 + jnp.exp(-pre))
        silu = pre * sigma
        hidden[:, t] = (silu * up_act).astype(BF16)
        by_up[:, t] = silu.astype(BF16)
        by_pre[:, t] = (up_act * sigma * (1.0 + pre * (1.0 - sigma))).astype(BF16)
    half = near.shape[1]
    on_left = lax.axis_index("ctx") < 2
    left, right = hidden[:, :half], hidden[:, half:]
    near[...] = jnp.where(on_left, left, right)
    gone = jnp.where(on_left, right, left).astype(F32)
    own = lax.axis_index("tp")
    for k in range(peers):
        start = pl.multiple_of((own ^ k) * capacity, 8)
        wide[pl.ds(start, capacity), :] = gone[k * capacity : (k + 1) * capacity]
    far[...] = wide[...].astype(BF16)


def back_kernel(
    hidden, by_up, by_pre, cot, gate, up, down, *refs,
):
    blocks, (gate_in, up_in, down_in, dpre, dup, sems) = refs[:-6], refs[-6:]
    capacity = blocks[0].shape[0]
    inner, width = down.shape
    step = inner // BACK_TILES
    inner_tiles = [slice(at, at + step) for at in range(0, inner, step)]
    tiles = [slice(at, at + WIDE) for at in range(0, width, WIDE)]
    stages = [[(down.at[t, :], down_in.at[t, :])] for t in inner_tiles]
    stages += [[(gate.at[t, :], gate_in.at[t, :]), (up.at[t, :], up_in.at[t, :])] for t in tiles]
    arrive = staged(stages, sems)
    for t in inner_tiles:
        arrive()
        dhid = lax.dot_general(cot[...], down_in[t, :], CONTRACT_LAST, preferred_element_type=F32)
        dup[:, t] = (dhid * by_up[:, t].astype(F32)).astype(BF16)
        dpre[:, t] = (dhid * by_pre[:, t].astype(F32)).astype(BF16)

    def leave(at, rows):
        for i, block in enumerate(blocks):
            block[:, at : at + WIDE] = rows[i * capacity : (i + 1) * capacity].astype(BF16)

    for t in tiles:
        leave(t.start, jnp.dot(hidden[...], down_in[:, t], preferred_element_type=F32))
        arrive()
        leave(
            width + t.start,
            lax.dot_general(dpre[...], gate_in[t, :], CONTRACT_LAST, preferred_element_type=F32)
            + lax.dot_general(dup[...], up_in[t, :], CONTRACT_LAST, preferred_element_type=F32),
        )


def quarters_kernel(after, h_own, h_remote, own, remote, mine, other):
    width = remote.shape[1]
    even = lax.rem(lax.axis_index("ctx"), 2) == 0
    left, right = h_own[...].astype(F32).T, h_remote[...].astype(F32).T
    size = left.shape[0] // 2

    def halves(turned):
        low, high = turned[:size].astype(BF16), turned[size:].astype(BF16)
        return jnp.where(even, low, high), jnp.where(even, high, low)

    (own_mine, own_other), (remote_mine, remote_other) = halves(left), halves(right)
    for at in range(0, width, WIDE):
        cols = slice(at, at + WIDE)
        for out, left, right in ((other, own_other, remote_other), (mine, own_mine, remote_mine)):
            out[:, cols] = (
                jnp.dot(left, own[:, cols], preferred_element_type=F32)
                + jnp.dot(right, remote[:, cols], preferred_element_type=F32)
            ).astype(BF16)


def home_kernel(order, after, slot, gates, cot, *refs):
    peers = len(order)
    blocks, (layer_output, token_grad, gate_grad, wide) = refs[:peers], refs[peers:]
    count, width = cot.shape
    capacity = blocks[0].shape[0]
    for k, block in zip(order, blocks):
        wide[k * capacity : (k + 1) * capacity, :] = block[...]
    placing = (
        lax.broadcasted_iota(jnp.int32, (count, wide.shape[0]), 1) == column(slot[1:2])
    ).astype(BF16)
    gate = column(gates[...])
    total = jnp.zeros((count, 1), F32)
    step = 512
    for at in range(0, width, step):
        cols, later = slice(at, at + step), slice(width + at, width + at + step)
        out_tok = jnp.dot(placing, wide[:, cols], preferred_element_type=F32)
        layer_output[:, cols] = (gate * out_tok).astype(BF16)
        total += jnp.sum(cot[:, cols].astype(F32) * out_tok, axis=1, keepdims=True)
        token_grad[:, cols] = jnp.dot(
            placing, wide[:, later], preferred_element_type=F32
        ).astype(BF16)
    gate_grad[...] = jnp.sum(jnp.where(diagonal(count), total, 0.0), axis=0, keepdims=True)


def add_kernel(left, right, out):
    out[0] = (left[...].astype(F32) + right[...].astype(F32)).astype(BF16)


def along(rows, step):
    return lax.ppermute(rows, "ctx", [(i, i ^ step) for i in range(4)])


def body_line(tokens, cotangent, routes, gate_weights, w_gate, w_up, w_down):
    count, width = tokens.shape
    peers = lax.axis_size("tp")
    capacity = 3 * count * routes.shape[1] // (2 * peers)
    slots = peers * capacity
    inner = w_gate.shape[2]
    quarter = inner // 4
    gates = gate_weights.reshape(1, count)
    whole, in_place = pl.BlockSpec(), pl.BlockSpec(memory_space=pltpu.HBM)
    after = pl.BlockSpec(memory_space=pl.ANY)

    def over_tp(rows):
        wide = rows.shape[1]
        return lax.all_to_all(
            rows.reshape(peers, capacity, wide), "tp", split_axis=0, concat_axis=0, tiled=True
        ).reshape(slots, wide)

    slot, across, *blocks = call(
        functools.partial(send_kernel, peers, capacity),
        [
            shaped((2, count), jnp.int32),
            shaped((width // LANES * count + TAIL, LANES)),
        ]
        + [shaped((capacity, 2 * width))]
        + [pltpu.HBM((capacity, 2 * width), BF16)] * (peers - 1),
        scratch_shapes=[pltpu.VMEM((count, width), BF16)],
    )(in_hbm(routes.reshape(1, count)), in_hbm(gates), in_hbm(tokens), in_hbm(cotangent))
    rows_across = along(across, 3)
    got = {0: blocks[0]}
    for k in range(1, peers):
        got[k] = lax.ppermute(blocks[k], "tp", [(i, i ^ k) for i in range(peers)])
    order = (6, 7, 2, 4, 3, 5, 1, 0)
    got = [got[k] for k in order]

    gate_mat, up_mat, down_mat = [in_hbm(w[0]) for w in (w_gate, w_up, w_down)]
    held = [pltpu.VMEM((width, inner), BF16)] * 2
    dma = pltpu.SemaphoreType.DMA
    hidden, by_up, by_pre, near, far, cot = call(
        functools.partial(hidden_kernel, order),
        [shaped((slots, inner))] * 3
        + [shaped((slots, inner // 2))] * 2
        + [shaped((slots, width))],
        in_specs=[whole] * peers + [in_place] * 2,
        scratch_shapes=held
        + [
            pltpu.VMEM((slots, inner // 2), F32),
            pltpu.VMEM((slots, width), BF16),
            dma((2 * TILES,)),
        ],
    )(*got, gate_mat, up_mat)
    far_across = along(far, 3)
    remote = over_tp(
        call(
            remote_kernel, shaped((slots, width)), in_specs=[whole] + [after] * (peers - 1)
        )(rows_across, *[g for k, g in zip(order, got) if k])
    )
    back = call(
        back_kernel,
        [shaped((capacity, 2 * width))] + [pltpu.HBM((capacity, 2 * width), BF16)] * (peers - 1),
        in_specs=[whole] * 4 + [in_place] * 3,
        scratch_shapes=held
        + [pltpu.VMEM((inner, width), BF16)]
        + [pltpu.VMEM((slots, inner), BF16)] * 2
        + [dma((BACK_TILES + 2 * (width // WIDE),))],
    )(hidden, by_up, by_pre, cot, gate_mat, up_mat, down_mat)
    home = [
        lax.ppermute(back[k], "tp", [(i, i ^ k) for i in range(peers)]) if k else back[0]
        for k in order
    ]

    mine, other = call(
        quarters_kernel,
        [shaped((quarter, width))] * 2,
        in_specs=[after] + [whole] * 4,
    )(in_hbm(back[1]), near, far_across, cot, remote)
    swapped = along(other, 1)

    down_grad = call(add_kernel, shaped((1, quarter, width)))(mine, swapped)
    layer_output, token_grad, gate_grad = call(
        functools.partial(home_kernel, order),
        [shaped((count, width)), shaped((count, width)), shaped((1, count), F32)],
        in_specs=[after] + [whole] * (3 + peers),
        scratch_shapes=[pltpu.VMEM((slots, 2 * width), BF16)],
    )(in_hbm(down_grad), slot, gates, cotangent, *home)
    return layer_output, token_grad, gate_grad.reshape(count, 1), down_grad


def body(tokens, cotangent, routes, gate_weights, w_gate, w_up, w_down):
    count, width = tokens.shape
    peers, inner = lax.axis_size("tp"), w_gate.shape[2]
    capacity = 3 * count * routes.shape[1] // (2 * peers)
    on_line = lax.axis_size("ctx") == 4 and peers == 8
    even = count == LANES and capacity % 8 == 0 and peers * capacity <= 256
    tiled = width % (2 * WIDE) == 0 and inner % (2 * TILES * LANES) == 0 and w_gate.shape[0] == 1
    chosen = body_line if on_line and even and tiled else body_any
    return chosen(tokens, cotangent, routes, gate_weights, w_gate, w_up, w_down)


def solution(mesh):
    rows = P(("ctx", "tp"), None)
    expert = P("tp", None, None)
    return jax.shard_map(
        body,
        mesh=mesh,
        in_specs=(rows, rows, rows, rows, expert, expert, expert),
        out_specs=(rows, rows, rows, P("tp", "ctx", None)),
        check_vma=False,
    )
```

```python
import functools

import jax
import jax.numpy as jnp
from jax import lax
from jax.experimental import pallas as pl
from jax.experimental.pallas import tpu as pltpu
from jax.sharding import PartitionSpec as P

BF16 = jnp.bfloat16
F32 = jnp.float32
CONTRACT_FIRST = (((0,), (0,)), ((), ()))
CONTRACT_LAST = (((1,), (1,)), ((), ()))


def expert_block(rows_in, rows_cot, gate_mat, up_mat, down_mat):
    pre_act = jnp.dot(rows_in, gate_mat, preferred_element_type=F32)
    up_act = jnp.dot(rows_in, up_mat, preferred_element_type=F32)
    sigma = jax.nn.sigmoid(pre_act)
    hidden = (pre_act * sigma * up_act).astype(BF16)
    output = jnp.dot(hidden, down_mat, preferred_element_type=F32).astype(BF16)
    dhidden = lax.dot_general(rows_cot, down_mat, CONTRACT_LAST, preferred_element_type=F32)
    dup_act = (dhidden * pre_act * sigma).astype(BF16)
    dpre_act = (dhidden * up_act * sigma * (1.0 + pre_act * (1.0 - sigma))).astype(BF16)
    first = lax.dot_general(dpre_act, gate_mat, CONTRACT_LAST, preferred_element_type=F32)
    second = lax.dot_general(dup_act, up_mat, CONTRACT_LAST, preferred_element_type=F32)
    input_grad = (first + second).astype(BF16)
    return (output, input_grad, hidden)


def body_any(tokens, cotangent, routes, gate_weights, w_gate, w_up, w_down):
    tok_rows, width = tokens.shape
    peers = lax.axis_size("tp")
    capacity = 3 * tok_rows * routes.shape[1] // (2 * peers)
    expert_ids = routes[:, 0]
    onehot = (expert_ids[:, None] == jnp.arange(peers, dtype=jnp.int32)[None, :]).astype(jnp.int32)
    rank = jnp.sum((jnp.cumsum(onehot, axis=0) - 1) * onehot, axis=1)
    slot = expert_ids * capacity + rank
    placing = (
        slot[None, :] == jnp.arange(peers * capacity, dtype=jnp.int32)[:, None]
    ).astype(BF16)
    scaled = (gate_weights * cotangent.astype(F32)).astype(BF16)
    send = jnp.dot(
        placing, jnp.concatenate([tokens, scaled], axis=1), preferred_element_type=F32
    ).astype(BF16)
    got = lax.all_to_all(
        send.reshape(peers, capacity, 2 * width), "tp", split_axis=0, concat_axis=0, tiled=True
    ).reshape(-1, 2 * width)
    got_cot = got[:, width:]
    output, input_grad, hidden = expert_block(
        got[:, :width], got_cot, w_gate[0], w_up[0], w_down[0]
    )
    back = lax.all_to_all(
        jnp.concatenate([output, input_grad], axis=1).reshape(peers, capacity, 2 * width),
        "tp", split_axis=0, concat_axis=0, tiled=True,
    ).reshape(-1, 2 * width)
    partial = lax.dot_general(hidden, got_cot, CONTRACT_FIRST, preferred_element_type=F32)
    summed = lax.psum_scatter(partial.astype(BF16), "ctx", scatter_dimension=0, tiled=True)
    home = lax.dot_general(placing, back, CONTRACT_FIRST, preferred_element_type=F32)
    out_tok = home[:, :width]
    layer_output = (gate_weights * out_tok).astype(BF16)
    gate_grad = jnp.sum(cotangent.astype(F32) * out_tok, axis=1, keepdims=True)
    return layer_output, home[:, width:].astype(BF16), gate_grad, summed[None]


LANES = 128
TILES, BACK_TILES = 3, 2
TAIL = 16
WIDE = 1024
VMEM_LIMIT = 24 * 1024 * 1024
TINY = pl.CostEstimate(flops=1, bytes_accessed=1, transcendentals=0)


def call(kernel, outs, cost=TINY, **more):
    return pl.pallas_call(
        kernel,
        out_shape=outs,
        cost_estimate=cost,
        compiler_params=pltpu.CompilerParams(vmem_limit_bytes=VMEM_LIMIT),
        **more,
    )


def shaped(shape, dtype=BF16):
    return jax.ShapeDtypeStruct(shape, dtype)


def in_hbm(array):
    return pltpu.with_memory_space_constraint(array, pltpu.HBM)


def diagonal(size):
    return lax.broadcasted_iota(jnp.int32, (size, size), 0) == lax.broadcasted_iota(
        jnp.int32, (size, size), 1
    )


def column(row):
    return jnp.sum(jnp.where(diagonal(row.shape[1]), row, 0), axis=1, keepdims=True)


def place(placing, rows, out, at, width):
    step = 512
    for col in range(0, width, step):
        out[:, at + col : at + col + step] = jnp.dot(
            placing, rows[:, col : col + step], preferred_element_type=F32
        ).astype(BF16)


def send_kernel(peers, capacity, routes, gates, tok, cot, slot_out, across, *refs):
    blocks, scaled = refs[:-1], refs[-1]
    ids = routes[...]
    count, width = cot.shape
    onehot = lax.broadcasted_iota(jnp.int32, (peers, count), 0) == ids
    upto = lax.broadcasted_iota(jnp.int32, (count, count), 0) <= lax.broadcasted_iota(
        jnp.int32, (count, count), 1
    )
    running = jnp.dot(onehot.astype(BF16), upto.astype(BF16), preferred_element_type=F32)
    rank = jnp.sum(jnp.where(onehot, running - 1.0, 0.0), axis=0, keepdims=True).astype(jnp.int32)
    slot = ids * capacity + rank
    slot_out[0:1] = slot
    scaled[...] = (column(gates[...]) * cot[...].astype(F32)).astype(BF16)
    chunks = width // LANES
    for c in range(chunks):
        across[c * count : (c + 1) * count] = scaled[:, c * LANES : (c + 1) * LANES]
    across[chunks * count :] = jnp.broadcast_to(slot.astype(F32), (TAIL, count)).astype(BF16)
    slot = (ids ^ lax.axis_index("tp")) * capacity + rank
    slot_out[1:2] = slot
    placing = (
        lax.broadcasted_iota(jnp.int32, (peers * capacity, count), 0) == slot
    ).astype(BF16)
    step = 512
    for at, rows in ((0, tok), (width, scaled)):
        for col in range(0, width, step):
            placed = jnp.dot(placing, rows[:, col : col + step], preferred_element_type=F32)
            for k, block in enumerate(blocks):
                block[:, at + col : at + col + step] = placed[
                    k * capacity : (k + 1) * capacity
                ].astype(BF16)


def remote_kernel(rows, *refs):
    out = refs[-1]
    count, chunks = LANES, out.shape[1] // LANES
    slot = rows[chunks * count : chunks * count + 8].astype(F32)[:1].astype(jnp.int32)
    placing = (
        lax.broadcasted_iota(jnp.int32, (out.shape[0], count), 0) == slot
    ).astype(BF16)
    group = WIDE // LANES
    for c in range(0, chunks, group):
        some = [rows[i * count : (i + 1) * count] for i in range(c, c + group)]
        out[:, c * LANES : (c + group) * LANES] = jnp.dot(
            placing, jnp.concatenate(some, axis=1), preferred_element_type=F32
        ).astype(BF16)


def staged(stages, sems, ahead=3):
    copies, used = [], 0
    for pairs in stages:
        copies.append(
            [pltpu.make_async_copy(source, target, sems.at[used + i]) for i, (source, target) in enumerate(pairs)]
        )
        used += len(pairs)
    for stage in copies[:ahead]:
        for copy in stage:
            copy.start()
    left = list(range(len(copies)))

    def arrive():
        now = left.pop(0)
        for copy in copies[now]:
            copy.wait()
        if now + ahead < len(copies):
            for copy in copies[now + ahead]:
                copy.start()

    return arrive


def hidden_kernel(order, *refs):
    peers = len(order)
    blocks, (gate, up, hidden, by_up, by_pre, near, far, cot) = refs[:peers], refs[peers : peers + 8]
    gate_in, up_in, wide, rows, sems = refs[peers + 8 :]
    width, inner = gate.shape
    capacity = blocks[0].shape[0]
    step = inner // TILES
    tiles = [slice(at, at + step) for at in range(0, inner, step)]
    arrive = staged(
        [((gate.at[:, t], gate_in.at[:, t]), (up.at[:, t], up_in.at[:, t])) for t in tiles], sems
    )
    for k, block in zip(order, blocks):
        at = slice(k * capacity, (k + 1) * capacity)
        rows[at] = block[:, :width]
        cot[at] = block[:, width:]
    for t in tiles:
        arrive()
        pre = jnp.dot(rows[...], gate_in[:, t], preferred_element_type=F32)
        up_act = jnp.dot(rows[...], up_in[:, t], preferred_element_type=F32)
        sigma = 1.0 / (1.0 + jnp.exp(-pre))
        silu = pre * sigma
        hidden[:, t] = (silu * up_act).astype(BF16)
        by_up[:, t] = silu.astype(BF16)
        by_pre[:, t] = (up_act * sigma * (1.0 + pre * (1.0 - sigma))).astype(BF16)
    half = near.shape[1]
    on_left = lax.axis_index("ctx") < 2
    left, right = hidden[:, :half], hidden[:, half:]
    near[...] = jnp.where(on_left, left, right)
    gone = jnp.where(on_left, right, left).astype(F32)
    own = lax.axis_index("tp")
    for k in range(peers):
        start = pl.multiple_of((own ^ k) * capacity, 8)
        wide[pl.ds(start, capacity), :] = gone[k * capacity : (k + 1) * capacity]
    far[...] = wide[...].astype(BF16)


def back_kernel(
    hidden, by_up, by_pre, cot, gate, up, down, *refs,
):
    blocks, (gate_in, up_in, down_in, dpre, dup, sems) = refs[:-6], refs[-6:]
    capacity = blocks[0].shape[0]
    inner, width = down.shape
    step = inner // BACK_TILES
    inner_tiles = [slice(at, at + step) for at in range(0, inner, step)]
    tiles = [slice(at, at + WIDE) for at in range(0, width, WIDE)]
    stages = [[(down.at[t, :], down_in.at[t, :])] for t in inner_tiles]
    stages += [[(gate.at[t, :], gate_in.at[t, :]), (up.at[t, :], up_in.at[t, :])] for t in tiles]
    arrive = staged(stages, sems)
    for t in inner_tiles:
        arrive()
        dhid = lax.dot_general(cot[...], down_in[t, :], CONTRACT_LAST, preferred_element_type=F32)
        dup[:, t] = (dhid * by_up[:, t].astype(F32)).astype(BF16)
        dpre[:, t] = (dhid * by_pre[:, t].astype(F32)).astype(BF16)

    def leave(at, rows):
        for i, block in enumerate(blocks):
            block[:, at : at + WIDE] = rows[i * capacity : (i + 1) * capacity].astype(BF16)

    for t in tiles:
        leave(t.start, jnp.dot(hidden[...], down_in[:, t], preferred_element_type=F32))
        arrive()
        leave(
            width + t.start,
            lax.dot_general(dpre[...], gate_in[t, :], CONTRACT_LAST, preferred_element_type=F32)
            + lax.dot_general(dup[...], up_in[t, :], CONTRACT_LAST, preferred_element_type=F32),
        )


def turned(hid, away):
    low = (lax.rem(lax.axis_index("ctx"), 2) == 0) != away
    size = hid.shape[1] // 2
    return jnp.where(low, hid[:, :size], hid[:, size:]).astype(F32).T.astype(BF16)


def quarters_kernel(after, h_own, h_remote, own, remote, other):
    left, right = turned(h_own, True), turned(h_remote, True)
    for at in range(0, remote.shape[1], WIDE):
        cols = slice(at, at + WIDE)
        other[:, cols] = (
            jnp.dot(left, own[:, cols], preferred_element_type=F32)
            + jnp.dot(right, remote[:, cols], preferred_element_type=F32)
        ).astype(BF16)


def home_kernel(order, after, slot, gates, cot, *refs):
    peers = len(order)
    blocks, (layer_output, token_grad, gate_grad, wide) = refs[:peers], refs[peers:]
    count, width = cot.shape
    capacity = blocks[0].shape[0]
    for k, block in zip(order, blocks):
        wide[k * capacity : (k + 1) * capacity, :] = block[...]
    placing = (
        lax.broadcasted_iota(jnp.int32, (count, wide.shape[0]), 1) == column(slot[1:2])
    ).astype(BF16)
    gate = column(gates[...])
    total = jnp.zeros((count, 1), F32)
    step = 512
    for at in range(0, width, step):
        cols, later = slice(at, at + step), slice(width + at, width + at + step)
        out_tok = jnp.dot(placing, wide[:, cols], preferred_element_type=F32)
        layer_output[:, cols] = (gate * out_tok).astype(BF16)
        total += jnp.sum(cot[:, cols].astype(F32) * out_tok, axis=1, keepdims=True)
        token_grad[:, cols] = jnp.dot(
            placing, wide[:, later], preferred_element_type=F32
        ).astype(BF16)
    gate_grad[...] = jnp.sum(jnp.where(diagonal(count), total, 0.0), axis=0, keepdims=True)


def add_kernel(h_own, h_remote, own, remote, got, out):
    left, right = turned(h_own, False), turned(h_remote, False)
    for at in range(0, remote.shape[1], WIDE):
        cols = slice(at, at + WIDE)
        mine = jnp.dot(left, own[:, cols], preferred_element_type=F32) + jnp.dot(
            right, remote[:, cols], preferred_element_type=F32
        )
        out[0, :, cols] = (mine + got[:, cols].astype(F32)).astype(BF16)


def along(rows, step):
    return lax.ppermute(rows, "ctx", [(i, i ^ step) for i in range(4)])


def body_line(tokens, cotangent, routes, gate_weights, w_gate, w_up, w_down):
    count, width = tokens.shape
    peers = lax.axis_size("tp")
    capacity = 3 * count * routes.shape[1] // (2 * peers)
    slots = peers * capacity
    inner = w_gate.shape[2]
    quarter = inner // 4
    gates = gate_weights.reshape(1, count)
    whole, in_place = pl.BlockSpec(), pl.BlockSpec(memory_space=pltpu.HBM)
    after = pl.BlockSpec(memory_space=pl.ANY)

    def over_tp(rows):
        wide = rows.shape[1]
        return lax.all_to_all(
            rows.reshape(peers, capacity, wide), "tp", split_axis=0, concat_axis=0, tiled=True
        ).reshape(slots, wide)

    slot, across, *blocks = call(
        functools.partial(send_kernel, peers, capacity),
        [
            shaped((2, count), jnp.int32),
            shaped((width // LANES * count + TAIL, LANES)),
        ]
        + [shaped((capacity, 2 * width))]
        + [pltpu.HBM((capacity, 2 * width), BF16)] * (peers - 1),
        scratch_shapes=[pltpu.VMEM((count, width), BF16)],
    )(in_hbm(routes.reshape(1, count)), in_hbm(gates), in_hbm(tokens), in_hbm(cotangent))
    rows_across = along(across, 3)
    got = {0: blocks[0]}
    for k in range(1, peers):
        got[k] = lax.ppermute(blocks[k], "tp", [(i, i ^ k) for i in range(peers)])
    order = (6, 7, 2, 4, 3, 5, 1, 0)
    got = [got[k] for k in order]

    gate_mat, up_mat, down_mat = [in_hbm(w[0]) for w in (w_gate, w_up, w_down)]
    held = [pltpu.VMEM((width, inner), BF16)] * 2
    dma = pltpu.SemaphoreType.DMA
    hidden, by_up, by_pre, near, far, cot = call(
        functools.partial(hidden_kernel, order),
        [shaped((slots, inner))] * 3
        + [shaped((slots, inner // 2))] * 2
        + [shaped((slots, width))],
        in_specs=[whole] * peers + [in_place] * 2,
        scratch_shapes=held
        + [
            pltpu.VMEM((slots, inner // 2), F32),
            pltpu.VMEM((slots, width), BF16),
            dma((2 * TILES,)),
        ],
    )(*got, gate_mat, up_mat)
    far_across = along(far, 3)
    remote = over_tp(
        call(
            remote_kernel, shaped((slots, width)), in_specs=[whole] + [after] * (peers - 1)
        )(rows_across, *[g for k, g in zip(order, got) if k])
    )
    back = call(
        back_kernel,
        [shaped((capacity, 2 * width))] + [pltpu.HBM((capacity, 2 * width), BF16)] * (peers - 1),
        in_specs=[whole] * 4 + [in_place] * 3,
        scratch_shapes=held
        + [pltpu.VMEM((inner, width), BF16)]
        + [pltpu.VMEM((slots, inner), BF16)] * 2
        + [dma((BACK_TILES + 2 * (width // WIDE),))],
    )(hidden, by_up, by_pre, cot, gate_mat, up_mat, down_mat)
    home = [
        lax.ppermute(back[k], "tp", [(i, i ^ k) for i in range(peers)]) if k else back[0]
        for k in order
    ]

    other = call(
        quarters_kernel,
        shaped((quarter, width)),
        in_specs=[after] + [whole] * 4,
    )(in_hbm(back[1]), near, far_across, cot, remote)
    swapped = along(other, 1)

    down_grad = call(add_kernel, shaped((1, quarter, width)))(
        near, far_across, cot, remote, swapped
    )
    layer_output, token_grad, gate_grad = call(
        functools.partial(home_kernel, order),
        [shaped((count, width)), shaped((count, width)), shaped((1, count), F32)],
        in_specs=[after] + [whole] * (3 + peers),
        scratch_shapes=[pltpu.VMEM((slots, 2 * width), BF16)],
    )(in_hbm(down_grad), slot, gates, cotangent, *home)
    return layer_output, token_grad, gate_grad.reshape(count, 1), down_grad


def body(tokens, cotangent, routes, gate_weights, w_gate, w_up, w_down):
    count, width = tokens.shape
    peers, inner = lax.axis_size("tp"), w_gate.shape[2]
    capacity = 3 * count * routes.shape[1] // (2 * peers)
    on_line = lax.axis_size("ctx") == 4 and peers == 8
    even = count == LANES and capacity % 8 == 0 and peers * capacity <= 256
    tiled = width % (2 * WIDE) == 0 and inner % (2 * TILES * LANES) == 0 and w_gate.shape[0] == 1
    chosen = body_line if on_line and even and tiled else body_any
    return chosen(tokens, cotangent, routes, gate_weights, w_gate, w_up, w_down)


def solution(mesh):
    rows = P(("ctx", "tp"), None)
    expert = P("tp", None, None)
    return jax.shard_map(
        body,
        mesh=mesh,
        in_specs=(rows, rows, rows, rows, expert, expert, expert),
        out_specs=(rows, rows, rows, P("tp", "ctx", None)),
        check_vma=False,
    )
```
